32 devices in a mesh: dev: 32 (over z, y, x, core).
Axes of the slice: x: 2, y: 2, z: 4, core: 2. Of those that a mesh axis runs over, the one named last changes fastest.
Arguments:
- tokens: bfloat16 [8192, 768], P('dev'), may hold values from -6 to 6
- cotangent: bfloat16 [8192, 768], P('dev'), may hold values from -6 to 6
- starts: int32 [8192], P('dev'), may hold values from 0 to 8191, as said below
- w_qkv: float32 [1769472], P('dev'), may hold values from -0.21875 to 0.21875
- m_qkv: float32 [1769472], P('dev'), may hold values from -24 to 24
- v_qkv: float32 [1769472], P('dev'), may hold values from 1.31072 to 5.24288
- w_out: float32 [589824], P('dev'), may hold values from -1.75 to 1.75
- m_out: float32 [589824], P('dev'), may hold values from -4 to 4
- v_out: float32 [589824], P('dev'), may hold values from 0.032 to 0.128
- w_up: float32 [2359296], P('dev'), may hold values from -0.21875 to 0.21875
- m_up: float32 [2359296], P('dev'), may hold values from -32 to 32
- v_up: float32 [2359296], P('dev'), may hold values from 2.94912 to 11.79648
- w_down: float32 [2359296], P('dev'), may hold values from -0.109375 to 0.109375
- m_down: float32 [2359296], P('dev'), may hold values from -40 to 40
- v_down: float32 [2359296], P('dev'), may hold values from 3.44064 to 13.9264
- vectors: float32 [9216], P('dev'), may hold values from -0.15 to 1.3, as said below
- m_vec: float32 [9216], P('dev'), may hold values from -40 to 40
- v_vec: float32 [9216], P('dev'), may hold values from 4.096 to 16.384
Outputs:
- out_tokens: bfloat16 [8192, 768], P('dev')
- input_grad: float32 [8192, 768], P('dev')
- qkv_moment: float32 [1769472], P('dev')
- qkv_second: float32 [1769472], P('dev')
- qkv_weight: float32 [1769472], P('dev')
- out_moment: float32 [589824], P('dev')
- out_second: float32 [589824], P('dev')
- out_weight: float32 [589824], P('dev')
- up_moment: float32 [2359296], P('dev')
- up_second: float32 [2359296], P('dev')
- up_weight: float32 [2359296], P('dev')
- down_moment: float32 [2359296], P('dev')
- down_second: float32 [2359296], P('dev')
- down_weight: float32 [2359296], P('dev')
- vec_moment: float32 [9216], P('dev')
- vec_second: float32 [9216], P('dev')
- vec_weight: float32 [9216], P('dev')
The draws below stay inside these ranges and needn't reach their ends.
Inputs may be any that keep to these rules, and one draw needn't show every extreme that they name: starts[i] is the index of the first token of the sequence that holds token i; sequences are contiguous runs of 512 to 1024 tokens, one of them exactly 1024, and only the last may be cut short by the end of the array. `vectors`: the gains (columns 0 and 5 of the table) lie in 0.7 to 1.3, all other entries (biases) in -0.15 to 0.15.
All inputs are finite; a program needn't handle non-finite values.
Results may differ from the reference program's by a relative error of at most 0.012.
The reference program's roundings to bfloat16 on the way count: a program that leaves them out, or rounds other values in their place, can miss the bound.
Values may be sent and summed in bfloat16 or wider, within the bound.
No kernel may reach another device: no remote copies, remote signals or barrier semaphores. Data moves between devices by JAX's collectives and lax.ppermute only.
A program may use at most 256 MiB of HBM per device.

```python
import math
import jax
import jax.numpy as jnp
from jax import lax

D = 768
HEADS = 12
HEAD_DIM = 64
FF = 3072
SEQ_MOST = 1024
STEP = 10
VROWS = 12
TOKENS = 8192


def draw_starts(key, part):
    key = jax.random.fold_in(key, 7)
    key_len, key_pick = jax.random.split(key)
    seq_count = TOKENS // (SEQ_MOST // 2) + 1
    lengths = jax.random.randint(key_len, (seq_count,), SEQ_MOST // 2, SEQ_MOST + 1)
    chosen = jax.random.randint(key_pick, (), 0, 4)
    lengths = jnp.where(jnp.arange(seq_count) == chosen, SEQ_MOST, lengths)
    firsts = jnp.cumsum(lengths) - lengths
    positions = jnp.arange(TOKENS, dtype=jnp.int32)
    owner = jnp.searchsorted(firsts, positions, side='right') - 1
    return firsts[owner].astype(jnp.int32)


def draw_vectors(key, part):
    key = jax.random.fold_in(key, 13)
    entries = jnp.arange(VROWS * D)
    column = entries % 8
    is_gain = (entries < 8 * D) & ((column == 0) | (column == 5))
    noise = jnp.clip(jax.random.normal(key, (VROWS * D,), jnp.float32) * 0.5, -1.0, 1.0)
    return jnp.where(is_gain, 1.0 + 0.3 * noise, 0.15 * noise).astype(jnp.float32)


def block_scale(own_key, shape, pieces, least, largest):
    def one(position, shards_of):
        heights = jax.random.uniform(jax.random.fold_in(jax.random.fold_in(own_key, 6), position), (shards_of,), jnp.float32, least / len(pieces), largest / len(pieces))
        return jnp.repeat(jnp.exp(heights), shape[position] // shards_of).reshape((-1,) + (1,) * (len(shape) - position - 1))

    level = one(*pieces[0])
    for cut in pieces[1:]:
        level = level * one(*cut)
    return level


def scatter_about(own_key, shape, scale, bound, cuts=(), kind=jnp.bfloat16):
    loudness = block_scale(own_key, shape, cuts, -0.22, 0.18) if cuts else 1.0
    values = jax.random.normal(own_key, shape, jnp.float32) * scale * loudness
    return jnp.minimum(jnp.maximum(values, -bound), bound).astype(kind)


def setup_inputs(seed: int = 0) -> dict:
    splits = jax.random.split(jax.random.key(seed), 19)
    return {
        "tokens": scatter_about(splits[0], (TOKENS, D), 1.0, 6.0, ((0, 32),)),
        "cotangent": scatter_about(splits[1], (TOKENS, D), 1.0, 6.0, ((0, 32),)),
        "starts": draw_starts(jax.random.fold_in(splits[18], 71), 0),
        "w_qkv": scatter_about(splits[3], (3 * D * D,), D ** -0.5, 0.21875, ((0, 32),), jnp.float32),
        "m_qkv": scatter_about(splits[4], (3 * D * D,), (0.044 * TOKENS ** 0.5), 24.0, ((0, 32),), jnp.float32),
        "v_qkv": jnp.clip(jnp.exp(math.log(5.24288) - 1.3862944 * jax.random.uniform(splits[5], (3 * D * D,), jnp.float32) ** block_scale(splits[5], (3 * D * D,), ((0, 32),), -0.2, 0.2)), 1.31072, 5.24288),
        "w_out": scatter_about(splits[6], (D * D,), (max(1, D * 16 // SEQ_MOST)) ** -0.5, 1.75, ((0, 32),), jnp.float32),
        "m_out": scatter_about(splits[7], (D * D,), (0.22 * (TOKENS // SEQ_MOST) ** 0.5), 4.0, ((0, 32),), jnp.float32),
        "v_out": jnp.clip(jnp.exp(math.log(0.128) - 1.3862944 * jax.random.uniform(splits[8], (D * D,), jnp.float32) ** block_scale(splits[8], (D * D,), ((0, 32),), -0.2, 0.2)), 0.032, 0.128),
        "w_up": scatter_about(splits[9], (D * FF,), D ** -0.5, 0.21875, ((0, 32),), jnp.float32),
        "m_up": scatter_about(splits[10], (D * FF,), (0.067 * TOKENS ** 0.5), 32.0, ((0, 32),), jnp.float32),
        "v_up": jnp.clip(jnp.exp(math.log(11.79648) - 1.3862944 * jax.random.uniform(splits[11], (D * FF,), jnp.float32) ** block_scale(splits[11], (D * FF,), ((0, 32),), -0.2, 0.2)), 2.94912, 11.79648),
        "w_down": scatter_about(splits[12], (FF * D,), FF ** -0.5, 0.109375, ((0, 32),), jnp.float32),
        "m_down": scatter_about(splits[13], (FF * D,), (0.072 * TOKENS ** 0.5), 40.0, ((0, 32),), jnp.float32),
        "v_down": jnp.clip(jnp.exp(math.log(13.9264) - 1.39812884 * jax.random.uniform(splits[14], (FF * D,), jnp.float32) ** block_scale(splits[14], (FF * D,), ((0, 32),), -0.2, 0.2)), 3.44064, 13.9264),
        "vectors": draw_vectors(jax.random.fold_in(splits[18], 71), 0),
        "m_vec": scatter_about(splits[16], (VROWS * D,), (0.078 * TOKENS ** 0.5), 40.0, ((0, 32),), jnp.float32),
        "v_vec": jnp.clip(jnp.exp(math.log(16.384) - 1.3862944 * jax.random.uniform(splits[17], (VROWS * D,), jnp.float32) ** block_scale(splits[17], (VROWS * D,), ((0, 32),), -0.2, 0.2)), 4.096, 16.384),
    }


NORM_EPS = 1e-05
BETA_ONE = 0.9
BETA_TWO = 0.999
ADAM_EPS = 1e-08
DECAY_RATE = 0.01
NEG_LARGE = -1e+30

@jax.custom_vjp
def low(v):
    return lax.optimization_barrier(v.astype(jnp.bfloat16)).astype(jnp.float32)

@jax.custom_vjp
def low_back(v):
    return v

def low_keep(v):
    return (low(v), None)

def low_pass(kept, grad):
    return (grad,)

def back_keep(v):
    return (v, None)

def back_low(kept, grad):
    return (low(grad),)
low.defvjp(low_keep, low_pass)
low_back.defvjp(back_keep, back_low)

def product(operand_a, operand_b):
    return jnp.dot(operand_a, operand_b, precision=lax.Precision.HIGHEST)

def layer_norm(values, gain_vec, shift_vec):
    centre = lax.optimization_barrier(jnp.mean(values, axis=-1, keepdims=True))
    centred = values - centre
    spread = lax.optimization_barrier(jnp.mean(centred * centred, axis=-1, keepdims=True))
    return centred * lax.rsqrt(spread + NORM_EPS) * gain_vec + shift_vec

def smooth_act(values):
    return jax.nn.gelu(values, approximate=True)

def adamw(weight, moment, second, gradient, step_rate, decay_rate):
    moment = BETA_ONE * moment + (1.0 - BETA_ONE) * gradient
    second = BETA_TWO * second + (1.0 - BETA_TWO) * gradient * gradient
    first_hat = moment / (1.0 - BETA_ONE ** STEP)
    second_hat = second / (1.0 - BETA_TWO ** STEP)
    weight = weight - step_rate * (first_hat / (jnp.sqrt(second_hat) + ADAM_EPS) + decay_rate * weight)
    return (moment, second, weight)

def matrix_rates():
    return (2.5 * D ** (-0.5), 2.5 * max(1, D * 16 // SEQ_MOST) ** (-0.5), 2.5 * D ** (-0.5), 2.5 * FF ** (-0.5))

def vector_rates(entries):
    column = entries % 8
    is_gain = (entries < 8 * D) & ((column == 0) | (column == 5))
    return jnp.where(is_gain, 0.3, 0.05).astype(jnp.float32)

def split_vectors(vec_all):
    return (vec_all[:8 * D].reshape(D, 8), vec_all[8 * D:])

def attention(query, keys_all, values_all, starts):
    block_rows = min(512, TOKENS)
    block_count = TOKENS // block_rows
    padding = jnp.zeros((SEQ_MOST, D), jnp.float32)
    keys_pad = jnp.concatenate([padding, keys_all], axis=0)
    values_pad = jnp.concatenate([padding, values_all], axis=0)
    scale = HEAD_DIM ** (-0.5)
    span = SEQ_MOST + block_rows

    def one_block(blk_index):
        blk_start = (blk_index * block_rows).astype(jnp.int32)
        q_block = lax.dynamic_slice_in_dim(query, blk_start, block_rows, 0).reshape(block_rows, HEADS, HEAD_DIM)
        k_block = lax.dynamic_slice_in_dim(keys_pad, blk_start, span, 0).reshape(span, HEADS, HEAD_DIM)
        v_block = lax.dynamic_slice_in_dim(values_pad, blk_start, span, 0).reshape(span, HEADS, HEAD_DIM)
        raw_scores = jnp.einsum('qhd,khd->hqk', q_block, k_block, precision=lax.Precision.HIGHEST)
        scores = low_back(raw_scores) * scale
        seen_pos = blk_start - SEQ_MOST + jnp.arange(span, dtype=jnp.int32)
        own_pos = blk_start + jnp.arange(block_rows, dtype=jnp.int32)
        own_start = lax.dynamic_slice_in_dim(starts, blk_start, block_rows, 0)
        allowed = (seen_pos[None, :] >= own_start[:, None]) & (seen_pos[None, :] <= own_pos[:, None])
        scores = jnp.where(allowed[None], scores, NEG_LARGE)
        peak = lax.optimization_barrier(jnp.max(scores, axis=-1, keepdims=True))
        weights = jnp.exp(scores - peak)
        weights = weights / lax.optimization_barrier(jnp.sum(weights, axis=-1, keepdims=True))
        blended = jnp.einsum('hqk,khd->qhd', low(weights), v_block, precision=lax.Precision.HIGHEST)
        return blended.reshape(block_rows, D)
    blended = lax.map(jax.checkpoint(one_block), jnp.arange(block_count, dtype=jnp.int32))
    return blended.reshape(TOKENS, D)

def layer(inputs, qkv_flat, out_flat, up_flat, down_flat, vec_flat, starts):
    vec_table, up_bias = split_vectors(low(vec_flat))
    qkv_w = low(qkv_flat).reshape(D, 3 * D)
    out_w = low(out_flat).reshape(D, D)
    up_w = low(up_flat).reshape(D, FF)
    down_w = low(down_flat).reshape(FF, D)
    normed = low(layer_norm(inputs, vec_table[:, 0], vec_table[:, 1]))
    joined = product(normed, qkv_w)
    joined = jnp.concatenate([joined[:, :D] + vec_table[:, 2], joined[:, D:2 * D], joined[:, 2 * D:] + vec_table[:, 3]], axis=1)
    joined = low_back(low(joined))
    attended = attention(joined[:, :D], joined[:, D:2 * D], joined[:, 2 * D:], starts)
    attended = low_back(low(attended))
    branch = low_back(product(attended, out_w) + vec_table[:, 4])
    middle = inputs + branch
    normed_two = low(layer_norm(middle, vec_table[:, 5], vec_table[:, 6]))
    hidden_pre = low_back(product(normed_two, up_w) + up_bias)
    active = low(smooth_act(hidden_pre))
    return middle + (product(active, down_w) + vec_table[:, 7])

def reference(tokens, cotangent, starts, w_qkv, m_qkv, v_qkv, w_out, m_out, v_out, w_up, m_up, v_up, w_down, m_down, v_down, vectors, m_vec, v_vec):
    inputs = tokens.astype(jnp.float32)

    def forward(inputs_f, qkv_flat, out_flat, up_flat, down_flat, vec_flat):
        return layer(inputs_f, qkv_flat, out_flat, up_flat, down_flat, vec_flat, starts)
    result, pullback = jax.vjp(forward, inputs, w_qkv, w_out, w_up, w_down, vectors)
    input_grad, grad_qkv, grad_out, grad_up, grad_down, grad_vec = pullback(cotangent.astype(jnp.float32))
    rate_qkv, rate_out, rate_up, rate_down = matrix_rates()
    qkv_new = adamw(w_qkv, m_qkv, v_qkv, grad_qkv, rate_qkv, DECAY_RATE)
    out_new = adamw(w_out, m_out, v_out, grad_out, rate_out, DECAY_RATE)
    up_new = adamw(w_up, m_up, v_up, grad_up, rate_up, DECAY_RATE)
    down_new = adamw(w_down, m_down, v_down, grad_down, rate_down, DECAY_RATE)
    vec_new = adamw(vectors, m_vec, v_vec, grad_vec, vector_rates(jnp.arange(VROWS * D, dtype=jnp.int32)), 0.0)
    return (result.astype(jnp.bfloat16), input_grad, qkv_new[0], qkv_new[1], qkv_new[2], out_new[0], out_new[1], out_new[2], up_new[0], up_new[1], up_new[2], down_new[0], down_new[1], down_new[2], vec_new[0], vec_new[1], vec_new[2])
```

```python
import jax
import jax.numpy as jnp
from jax import lax
from jax.sharding import PartitionSpec as P

D = 768
HEAD_DIM = 64
HEADS = D // HEAD_DIM
FF = 3072
SEQ_MOST = 1024
STEP = 10
VCOLS = 12


NORM_EPS = 1e-05
BETA_ONE = 0.9
BETA_TWO = 0.999
ADAM_EPS = 1e-08
DECAY_RATE = 0.01
NEG_LARGE = -1e30

LOW = jnp.bfloat16
FULL = jnp.float32


def layer_norm(values, gain_vec, shift_vec):
    centre = jnp.mean(values, axis=-1, keepdims=True)
    centred = values - centre
    spread = jnp.mean(centred * centred, axis=-1, keepdims=True)
    return centred * lax.rsqrt(spread + NORM_EPS) * gain_vec + shift_vec


def norm_parts(values):
    centre = jnp.mean(values, axis=-1, keepdims=True)
    centred = values - centre
    spread = jnp.mean(centred * centred, axis=-1, keepdims=True)
    inverse = lax.rsqrt(spread + NORM_EPS)
    return centred * inverse, inverse


def norm_back(grad, unit, inverse, gain_vec):
    scaled = grad * gain_vec
    along = jnp.mean(scaled * unit, axis=-1, keepdims=True)
    return inverse * (scaled - jnp.mean(scaled, axis=-1, keepdims=True) - unit * along)


def smooth_act(values):
    return jax.nn.gelu(values, approximate=True)


def adamw(weight, moment, second, gradient, step_rate, decay_rate):
    moment = BETA_ONE * moment + (1.0 - BETA_ONE) * gradient
    second = BETA_TWO * second + (1.0 - BETA_TWO) * gradient * gradient
    first_hat = moment / (1.0 - BETA_ONE**STEP)
    second_hat = second / (1.0 - BETA_TWO**STEP)
    weight = weight - step_rate * (
        first_hat / (jnp.sqrt(second_hat) + ADAM_EPS) + decay_rate * weight
    )
    return (moment, second, weight)


def matrix_rates():
    return (
        2.5 * D ** (-0.5),
        2.5 * max(1, D * 16 // SEQ_MOST) ** (-0.5),
        2.5 * D ** (-0.5),
        2.5 * FF ** (-0.5),
    )


def vector_rates(entries):
    column = entries % 8
    is_gain = (entries < 8 * D) & ((column == 0) | (column == 5))
    return jnp.where(is_gain, 0.3, 0.05).astype(jnp.float32)


def shifted(x, by):
    length = lax.axis_size("dev")
    return lax.ppermute(x, "dev", [(i, i + by) for i in range(length) if 0 <= i + by < length])


def flipped(x, mask):
    return lax.ppermute(x, "dev", [(i, i ^ mask) for i in range(lax.axis_size("dev"))])


class Index:
    def __init__(self):
        self.count = lax.axis_size("dev")
        self.bits = self.count.bit_length() - 1
        self.me = lax.axis_index("dev")
        self.top = self.bits - 2
        self.quarter = self.me >> self.top
        self.lead = (4,) + (2,) * self.top
        self.middle = tuple(range(1, self.top))

    def bit(self, b):
        return (self.me >> b) & 1

    def dim(self, b):
        return self.top - b


def ordered(bit, own, other, dim):
    flag = bit == 1
    return jnp.concatenate([jnp.where(flag, other, own), jnp.where(flag, own, other)], axis=dim)


def gather_top(ix, x):
    x = x.reshape((1,) * (ix.bits - 1) + x.shape)
    near, far, both = (flipped(x, r << ix.top) for r in (1, 2, 3))
    low_bit, high_bit = ix.quarter & 1, ix.quarter >> 1
    return ordered(high_bit, ordered(low_bit, x, near, 0), ordered(low_bit, far, both, 0), 0)


def gather_bits(ix, x, bits):
    for b in bits:
        x = ordered(ix.bit(b), x, flipped(x, 1 << b), ix.dim(b))
    return x


def joined_rows(x):
    return x.reshape(-1, x.shape[-1])


def scatter_bits(ix, x, bits):
    for b in bits:
        bit, dim = ix.bit(b), ix.dim(b)
        keep = lax.dynamic_slice_in_dim(x, bit, 1, dim)
        other = flipped(lax.dynamic_slice_in_dim(x, 1 - bit, 1, dim), 1 << b)
        x = (keep.astype(FULL) + other.astype(FULL)).astype(LOW)
    return x


def scatter_top(ix, x):
    total = lax.dynamic_slice_in_dim(x, ix.quarter, 1, 0).astype(FULL)
    others = [
        flipped(lax.dynamic_slice_in_dim(x, ix.quarter ^ r, 1, 0), r << ix.top) for r in (1, 2, 3)
    ]
    for other in others:
        total = total + other.astype(FULL)
    return total.reshape(total.shape[-2:])


def spread_rows(ix, x):
    return x.reshape(ix.lead + (x.shape[0] // ix.count, x.shape[1]))


def outer_sum(operand_a, operand_b):
    return jnp.einsum("ti,tj->ij", operand_a, operand_b, preferred_element_type=FULL).astype(LOW)


def body(
    tokens,
    cotangent,
    starts,
    w_qkv,
    m_qkv,
    v_qkv,
    w_out,
    m_out,
    v_out,
    w_up,
    m_up,
    v_up,
    w_down,
    m_down,
    v_down,
    vectors,
    m_vec,
    v_vec,
):
    ix = Index()
    rows = D // ix.count
    tok_rows = tokens.shape[0]
    reach_count = (SEQ_MOST + tok_rows - 2) // tok_rows
    near_rows = (reach_count + 1) * tok_rows
    scale = HEAD_DIM ** (-0.5)
    odd = ix.bit(0) == 1
    ahead = tuple(reversed(ix.middle))
    back = ix.middle

    assert reach_count == 4
    two_before, four_before = shifted(tokens, 2), shifted(tokens, 4)
    from_mate = flipped(
        jnp.where(
            odd,
            jnp.concatenate([two_before, four_before], axis=0),
            jnp.concatenate([tokens, two_before], axis=0),
        ),
        1,
    )
    near_tokens = jnp.concatenate(
        [four_before, from_mate[tok_rows:], two_before, from_mate[:tok_rows], tokens], axis=0
    )

    vec_piece = jnp.pad(vectors.astype(LOW).reshape(rows, VCOLS), ((0, 0), (0, 128 - VCOLS)))
    first = jnp.concatenate([w_qkv.astype(LOW).reshape(rows, 3 * D), vec_piece], axis=1)
    first = gather_top(ix, first)
    half = 3 * D // 2
    left = joined_rows(gather_bits(ix, first[..., :half], ahead + (0,)))
    right = joined_rows(gather_bits(ix, first[..., half:], back + (0,)))
    qkv_w = jnp.concatenate([left, right[:, : 3 * D - half]], axis=1)
    vec_all = right[:, 3 * D - half : 3 * D - half + VCOLS].reshape(-1).astype(FULL)

    second = jnp.concatenate(
        [w_out.astype(LOW).reshape(rows, D), w_up.astype(LOW).reshape(rows, FF)], axis=1
    )
    second = joined_rows(gather_bits(ix, gather_top(ix, second), ahead + (0,)))
    out_w, up_w = second[:, :D], second[:, D:]
    down_w = joined_rows(
        gather_bits(ix, gather_top(ix, w_down.astype(LOW).reshape(4 * rows, D)), back + (0,))
    )

    vec_table, up_bias = vec_all[: 8 * D].reshape(D, 8), vec_all[8 * D :]
    gain_one, shift_one, bias_q, bias_v, bias_o, gain_two, shift_two, bias_down = (
        vec_table[:, i] for i in range(8)
    )

    inputs = tokens.astype(FULL)
    near_unit, near_inverse = norm_parts(near_tokens.astype(FULL))
    near_normed = (near_unit * gain_one + shift_one).astype(LOW)
    normed = near_normed[near_rows - tok_rows :]
    query = (jnp.dot(normed, qkv_w[:, :D], preferred_element_type=FULL) + bias_q).astype(LOW)
    kv_bias = jnp.concatenate([jnp.zeros((D,), FULL), bias_v])
    near_kv = (jnp.dot(near_normed, qkv_w[:, D:], preferred_element_type=FULL) + kv_bias).astype(
        LOW
    )
    base_pos = ix.me * tok_rows
    query_pos = base_pos + jnp.arange(tok_rows, dtype=jnp.int32)
    key_pos = base_pos - reach_count * tok_rows + jnp.arange(near_rows, dtype=jnp.int32)
    allowed = (key_pos[None, :] >= starts[:, None]) & (key_pos[None, :] <= query_pos[:, None])
    q_heads = query.reshape(tok_rows, HEADS, HEAD_DIM)
    k_heads = near_kv[:, :D].reshape(near_rows, HEADS, HEAD_DIM)
    v_heads = near_kv[:, D:].reshape(near_rows, HEADS, HEAD_DIM)

    scores = jnp.einsum("qhd,khd->hqk", q_heads, k_heads, preferred_element_type=FULL) * scale
    scores = jnp.where(allowed[None], scores, NEG_LARGE)
    peak = jnp.max(scores, axis=-1, keepdims=True)
    weights = jnp.exp(scores - peak)
    weights = weights / jnp.sum(weights, axis=-1, keepdims=True)
    weights_low = weights.astype(LOW)
    blended = jnp.einsum("hqk,khd->qhd", weights_low, v_heads, preferred_element_type=FULL)
    attended = blended.reshape(tok_rows, D).astype(LOW)

    branch = jnp.dot(attended, out_w, preferred_element_type=FULL) + bias_o
    middle = inputs + branch
    unit_two, inverse_two = norm_parts(middle)
    normed_two = (unit_two * gain_two + shift_two).astype(LOW)
    hidden_pre = jnp.dot(normed_two, up_w, preferred_element_type=FULL) + up_bias
    hidden_low = smooth_act(hidden_pre).astype(LOW)
    result = middle + (jnp.dot(hidden_low, down_w, preferred_element_type=FULL) + bias_down)
    out_tokens = result.astype(LOW)

    grad_out = cotangent.astype(FULL)
    grad_downw = outer_sum(hidden_low, cotangent)
    sum_down = scatter_top(
        ix, scatter_bits(ix, spread_rows(ix, grad_downw), (0,) + back)
    )
    grad_hidden = jnp.dot(cotangent, down_w.T, preferred_element_type=FULL)
    act_value, act_back = jax.vjp(smooth_act, hidden_pre)
    grad_pre = act_back(grad_hidden)[0].astype(LOW)
    grad_upw = outer_sum(normed_two, grad_pre)
    grad_normed_two = jnp.dot(grad_pre, up_w.T, preferred_element_type=FULL)
    grad_gain_two = jnp.sum(grad_normed_two * unit_two, axis=0)
    grad_shift_two = jnp.sum(grad_normed_two, axis=0)
    grad_middle = grad_out + norm_back(grad_normed_two, unit_two, inverse_two, gain_two)
    grad_branch = grad_middle.astype(LOW)
    grad_outw = outer_sum(attended, grad_branch)
    sum_second = scatter_top(
        ix,
        scatter_bits(
            ix,
            spread_rows(ix, jnp.concatenate([grad_outw, grad_upw], axis=1)),
            (0,) + ahead,
        ),
    )
    grad_attended = jnp.dot(grad_branch, out_w.T, preferred_element_type=FULL).astype(LOW)

    grad_heads = grad_attended.reshape(tok_rows, HEADS, HEAD_DIM)
    grad_weights = jnp.einsum("qhd,khd->hqk", grad_heads, v_heads, preferred_element_type=FULL)
    inner_sum = jnp.sum(weights * grad_weights, axis=-1, keepdims=True)
    grad_scores = (weights * (grad_weights - inner_sum) * scale).astype(LOW)
    grad_q = jnp.einsum("hqk,khd->qhd", grad_scores, k_heads, preferred_element_type=FULL)
    grad_k = jnp.einsum("hqk,qhd->khd", grad_scores, q_heads, preferred_element_type=FULL)
    grad_v = jnp.einsum("hqk,qhd->khd", weights_low, grad_heads, preferred_element_type=FULL)
    grad_q = grad_q.reshape(tok_rows, D).astype(LOW)
    grad_kv = jnp.concatenate(
        [grad_k.reshape(near_rows, D), grad_v.reshape(near_rows, D)], axis=1
    ).astype(LOW)

    grad_near = jnp.dot(grad_kv, qkv_w[:, D:].T, preferred_element_type=FULL)
    grad_near = grad_near + jnp.pad(
        jnp.dot(grad_q, qkv_w[:, :D].T, preferred_element_type=FULL),
        ((near_rows - tok_rows, 0), (0, 0)),
    )
    grad_gain_one = jnp.sum(grad_near * near_unit, axis=0)
    grad_shift_one = jnp.sum(grad_near, axis=0)
    grad_qkvw = jnp.concatenate([outer_sum(normed, grad_q), outer_sum(near_normed, grad_kv)], axis=1)

    vec_rows = jnp.stack(
        [
            grad_gain_one,
            grad_shift_one,
            jnp.sum(grad_q.astype(FULL), axis=0),
            jnp.sum(grad_kv[:, D:].astype(FULL), axis=0),
            jnp.sum(grad_branch.astype(FULL), axis=0),
            grad_gain_two,
            grad_shift_two,
            jnp.sum(grad_out, axis=0),
        ],
        axis=1,
    )
    grad_vec = jnp.concatenate([vec_rows.reshape(-1), jnp.sum(grad_pre.astype(FULL), axis=0)])
    grad_vec = jnp.pad(grad_vec.astype(LOW).reshape(D, VCOLS), ((0, 0), (0, 128 - VCOLS)))
    sum_left = scatter_bits(ix, spread_rows(ix, grad_qkvw[:, :half]), (0,) + ahead)
    sum_right = scatter_bits(
        ix,
        spread_rows(ix, jnp.concatenate([grad_qkvw[:, half:], grad_vec], axis=1)),
        (0,) + back,
    )
    sum_first = scatter_top(ix, jnp.concatenate([sum_left, sum_right], axis=-1))

    parts = grad_near.astype(LOW).reshape(reach_count + 1, tok_rows, D)
    from_mate = flipped(jnp.concatenate([parts[3], parts[1]], axis=0), 1)
    near_mate, far_mate = from_mate[:tok_rows].astype(FULL), from_mate[tok_rows:].astype(FULL)
    own = grad_near[near_rows - tok_rows :] + jnp.where(odd, 0.0, near_mate)
    two_back = parts[2].astype(FULL) + jnp.where(odd, near_mate, far_mate)
    four_back = parts[0].astype(FULL) + jnp.where(odd, far_mate, 0.0)
    own = (
        own
        + shifted(two_back.astype(LOW), -2).astype(FULL)
        + shifted(four_back.astype(LOW), -4).astype(FULL)
    )
    unit_one = near_unit[near_rows - tok_rows :]
    inverse_one = near_inverse[near_rows - tok_rows :]
    input_grad = grad_middle + norm_back(own, unit_one, inverse_one, gain_one)

    rate_qkv, rate_out, rate_up, rate_down = matrix_rates()
    entries = ix.me * vectors.shape[0] + jnp.arange(vectors.shape[0], dtype=jnp.int32)
    g_qkv = sum_first[:, : 3 * D].reshape(-1)
    g_vec = sum_first[:, 3 * D : 3 * D + VCOLS].reshape(-1)
    g_out = sum_second[:, :D].reshape(-1)
    g_up = sum_second[:, D:].reshape(-1)
    g_down = sum_down.reshape(-1)
    qkv_new = adamw(w_qkv, m_qkv, v_qkv, g_qkv, rate_qkv, DECAY_RATE)
    out_new = adamw(w_out, m_out, v_out, g_out, rate_out, DECAY_RATE)
    up_new = adamw(w_up, m_up, v_up, g_up, rate_up, DECAY_RATE)
    down_new = adamw(w_down, m_down, v_down, g_down, rate_down, DECAY_RATE)
    vec_new = adamw(vectors, m_vec, v_vec, g_vec, vector_rates(entries), 0.0)
    return (out_tokens, input_grad) + qkv_new + out_new + up_new + down_new + vec_new


def solution(mesh):
    in_specs = (P("dev", None), P("dev", None)) + (P("dev"),) * 16
    out_specs = (P("dev", None), P("dev", None)) + (P("dev"),) * 15
    return jax.shard_map(body, mesh=mesh, in_specs=in_specs, out_specs=out_specs, check_vma=False)
```

```python
import jax
import jax.numpy as jnp
from jax import lax
from jax.experimental import pallas as pl
from jax.experimental.pallas import tpu as pltpu
from jax.sharding import PartitionSpec as P

D = 768
HEAD_DIM = 64
HEADS = D // HEAD_DIM
FF = 3072
SEQ_MOST = 1024
STEP = 10
VCOLS = 12


NORM_EPS = 1e-05
BETA_ONE = 0.9
BETA_TWO = 0.999
ADAM_EPS = 1e-08
DECAY_RATE = 0.01
NEG_LARGE = -1e30

LOW = jnp.bfloat16
FULL = jnp.float32


def layer_norm(values, gain_vec, shift_vec):
    centre = jnp.mean(values, axis=-1, keepdims=True)
    centred = values - centre
    spread = jnp.mean(centred * centred, axis=-1, keepdims=True)
    return centred * lax.rsqrt(spread + NORM_EPS) * gain_vec + shift_vec


def norm_parts(values):
    centre = jnp.mean(values, axis=-1, keepdims=True)
    centred = values - centre
    spread = jnp.mean(centred * centred, axis=-1, keepdims=True)
    inverse = lax.rsqrt(spread + NORM_EPS)
    return centred * inverse, inverse


def norm_back(grad, unit, inverse, gain_vec):
    scaled = grad * gain_vec
    along = jnp.mean(scaled * unit, axis=-1, keepdims=True)
    return inverse * (scaled - jnp.mean(scaled, axis=-1, keepdims=True) - unit * along)


def smooth_act(values):
    return jax.nn.gelu(values, approximate=True)


def adamw(weight, moment, second, gradient, step_rate, decay_rate):
    moment = BETA_ONE * moment + (1.0 - BETA_ONE) * gradient
    second = BETA_TWO * second + (1.0 - BETA_TWO) * gradient * gradient
    first_hat = moment / (1.0 - BETA_ONE**STEP)
    second_hat = second / (1.0 - BETA_TWO**STEP)
    weight = weight - step_rate * (
        first_hat / (jnp.sqrt(second_hat) + ADAM_EPS) + decay_rate * weight
    )
    return (moment, second, weight)


def matrix_rates():
    return (
        2.5 * D ** (-0.5),
        2.5 * max(1, D * 16 // SEQ_MOST) ** (-0.5),
        2.5 * D ** (-0.5),
        2.5 * FF ** (-0.5),
    )


def vector_rates(entries):
    column = entries % 8
    is_gain = (entries < 8 * D) & ((column == 0) | (column == 5))
    return jnp.where(is_gain, 0.3, 0.05).astype(jnp.float32)


def shifted(x, by):
    length = lax.axis_size("dev")
    return lax.ppermute(x, "dev", [(i, i + by) for i in range(length) if 0 <= i + by < length])


def flipped(x, mask):
    return lax.ppermute(x, "dev", [(i, i ^ mask) for i in range(lax.axis_size("dev"))])


class Index:
    def __init__(self):
        self.count = lax.axis_size("dev")
        self.bits = self.count.bit_length() - 1
        self.me = lax.axis_index("dev")
        self.top = self.bits - 2
        self.quarter = self.me >> self.top
        self.lead = (4,) + (2,) * self.top
        self.middle = tuple(range(1, self.top))

    def bit(self, b):
        return (self.me >> b) & 1

    def dim(self, b):
        return self.top - b


def ordered(bit, own, other, dim):
    flag = bit == 1
    return jnp.concatenate([jnp.where(flag, other, own), jnp.where(flag, own, other)], axis=dim)


def gather_top(ix, x):
    x = x.reshape((1,) * (ix.bits - 1) + x.shape)
    near, far, both = (flipped(x, r << ix.top) for r in (1, 2, 3))
    low_bit, high_bit = ix.quarter & 1, ix.quarter >> 1
    return ordered(high_bit, ordered(low_bit, x, near, 0), ordered(low_bit, far, both, 0), 0)


def gather_bits(ix, x, bits):
    for b in bits:
        x = ordered(ix.bit(b), x, flipped(x, 1 << b), ix.dim(b))
    return x


def joined_rows(x):
    return x.reshape(-1, x.shape[-1])


def scatter_bits(ix, x, bits):
    for b in bits:
        bit, dim = ix.bit(b), ix.dim(b)
        keep = lax.dynamic_slice_in_dim(x, bit, 1, dim)
        other = flipped(lax.dynamic_slice_in_dim(x, 1 - bit, 1, dim), 1 << b)
        x = (keep.astype(FULL) + other.astype(FULL)).astype(LOW)
    return x


def scatter_sides(ix, sides, step):
    orders = (tuple(reversed(ix.middle)), ix.middle)
    return tuple(scatter_bits(ix, side, order[step]) for side, order in zip(sides, orders))


def halves(x):
    cut = x.shape[-1] // 2
    return (x[..., :cut], x[..., cut:])


def scatter_top(ix, x):
    total = lax.dynamic_slice_in_dim(x, ix.quarter, 1, 0).astype(FULL)
    others = [
        flipped(lax.dynamic_slice_in_dim(x, ix.quarter ^ r, 1, 0), r << ix.top) for r in (1, 2, 3)
    ]
    for other in others:
        total = total + other.astype(FULL)
    return total.reshape(total.shape[-2:])


def spread_rows(ix, x):
    return x.reshape(ix.lead + (x.shape[0] // ix.count, x.shape[1]))


PAIR = 2 * HEAD_DIM
PAIRS = HEADS // 2
SIDE = PAIRS // 2
SCALE = HEAD_DIM ** (-0.5)
VMEM_BYTES = 48 * 1024 * 1024


def by_head(pair):
    low_half = lax.broadcasted_iota(jnp.int32, pair.shape, 1) < HEAD_DIM
    zero = jnp.zeros_like(pair)
    return (
        low_half,
        jnp.where(low_half, pair, zero).astype(LOW),
        jnp.where(low_half, zero, pair).astype(LOW),
    )


def dot_over(operand_a, operand_b, dim_a, dim_b):
    return lax.dot_general(
        operand_a, operand_b, (((dim_a,), (dim_b,)), ((), ())), preferred_element_type=FULL
    )


def attend_kernel(first_ref, q_ref, kv_ref, out_ref, weights_ref):
    rows, near = q_ref.shape[0], kv_ref.shape[0]
    low_half, *q_heads = by_head(q_ref[...].astype(FULL) * SCALE)
    k, v = kv_ref[:, :PAIR], kv_ref[:, PAIR:]
    key = lax.broadcasted_iota(jnp.int32, (rows, near), 1)
    last = lax.broadcasted_iota(jnp.int32, (rows, near), 0) + (near - rows)
    allowed = (key >= first_ref[...]) & (key <= last)
    blended = []
    for head in range(2):
        scores = jnp.where(allowed, dot_over(q_heads[head], k, 1, 1), NEG_LARGE)
        weights = jnp.exp(scores - jnp.max(scores, axis=-1, keepdims=True))
        weights = weights * (1.0 / jnp.sum(weights, axis=-1, keepdims=True))
        weights = weights.astype(LOW)
        weights_ref[head] = weights
        blended.append(dot_over(weights, v, 1, 0))
    out_ref[...] = jnp.where(low_half, blended[0], blended[1]).astype(LOW)


def attend(first_key, query, kv):
    rows, near, pairs = query.shape[0], kv.shape[0], query.shape[1] // PAIR
    return pl.pallas_call(
        attend_kernel,
        grid=(pairs,),
        in_specs=[
            pl.BlockSpec((rows, 1), lambda i: (0, 0)),
            pl.BlockSpec((rows, PAIR), lambda i: (0, i)),
            pl.BlockSpec((near, 2 * PAIR), lambda i: (0, i)),
        ],
        out_specs=[
            pl.BlockSpec((rows, PAIR), lambda i: (0, i)),
            pl.BlockSpec((2, rows, near), lambda i: (i, 0, 0)),
        ],
        out_shape=[
            jax.ShapeDtypeStruct((rows, pairs * PAIR), LOW),
            jax.ShapeDtypeStruct((2 * pairs, rows, near), LOW),
        ],
        compiler_params=pltpu.CompilerParams(vmem_limit_bytes=VMEM_BYTES),
        cost_estimate=pl.CostEstimate(
            flops=16 * pairs * rows * near * PAIR,
            bytes_accessed=8 * pairs * rows * near,
            transcendentals=2 * pairs * rows * near,
        ),
    )(first_key, query, kv)


def attend_back_kernel(weights_ref, grad_ref, q_ref, kv_ref, dq_ref, dkv_ref):
    low_half, *grad_heads = by_head(grad_ref[...].astype(FULL))
    _, *q_heads = by_head(q_ref[...].astype(FULL))
    k, v = kv_ref[:, :PAIR], kv_ref[:, PAIR:]
    dq = []
    dk_turned = dv_turned = 0.0
    for head in range(2):
        weights_low = weights_ref[head]
        weights = weights_low.astype(FULL)
        grad_weights = dot_over(grad_heads[head], v, 1, 1)
        inner_sum = jnp.sum(weights * grad_weights, axis=-1, keepdims=True)
        grad_scores = (weights * (grad_weights - inner_sum)).astype(LOW)
        dq.append(dot_over(grad_scores, k, 1, 0))
        dk_turned += dot_over(q_heads[head], grad_scores, 0, 0)
        dv_turned += dot_over(grad_heads[head], weights_low, 0, 0)
    dq_ref[...] = (jnp.where(low_half, dq[0], dq[1]) * SCALE).astype(LOW)
    dkv_ref[:, :PAIR] = (dk_turned * SCALE).T.astype(LOW)
    dkv_ref[:, PAIR:] = dv_turned.T.astype(LOW)


def attend_back(weights, grad, query, kv):
    rows, near, pairs = query.shape[0], kv.shape[0], query.shape[1] // PAIR
    return pl.pallas_call(
        attend_back_kernel,
        grid=(pairs,),
        in_specs=[
            pl.BlockSpec((2, rows, near), lambda i: (i, 0, 0)),
            pl.BlockSpec((rows, PAIR), lambda i: (0, i)),
            pl.BlockSpec((rows, PAIR), lambda i: (0, i)),
            pl.BlockSpec((near, 2 * PAIR), lambda i: (0, i)),
        ],
        out_specs=[
            pl.BlockSpec((rows, PAIR), lambda i: (0, i)),
            pl.BlockSpec((near, 2 * PAIR), lambda i: (0, i)),
        ],
        out_shape=[
            jax.ShapeDtypeStruct((rows, pairs * PAIR), LOW),
            jax.ShapeDtypeStruct((near, 2 * pairs * PAIR), LOW),
        ],
        compiler_params=pltpu.CompilerParams(vmem_limit_bytes=VMEM_BYTES),
        cost_estimate=pl.CostEstimate(
            flops=32 * pairs * rows * near * PAIR,
            bytes_accessed=8 * pairs * rows * near,
            transcendentals=0,
        ),
    )(weights, grad, query, kv)


def paired_columns(x):
    rows = x.shape[0]
    query = x[:, :D].reshape(rows, 2, SIDE * PAIR)
    kv = x[:, D:].reshape(rows, 2, 2, SIDE, PAIR).transpose(0, 2, 3, 1, 4)
    kv = kv.reshape(rows, 2, 2 * SIDE * PAIR)
    return [jnp.concatenate([query[:, s], kv[:, s]], axis=1) for s in range(2)]


def plain_columns(sides):
    rows, wide = sides[0].shape[0], SIDE * PAIR
    query = [side[:, :wide] for side in sides]
    kv = [side[:, wide:].reshape(rows, SIDE, 2, PAIR).transpose(0, 2, 1, 3) for side in sides]
    key_value = [kv[s][:, which].reshape(rows, wide) for which in range(2) for s in range(2)]
    return jnp.concatenate(query + key_value, axis=1)


def outer_sum(operand_a, operand_b):
    return jnp.einsum("ti,tj->ij", operand_a, operand_b, preferred_element_type=FULL).astype(LOW)


def body(
    tokens,
    cotangent,
    starts,
    w_qkv,
    m_qkv,
    v_qkv,
    w_out,
    m_out,
    v_out,
    w_up,
    m_up,
    v_up,
    w_down,
    m_down,
    v_down,
    vectors,
    m_vec,
    v_vec,
):
    ix = Index()
    rows = D // ix.count
    tok_rows = tokens.shape[0]
    reach_count = (SEQ_MOST + tok_rows - 2) // tok_rows
    near_rows = (reach_count + 1) * tok_rows
    scale = HEAD_DIM ** (-0.5)
    odd = ix.bit(0) == 1
    ahead = tuple(reversed(ix.middle))
    back = ix.middle

    assert reach_count == 4
    two_before, four_before = shifted(tokens, 2), shifted(tokens, 4)
    from_mate = flipped(
        jnp.where(
            odd,
            jnp.concatenate([two_before, four_before], axis=0),
            jnp.concatenate([tokens, two_before], axis=0),
        ),
        1,
    )
    near_tokens = jnp.concatenate(
        [four_before, from_mate[tok_rows:], two_before, from_mate[:tok_rows], tokens], axis=0
    )

    wide = SIDE * PAIR
    columns = 3 * wide
    vec_piece = jnp.pad(vectors.astype(LOW).reshape(rows, VCOLS), ((0, 0), (0, 128 - VCOLS)))
    first = gather_top(
        ix,
        jnp.concatenate(
            paired_columns(w_qkv.astype(LOW).reshape(rows, 3 * D)) + [vec_piece], axis=1
        ),
    )
    second = gather_top(
        ix,
        jnp.concatenate(
            [w_out.astype(LOW).reshape(rows, D), w_up.astype(LOW).reshape(rows, FF)], axis=1
        ),
    )
    third = gather_top(ix, w_down.astype(LOW).reshape(4 * rows, D))
    left = gather_bits(ix, first[..., :columns], ahead[:1])
    right = gather_bits(ix, first[..., columns:], back[:1])
    left, right, second = lax.optimization_barrier((left, right, second))
    left = joined_rows(gather_bits(ix, left, ahead[1:] + (0,)))
    right = joined_rows(gather_bits(ix, right, back[1:] + (0,)))
    cut = (D + FF) // 2
    second_left = gather_bits(ix, second[..., :cut], ahead[:1])
    second_right = gather_bits(ix, second[..., cut:], back[:1])
    left, right, second_left, second_right, third = lax.optimization_barrier(
        (left, right, second_left, second_right, third)
    )
    second_left = joined_rows(gather_bits(ix, second_left, ahead[1:] + (0,)))
    second_right = joined_rows(gather_bits(ix, second_right, back[1:] + (0,)))
    third = gather_bits(ix, third, back[:1])
    qkv_w = (left, right[:, :columns])
    vec_all = right[:, columns : columns + VCOLS].reshape(-1).astype(FULL)
    vec_table, up_bias = vec_all[: 8 * D].reshape(D, 8), vec_all[8 * D :]
    gain_one, shift_one, bias_q, bias_v, bias_o, gain_two, shift_two, bias_down = (
        vec_table[:, i] for i in range(8)
    )

    inputs = tokens.astype(FULL)
    near_unit, near_inverse = norm_parts(near_tokens.astype(FULL))
    near_normed = (near_unit * gain_one + shift_one).astype(LOW)
    normed = near_normed[near_rows - tok_rows :]
    kv_bias = jnp.stack(
        [jnp.zeros((PAIRS, PAIR), FULL), bias_v.reshape(PAIRS, PAIR)], axis=1
    ).reshape(2, 2 * wide)
    q_bias = bias_q.reshape(2, wide)
    first_key = (starts - (ix.me - reach_count) * tok_rows)[:, None]
    query, kv, attended, weights = [], [], [], []
    for s in range(2):
        weight = qkv_w[s]
        query.append(
            (jnp.dot(normed, weight[:, :wide], preferred_element_type=FULL) + q_bias[s]).astype(LOW)
        )
        kv.append(
            (
                jnp.dot(near_normed, weight[:, wide:], preferred_element_type=FULL) + kv_bias[s]
            ).astype(LOW)
        )
        mixed, kept = attend(first_key, query[s], kv[s])
        attended.append(mixed)
        weights.append(kept)
    attended = jnp.concatenate(attended, axis=1)
    attended, second_left, second_right, third = lax.optimization_barrier(
        (attended, second_left, second_right, third)
    )
    second = jnp.concatenate([second_left, second_right], axis=1)
    out_w, up_w = second[:, :D], second[:, D:]
    down_w = joined_rows(gather_bits(ix, third, back[1:] + (0,)))

    branch = jnp.dot(attended, out_w, preferred_element_type=FULL) + bias_o
    middle = inputs + branch
    unit_two, inverse_two = norm_parts(middle)
    normed_two = (unit_two * gain_two + shift_two).astype(LOW)
    hidden_pre = jnp.dot(normed_two, up_w, preferred_element_type=FULL) + up_bias
    hidden_low = smooth_act(hidden_pre).astype(LOW)
    result = middle + (jnp.dot(hidden_low, down_w, preferred_element_type=FULL) + bias_down)
    out_tokens = result.astype(LOW)

    grad_out = cotangent.astype(FULL)
    grad_downw = outer_sum(hidden_low, cotangent)
    sum_down = scatter_bits(ix, spread_rows(ix, grad_downw), (0,))
    grad_hidden = jnp.dot(cotangent, down_w.T, preferred_element_type=FULL)
    act_value, act_back = jax.vjp(smooth_act, hidden_pre)
    grad_pre = act_back(grad_hidden)[0].astype(LOW)
    grad_pre, sum_down = lax.optimization_barrier((grad_pre, sum_down))
    first_step, last_step = slice(0, 1), slice(1, None)
    sum_down = scatter_sides(ix, halves(sum_down), first_step)
    grad_upw = outer_sum(normed_two, grad_pre)
    grad_normed_two = jnp.dot(grad_pre, up_w.T, preferred_element_type=FULL)
    grad_gain_two = jnp.sum(grad_normed_two * unit_two, axis=0)
    grad_shift_two = jnp.sum(grad_normed_two, axis=0)
    grad_middle = grad_out + norm_back(grad_normed_two, unit_two, inverse_two, gain_two)
    grad_branch = grad_middle.astype(LOW)
    grad_outw = outer_sum(attended, grad_branch)
    sum_second = scatter_bits(
        ix, spread_rows(ix, jnp.concatenate([grad_outw, grad_upw], axis=1)), (0,)
    )
    grad_attended = jnp.dot(grad_branch, out_w.T, preferred_element_type=FULL).astype(LOW)

    grad_near = 0.0
    grad_query, grad_kv, sums = [], [], []
    for s in range(2):
        part = slice(s * wide, (s + 1) * wide)
        dq, dkv = attend_back(weights[s], grad_attended[:, part], query[s], kv[s])
        if s == 0:
            dq, dkv, grad_attended, sum_down, sum_second = lax.optimization_barrier(
                (dq, dkv, grad_attended, sum_down, sum_second)
            )
            sum_down = scatter_sides(ix, sum_down, last_step)
            sum_second = scatter_sides(ix, halves(sum_second), first_step)
        else:
            dq, dkv, sum_down, sums = lax.optimization_barrier((dq, dkv, sum_down, sums))
            sum_down = scatter_top(ix, jnp.concatenate(sum_down, axis=-1))
        grad_query.append(dq)
        grad_kv.append(dkv)
        weight = qkv_w[s]
        grad_near = grad_near + jnp.dot(dkv, weight[:, wide:].T, preferred_element_type=FULL)
        grad_near = grad_near + jnp.pad(
            jnp.dot(dq, weight[:, :wide].T, preferred_element_type=FULL),
            ((near_rows - tok_rows, 0), (0, 0)),
        )
        side_sum = jnp.concatenate([outer_sum(normed, dq), outer_sum(near_normed, dkv)], axis=1)
        if s == 0:
            side_sum = scatter_bits(ix, spread_rows(ix, side_sum), (0,))
        sums.append(side_sum)
    grad_gain_one = jnp.sum(grad_near * near_unit, axis=0)
    grad_shift_one = jnp.sum(grad_near, axis=0)

    grad_kv_sum = jnp.stack([jnp.sum(g.astype(FULL), axis=0) for g in grad_kv])
    vec_rows = jnp.stack(
        [
            grad_gain_one,
            grad_shift_one,
            jnp.concatenate([jnp.sum(g.astype(FULL), axis=0) for g in grad_query]),
            grad_kv_sum.reshape(PAIRS, 2, PAIR)[:, 1].reshape(-1),
            jnp.sum(grad_branch.astype(FULL), axis=0),
            grad_gain_two,
            grad_shift_two,
            jnp.sum(grad_out, axis=0),
        ],
        axis=1,
    )
    grad_vec = jnp.concatenate([vec_rows.reshape(-1), jnp.sum(grad_pre.astype(FULL), axis=0)])
    grad_vec = jnp.pad(grad_vec.astype(LOW).reshape(D, VCOLS), ((0, 0), (0, 128 - VCOLS)))
    sum_right = scatter_bits(
        ix, spread_rows(ix, jnp.concatenate([sums[1], grad_vec], axis=1)), (0,)
    )
    sum_second = scatter_sides(ix, sum_second, last_step)
    sum_first = scatter_sides(ix, (sums[0], sum_right), first_step)
    sum_first = scatter_sides(ix, sum_first, last_step)
    sum_second = scatter_top(ix, jnp.concatenate(sum_second, axis=-1))
    sum_first = scatter_top(ix, jnp.concatenate(sum_first, axis=-1))

    parts = grad_near.astype(LOW).reshape(reach_count + 1, tok_rows, D)
    from_mate = flipped(jnp.concatenate([parts[3], parts[1]], axis=0), 1)
    near_mate, far_mate = from_mate[:tok_rows].astype(FULL), from_mate[tok_rows:].astype(FULL)
    own = grad_near[near_rows - tok_rows :] + jnp.where(odd, 0.0, near_mate)
    two_back = parts[2].astype(FULL) + jnp.where(odd, near_mate, far_mate)
    four_back = parts[0].astype(FULL) + jnp.where(odd, far_mate, 0.0)
    own = (
        own
        + shifted(two_back.astype(LOW), -2).astype(FULL)
        + shifted(four_back.astype(LOW), -4).astype(FULL)
    )
    unit_one = near_unit[near_rows - tok_rows :]
    inverse_one = near_inverse[near_rows - tok_rows :]
    input_grad = grad_middle + norm_back(own, unit_one, inverse_one, gain_one)

    rate_qkv, rate_out, rate_up, rate_down = matrix_rates()
    entries = ix.me * vectors.shape[0] + jnp.arange(vectors.shape[0], dtype=jnp.int32)
    g_qkv = plain_columns((sum_first[:, :columns], sum_first[:, columns : 2 * columns])).reshape(-1)
    g_vec = sum_first[:, 3 * D : 3 * D + VCOLS].reshape(-1)
    g_out = sum_second[:, :D].reshape(-1)
    g_up = sum_second[:, D:].reshape(-1)
    g_down = sum_down.reshape(-1)
    qkv_new = adamw(w_qkv, m_qkv, v_qkv, g_qkv, rate_qkv, DECAY_RATE)
    out_new = adamw(w_out, m_out, v_out, g_out, rate_out, DECAY_RATE)
    up_new = adamw(w_up, m_up, v_up, g_up, rate_up, DECAY_RATE)
    down_new = adamw(w_down, m_down, v_down, g_down, rate_down, DECAY_RATE)
    vec_new = adamw(vectors, m_vec, v_vec, g_vec, vector_rates(entries), 0.0)
    return (out_tokens, input_grad) + qkv_new + out_new + up_new + down_new + vec_new


def solution(mesh):
    in_specs = (P("dev", None), P("dev", None)) + (P("dev"),) * 16
    out_specs = (P("dev", None), P("dev", None)) + (P("dev"),) * 15
    return jax.shard_map(body, mesh=mesh, in_specs=in_specs, out_specs=out_specs, check_vma=False)
```

```python
import jax
import jax.numpy as jnp
from jax import lax
from jax.experimental import pallas as pl
from jax.experimental.pallas import tpu as pltpu
from jax.sharding import PartitionSpec as P

D = 768
HEAD_DIM = 64
HEADS = D // HEAD_DIM
FF = 3072
SEQ_MOST = 1024
STEP = 10
VCOLS = 12


NORM_EPS = 1e-05
BETA_ONE = 0.9
BETA_TWO = 0.999
ADAM_EPS = 1e-08
DECAY_RATE = 0.01
NEG_LARGE = -1e30

LOW = jnp.bfloat16
FULL = jnp.float32


def norm_parts(values):
    centre = jnp.mean(values, axis=-1, keepdims=True)
    centred = values - centre
    spread = jnp.mean(centred * centred, axis=-1, keepdims=True)
    inverse = lax.rsqrt(spread + NORM_EPS)
    return centred * inverse, inverse


def norm_back(grad, unit, inverse, gain_vec):
    scaled = grad * gain_vec
    along = jnp.mean(scaled * unit, axis=-1, keepdims=True)
    return inverse * (scaled - jnp.mean(scaled, axis=-1, keepdims=True) - unit * along)


def smooth_act(values):
    return jax.nn.gelu(values, approximate=True)


def adamw(weight, moment, second, gradient, step_rate, decay_rate):
    moment = BETA_ONE * moment + (1.0 - BETA_ONE) * gradient
    second = BETA_TWO * second + (1.0 - BETA_TWO) * gradient * gradient
    first_hat = moment / (1.0 - BETA_ONE**STEP)
    second_hat = second / (1.0 - BETA_TWO**STEP)
    weight = weight - step_rate * (
        first_hat / (jnp.sqrt(second_hat) + ADAM_EPS) + decay_rate * weight
    )
    return (moment, second, weight)


def matrix_rates():
    return (
        2.5 * D ** (-0.5),
        2.5 * max(1, D * 16 // SEQ_MOST) ** (-0.5),
        2.5 * D ** (-0.5),
        2.5 * FF ** (-0.5),
    )


def vector_rates(entries):
    column = entries % 8
    is_gain = (entries < 8 * D) & ((column == 0) | (column == 5))
    return jnp.where(is_gain, 0.3, 0.05).astype(jnp.float32)


def shifted(x, by):
    length = lax.axis_size("dev")
    return lax.ppermute(x, "dev", [(i, i + by) for i in range(length) if 0 <= i + by < length])


def flipped(x, mask):
    return lax.ppermute(x, "dev", [(i, i ^ mask) for i in range(lax.axis_size("dev"))])


def tied(*arrays):
    return lax.optimization_barrier(arrays)


class Index:
    def __init__(self):
        self.count = lax.axis_size("dev")
        self.me = lax.axis_index("dev")
        self.top = self.count.bit_length() - 3
        self.core = self.me & 1
        self.odd = self.core == 1
        middle = tuple(range(1, self.top))
        self.orders = (middle, tuple(reversed(middle)))

    def relative(self, order):
        seen = [r << self.top for r in range(4)]
        for b in reversed(order):
            seen = seen + [s | 1 << b for s in seen]
        return [s >> 1 for s in seen]


def by_core(ix, own, other):
    return jnp.where(ix.odd, other, own), jnp.where(ix.odd, own, other)


def cut_sides(x):
    cut = x.shape[-1] // 256 * 128
    return (x[..., :cut], x[..., cut:])


def gather_top(ix, piece):
    return jnp.stack([piece] + [flipped(piece, r << ix.top) for r in (1, 2, 3)])


def gather_mid(ix, sides):
    done = []
    for x, order in zip(sides, ix.orders):
        for b in reversed(order[1:]):
            x = jnp.concatenate([x, flipped(x, 1 << b)], axis=0)
        done.append(x)
    return done


def gather_last(ix, sides):
    return [(x, flipped(x, 1 << order[0])) for x, order in zip(sides, ix.orders)]


def place_kernel(rows, moves, chip_ref, *refs):
    ins, outs, sem = refs[: moves[0]], refs[moves[0] : -1], refs[-1]
    chip = chip_ref[0]
    copies = []
    for source, at, target, relative, column, width in moves[1]:
        start = pl.multiple_of((chip ^ relative) * rows, rows)
        spot = (pl.ds(start, rows), pl.ds(column, width))
        if at[0] == 0:
            copy = (ins[source].at[at[1]], outs[target].at[spot])
        else:
            copy = (ins[source].at[spot], outs[target].at[at[1]])
        copies.append(pltpu.make_async_copy(*copy, sem.at[len(copies)]))
        copies[-1].start()
    for copy in copies:
        copy.wait()


def place(ix, rows, ins, moves, out_shape):
    return pl.pallas_call(
        lambda *refs: place_kernel(rows, (len(ins), moves), *refs),
        in_specs=[pl.BlockSpec(memory_space=pltpu.SMEM)]
        + [pl.BlockSpec(memory_space=pl.ANY)] * len(ins),
        out_specs=[pl.BlockSpec(memory_space=pl.ANY)] * len(out_shape),
        out_shape=[jax.ShapeDtypeStruct(shape, LOW) for shape in out_shape],
        scratch_shapes=[pltpu.SemaphoreType.DMA((len(moves),))],
        cost_estimate=pl.CostEstimate(
            flops=0, bytes_accessed=4 * sum(rows * m[5] for m in moves), transcendentals=0
        ),
    )((ix.me >> 1).astype(jnp.int32).reshape(1), *ins)


def assemble(ix, sides):
    chips = ix.count // 2
    rows = sides[0][0].shape[1]
    widths = [side[0].shape[2] for side in sides]
    if rows % 16:
        whole = []
        for side, order in zip(sides, ix.orders):
            place_of = [0] * chips
            for spot, relative in enumerate(ix.relative(order)):
                place_of[relative] = spot
            pick = jnp.array(place_of, jnp.int32)[(ix.me >> 1) ^ jnp.arange(chips)]
            full = jnp.take(jnp.concatenate(side, axis=0), pick, axis=0)
            whole.append(full.reshape(chips * rows, -1))
        return jnp.concatenate(whole, axis=1)
    moves = []
    for s, order in enumerate(ix.orders):
        for spot, relative in enumerate(ix.relative(order)):
            half, at = divmod(spot, chips // 2)
            moves.append((2 * s + half, (0, at), 0, relative, s * widths[0], widths[s]))
    ins = [array for side in sides for array in side]
    return place(ix, rows, ins, moves, [(chips * rows, sum(widths))])[0]


def take_apart(ix, whole):
    chips = ix.count // 2
    rows = whole.shape[0] // chips
    if rows % 16:
        sides = []
        for side, order in zip(cut_sides(whole), ix.orders):
            pick = (ix.me >> 1) ^ jnp.array(ix.relative(order), jnp.int32)
            full = jnp.take(side.reshape(chips, rows, -1), pick, axis=0)
            sides.append((full[: chips // 2], full[chips // 2 :]))
        return sides
    widths = [side.shape[1] for side in cut_sides(whole)]
    moves, shapes = [], []
    for s, order in enumerate(ix.orders):
        shapes += [(chips // 2, rows, widths[s])] * 2
        for spot, relative in enumerate(ix.relative(order)):
            half, at = divmod(spot, chips // 2)
            moves.append((0, (1, at), 2 * s + half, relative, s * widths[0], widths[s]))
    outs = place(ix, rows, [whole], moves, shapes)
    return [(outs[0], outs[1]), (outs[2], outs[3])]


def settle(keep, other, parts):
    size = keep.shape[0] // parts
    return [
        (
            keep[i * size : (i + 1) * size].astype(FULL)
            + other[i * size : (i + 1) * size].astype(FULL)
        ).astype(LOW)
        for i in range(parts)
    ]


def scatter_mid(ix, sides, first, last):
    done = []
    for (keep, send), order in zip(sides, ix.orders):
        for i in range(first, min(last, len(order))):
            parts = 2 if i < len(order) - 1 else 4
            settled = settle(keep, flipped(send, 1 << order[i]), parts)
            keep, send = settled[0], settled[1] if parts == 2 else settled[1:]
        done.append((keep, send))
    return done


def scatter_top(ix, sides):
    total = jnp.concatenate([keep[0] for keep, _ in sides], axis=-1).astype(FULL)
    for r in (1, 2, 3):
        part = jnp.concatenate([send[r - 1][0] for _, send in sides], axis=-1)
        total = total + flipped(part, r << ix.top).astype(FULL)
    return total


def own_rows(ix, summed):
    rows = summed.shape[0] // 2
    keep = lax.dynamic_slice_in_dim(summed, ix.core * rows, rows, 0)
    other = lax.dynamic_slice_in_dim(summed, (1 - ix.core) * rows, rows, 0)
    return keep, flipped(other, 1)


PAIR = 2 * HEAD_DIM
PAIRS = HEADS // 2
SIDE = PAIRS // 2
SCALE = HEAD_DIM ** (-0.5)
VMEM_BYTES = 48 * 1024 * 1024


def by_head(pair):
    low_half = lax.broadcasted_iota(jnp.int32, pair.shape, 1) < HEAD_DIM
    zero = jnp.zeros_like(pair)
    return (
        low_half,
        jnp.where(low_half, pair, zero).astype(LOW),
        jnp.where(low_half, zero, pair).astype(LOW),
    )


def dot_over(operand_a, operand_b, dim_a, dim_b):
    return lax.dot_general(
        operand_a, operand_b, (((dim_a,), (dim_b,)), ((), ())), preferred_element_type=FULL
    )


def attend_kernel(first_ref, q_ref, kv_ref, out_ref, weights_ref):
    rows, near = weights_ref.shape[-2:]
    key = lax.broadcasted_iota(jnp.int32, (rows, near), 1)
    last = lax.broadcasted_iota(jnp.int32, (rows, near), 0) + (near - rows)
    for block in range(2):
        own, seen = pl.ds(block * rows, rows), pl.ds(block * rows, near)
        low_half, *q_heads = by_head(q_ref[own, :].astype(FULL) * SCALE)
        k, v = kv_ref[seen, :PAIR], kv_ref[seen, PAIR:]
        allowed = (key >= first_ref[own, :] - block * rows) & (key <= last)
        blended = []
        for head in range(2):
            scores = jnp.where(allowed, dot_over(q_heads[head], k, 1, 1), NEG_LARGE)
            weights = jnp.exp(scores - jnp.max(scores, axis=-1, keepdims=True))
            weights = weights * (1.0 / jnp.sum(weights, axis=-1, keepdims=True))
            weights = weights.astype(LOW)
            weights_ref[0, 2 * block + head] = weights
            blended.append(dot_over(weights, v, 1, 0))
        out_ref[own, :] = jnp.where(low_half, blended[0], blended[1]).astype(LOW)


def attend(first_key, query, kv, rows, first, pairs):
    near = kv.shape[0] - rows
    return pl.pallas_call(
        attend_kernel,
        grid=(pairs,),
        in_specs=[
            pl.BlockSpec((2 * rows, 1), lambda i: (0, 0)),
            pl.BlockSpec((2 * rows, PAIR), lambda i: (0, i + first)),
            pl.BlockSpec((near + rows, 2 * PAIR), lambda i: (0, i + first)),
        ],
        out_specs=[
            pl.BlockSpec((2 * rows, PAIR), lambda i: (0, i)),
            pl.BlockSpec((1, 4, rows, near), lambda i: (i, 0, 0, 0)),
        ],
        out_shape=[
            jax.ShapeDtypeStruct((2 * rows, pairs * PAIR), LOW),
            jax.ShapeDtypeStruct((pairs, 4, rows, near), LOW),
        ],
        compiler_params=pltpu.CompilerParams(vmem_limit_bytes=VMEM_BYTES),
        cost_estimate=pl.CostEstimate(
            flops=32 * pairs * rows * near * PAIR,
            bytes_accessed=16 * pairs * rows * near,
            transcendentals=4 * pairs * rows * near,
        ),
    )(first_key, query, kv)


def attend_back_kernel(weights_ref, grad_ref, q_ref, kv_ref, dq_ref, dkv_ref):
    rows, near = weights_ref.shape[-2:]
    turned = []
    for block in range(2):
        own, seen = pl.ds(block * rows, rows), pl.ds(block * rows, near)
        low_half, *grad_heads = by_head(grad_ref[own, :].astype(FULL))
        _, *q_heads = by_head(q_ref[own, :].astype(FULL))
        k, v = kv_ref[seen, :PAIR], kv_ref[seen, PAIR:]
        dq = []
        dk_turned = dv_turned = 0.0
        for head in range(2):
            weights_low = weights_ref[0, 2 * block + head]
            weights = weights_low.astype(FULL)
            grad_weights = dot_over(grad_heads[head], v, 1, 1)
            inner_sum = jnp.sum(weights * grad_weights, axis=-1, keepdims=True)
            grad_scores = (weights * (grad_weights - inner_sum)).astype(LOW)
            dq.append(dot_over(grad_scores, k, 1, 0))
            dk_turned += dot_over(q_heads[head], grad_scores, 0, 0)
            dv_turned += dot_over(grad_heads[head], weights_low, 0, 0)
        dq_ref[own, :] = (jnp.where(low_half, dq[0], dq[1]) * SCALE).astype(LOW)
        turned.append((dk_turned * SCALE, dv_turned))
    for which in range(2):
        early, late = turned[0][which], turned[1][which]
        whole = jnp.concatenate(
            [early[:, :rows], early[:, rows:] + late[:, : near - rows], late[:, near - rows :]],
            axis=1,
        )
        dkv_ref[:, which * PAIR : (which + 1) * PAIR] = whole.T.astype(LOW)


def attend_back(weights, grad, query, kv, rows, first, pairs):
    near = kv.shape[0] - rows
    return pl.pallas_call(
        attend_back_kernel,
        grid=(pairs,),
        in_specs=[
            pl.BlockSpec((1, 4, rows, near), lambda i: (i, 0, 0, 0)),
            pl.BlockSpec((2 * rows, PAIR), lambda i: (0, i + first)),
            pl.BlockSpec((2 * rows, PAIR), lambda i: (0, i + first)),
            pl.BlockSpec((near + rows, 2 * PAIR), lambda i: (0, i + first)),
        ],
        out_specs=[
            pl.BlockSpec((2 * rows, PAIR), lambda i: (0, i)),
            pl.BlockSpec((near + rows, 2 * PAIR), lambda i: (0, i)),
        ],
        out_shape=[
            jax.ShapeDtypeStruct((2 * rows, pairs * PAIR), LOW),
            jax.ShapeDtypeStruct((near + rows, 2 * pairs * PAIR), LOW),
        ],
        compiler_params=pltpu.CompilerParams(vmem_limit_bytes=VMEM_BYTES),
        cost_estimate=pl.CostEstimate(
            flops=64 * pairs * rows * near * PAIR,
            bytes_accessed=16 * pairs * rows * near,
            transcendentals=0,
        ),
    )(weights, grad, query, kv)


def paired_columns(x):
    rows = x.shape[0]
    query = x[:, :D].reshape(rows, 2, SIDE * PAIR)
    kv = x[:, D:].reshape(rows, 2, 2, SIDE, PAIR).transpose(0, 2, 3, 1, 4)
    kv = kv.reshape(rows, 2, 2 * SIDE * PAIR)
    return [jnp.concatenate([query[:, s], kv[:, s]], axis=1) for s in range(2)]


def plain_columns(sides):
    rows, wide = sides[0].shape[0], SIDE * PAIR
    query = [side[:, :wide] for side in sides]
    kv = [side[:, wide:].reshape(rows, SIDE, 2, PAIR).transpose(0, 2, 1, 3) for side in sides]
    key_value = [kv[s][:, which].reshape(rows, wide) for which in range(2) for s in range(2)]
    return jnp.concatenate(query + key_value, axis=1)


def hidden_columns(x, share):
    parts = x.reshape(x.shape[0], FF // (2 * share), 2, share)
    return [parts[:, :, s].reshape(x.shape[0], FF // 2) for s in range(2)]


def plain_hidden(sides, share):
    rows = sides[0].shape[0]
    parts = [side.reshape(rows, FF // (2 * share), 1, share) for side in sides]
    return jnp.concatenate(parts, axis=2).reshape(rows, FF)


def dot(operand_a, operand_b):
    return jnp.dot(operand_a, operand_b, preferred_element_type=FULL)


def outer_sum(operand_a, operand_b):
    return jnp.einsum("ti,tj->ij", operand_a, operand_b, preferred_element_type=FULL).astype(LOW)


def dot_turned(operand_a, operand_b):
    return jnp.einsum("ti,ji->tj", operand_a, operand_b, preferred_element_type=FULL)


def body(
    tokens,
    cotangent,
    starts,
    w_qkv,
    m_qkv,
    v_qkv,
    w_out,
    m_out,
    v_out,
    w_up,
    m_up,
    v_up,
    w_down,
    m_down,
    v_down,
    vectors,
    m_vec,
    v_vec,
):
    ix = Index()
    rows = D // ix.count
    share = FF // ix.count
    tok_rows = tokens.shape[0]
    reach_count = (SEQ_MOST + tok_rows - 2) // tok_rows
    assert reach_count == 4
    chip_rows = 2 * tok_rows
    near_rows = (reach_count + 2) * tok_rows
    wide = SIDE * PAIR
    columns = 3 * wide
    out_wide, up_wide = D // 2, FF // 2

    vec_piece = jnp.pad(vectors.astype(LOW).reshape(rows, VCOLS), ((0, 0), (0, 128 - VCOLS)))
    qkv_sides = paired_columns(w_qkv.astype(LOW).reshape(rows, 3 * D))
    up_sides = hidden_columns(w_up.astype(LOW).reshape(rows, FF), share)
    out_low = w_out.astype(LOW).reshape(rows, D)
    pieces = [
        jnp.concatenate(
            [qkv_sides[s], vec_piece, out_low[:, s * out_wide : (s + 1) * out_wide], up_sides[s]],
            axis=1,
        )
        for s in range(2)
    ]
    mine, others = by_core(ix, *pieces)
    both = jnp.concatenate(by_core(ix, mine, flipped(others, 1)), axis=0)
    first, second = both[:, : columns + 128], both[:, columns + 128 :]
    first = gather_top(ix, first)

    mine = jnp.stack([shifted(tokens, 4), shifted(tokens, 2), tokens])
    near_tokens = jnp.stack(by_core(ix, mine, flipped(mine, 1)), axis=1).reshape(near_rows, D)
    chip_starts = jnp.concatenate(by_core(ix, starts, flipped(starts, 1)))
    chip_cotangent = jnp.concatenate(by_core(ix, cotangent, flipped(cotangent, 1)), axis=0)

    first, second, near_tokens, chip_starts = tied(first, second, near_tokens, chip_starts)
    second = gather_top(ix, second)
    first = gather_last(ix, gather_mid(ix, cut_sides(first)))
    third = w_down.astype(LOW).reshape(4 * rows, D)
    first, second, third, chip_cotangent = tied(first, second, third, chip_cotangent)
    third = gather_top(ix, third)
    second = gather_mid(ix, cut_sides(second))
    first = assemble(ix, first)
    qkv_w = first[:, :columns]
    vec_all = first[:, columns : columns + VCOLS].reshape(-1).astype(FULL)
    vec_table, up_bias = vec_all[: 8 * D].reshape(D, 8).T, vec_all[8 * D :]
    gain_one, shift_one, bias_q, bias_v, bias_o, gain_two, shift_two, bias_down = (
        vec_table[i] for i in range(8)
    )
    up_bias = lax.dynamic_index_in_dim(
        up_bias.reshape(ix.count // 2, 2, share), ix.core, 1, keepdims=False
    ).reshape(up_wide)
    bias_q = lax.dynamic_slice_in_dim(bias_q, ix.core * wide, wide)
    bias_v = lax.dynamic_slice_in_dim(bias_v, ix.core * wide, wide)

    near_unit, near_inverse = norm_parts(near_tokens.astype(FULL))
    near_normed = (near_unit * gain_one + shift_one).astype(LOW)
    normed = near_normed[near_rows - chip_rows :]
    kv_bias = jnp.stack(
        [jnp.zeros((SIDE, PAIR), FULL), bias_v.reshape(SIDE, PAIR)], axis=1
    ).reshape(2 * wide)
    first_key = (chip_starts - ((ix.me >> 1) * chip_rows - reach_count * tok_rows))[:, None]
    query = (dot(normed, qkv_w[:, :wide]) + bias_q).astype(LOW)
    kv = (dot(near_normed, qkv_w[:, wide:]) + kv_bias).astype(LOW)
    query, kv, second = tied(query, kv, second)
    second = gather_last(ix, second)
    splits = ((0, SIDE - 1), (SIDE - 1, 1))
    mixed, weights = [None, None], [None, None]
    mixed[0], weights[0] = attend(first_key, query, kv, tok_rows, *splits[0])
    mixed[0], query, third = tied(mixed[0], query, third)
    third = gather_mid(ix, cut_sides(third))
    mixed[1], weights[1] = attend(first_key, query, kv, tok_rows, *splits[1])
    mixed = jnp.concatenate(mixed, axis=1)
    mixed, second, third = tied(mixed, second, third)
    third = gather_last(ix, third)
    attended = jnp.concatenate(by_core(ix, mixed, flipped(mixed, 1)), axis=1)
    second = assemble(ix, second)
    out_half, up_w = second[:, :out_wide], second[:, out_wide:]
    out_w = jnp.concatenate(by_core(ix, out_half, flipped(out_half, 1)), axis=1)

    inputs = near_tokens[near_rows - chip_rows :].astype(FULL)
    middle = inputs + (dot(attended, out_w) + bias_o)
    unit_two, inverse_two = norm_parts(middle)
    normed_two = (unit_two * gain_two + shift_two).astype(LOW)
    hidden_pre = dot(normed_two, up_w) + up_bias
    hidden_low = smooth_act(hidden_pre).astype(LOW)
    grad_downw = outer_sum(hidden_low, chip_cotangent)
    hidden_low, hidden_pre, grad_downw = tied(hidden_low, hidden_pre, grad_downw)
    sum_down = scatter_mid(ix, take_apart(ix, grad_downw), 0, 1)
    down_w = assemble(ix, third)
    result = dot(hidden_low, down_w).reshape(2, tok_rows, D)
    own_result, other_result = by_core(ix, result[0], result[1])
    own_result = own_result + flipped(other_result.astype(LOW), 1).astype(FULL)
    own_middle = lax.dynamic_slice_in_dim(middle, ix.core * tok_rows, tok_rows, 0)
    out_tokens = (own_middle + (own_result + bias_down)).astype(LOW)

    grad_hidden = dot_turned(chip_cotangent, down_w)
    act_value, act_back = jax.vjp(smooth_act, hidden_pre)
    grad_pre = act_back(grad_hidden)[0].astype(LOW)
    partial_two = dot_turned(grad_pre, up_w)
    grad_gain_two = jnp.sum(partial_two * unit_two, axis=0)
    grad_shift_two = jnp.sum(partial_two, axis=0)
    grad_normed_two = partial_two + flipped(partial_two.astype(LOW), 1).astype(FULL)
    grad_upw = outer_sum(normed_two, grad_pre)
    grad_middle = chip_cotangent.astype(FULL) + norm_back(
        grad_normed_two, unit_two, inverse_two, gain_two
    )
    grad_branch = grad_middle.astype(LOW)
    own_part = lax.dynamic_slice_in_dim(grad_branch, ix.core * out_wide, out_wide, 1)
    grad_second = jnp.concatenate([outer_sum(attended, own_part), grad_upw], axis=1)
    own_out = lax.dynamic_slice_in_dim(out_w, ix.core * wide, wide, 0)
    grad_mixed = dot_turned(grad_branch, own_out).astype(LOW)
    grad_mixed, grad_second, sum_down = tied(grad_mixed, grad_second, sum_down)
    sum_second = scatter_mid(ix, take_apart(ix, grad_second), 0, 1)
    sum_down = scatter_mid(ix, sum_down, 1, 9)
    dq, dkv = [None, None], [None, None]
    dq[0], dkv[0] = attend_back(weights[0], grad_mixed, query, kv, tok_rows, *splits[0])
    dq[0], dkv[0], grad_mixed, sum_down = tied(dq[0], dkv[0], grad_mixed, sum_down)
    sum_down = scatter_top(ix, sum_down)
    dq[1], dkv[1] = attend_back(weights[1], grad_mixed, query, kv, tok_rows, *splits[1])
    dq, dkv = jnp.concatenate(dq, axis=1), jnp.concatenate(dkv, axis=1)
    dq, dkv, sum_second = tied(dq, dkv, sum_second)
    sum_second = scatter_mid(ix, sum_second, 1, 9)

    grad_near = dot_turned(dkv, qkv_w[:, wide:]) + jnp.pad(
        dot_turned(dq, qkv_w[:, :wide]), ((near_rows - chip_rows, 0), (0, 0))
    )
    grad_gain_one = jnp.sum(grad_near * near_unit, axis=0)
    grad_shift_one = jnp.sum(grad_near, axis=0)
    own_half = (jnp.arange(2) == ix.core).astype(FULL)[:, None]
    grad_bias_v = jnp.sum(dkv.astype(FULL), axis=0).reshape(SIDE, 2, PAIR)[:, 1].reshape(1, wide)
    vec_rows = jnp.stack(
        [
            grad_gain_one,
            grad_shift_one,
            (jnp.sum(dq.astype(FULL), axis=0)[None] * own_half).reshape(D),
            (grad_bias_v * own_half).reshape(D),
            0.5 * jnp.sum(grad_branch.astype(FULL), axis=0),
            grad_gain_two,
            grad_shift_two,
            jnp.sum(cotangent.astype(FULL), axis=0),
        ],
        axis=0,
    )
    grad_bias_up = jnp.sum(grad_pre.astype(FULL), axis=0).reshape(ix.count // 2, 1, share)
    grad_vec = jnp.concatenate([vec_rows.T.reshape(-1), (grad_bias_up * own_half).reshape(-1)])
    grad_vec = lax.optimization_barrier(grad_vec).astype(LOW).reshape(D, VCOLS)
    grad_vec = jnp.pad(grad_vec, ((0, 0), (0, 128 - VCOLS)))
    grad_first = jnp.concatenate(
        [outer_sum(normed, dq), outer_sum(near_normed, dkv), grad_vec], axis=1
    )
    sum_first = scatter_mid(ix, take_apart(ix, grad_first), 0, 1)
    sum_second = scatter_top(ix, sum_second)
    sum_first = scatter_mid(ix, sum_first, 1, 9)

    blocks = grad_near.reshape(reach_count // 2 + 1, 2, tok_rows, D)
    own_blocks, other_blocks = by_core(ix, blocks[:, 0], blocks[:, 1])
    own_blocks = own_blocks + flipped(other_blocks.astype(LOW), 1).astype(FULL)
    four_back, two_back = own_blocks[0].astype(LOW), own_blocks[1].astype(LOW)
    own = (
        own_blocks[2]
        + shifted(two_back, -2).astype(FULL)
        + shifted(four_back, -4).astype(FULL)
    )
    unit_one, inverse_one = norm_parts(tokens.astype(FULL))
    own_grad_middle = lax.dynamic_slice_in_dim(grad_middle, ix.core * tok_rows, tok_rows, 0)
    input_grad = own_grad_middle + norm_back(own, unit_one, inverse_one, gain_one)

    sum_first = scatter_top(ix, sum_first)
    keep_second, other_second = own_rows(ix, sum_second)
    keep_first, other_first = own_rows(ix, sum_first)
    g_vec = (keep_first[:, columns:] + other_first[:, columns:])[:, :VCOLS].reshape(-1)
    g_qkv = plain_columns(by_core(ix, keep_first[:, :columns], other_first[:, :columns]))
    g_out = jnp.concatenate(
        by_core(ix, keep_second[:, :out_wide], other_second[:, :out_wide]), axis=1
    )
    g_up = plain_hidden(by_core(ix, keep_second[:, out_wide:], other_second[:, out_wide:]), share)

    rate_qkv, rate_out, rate_up, rate_down = matrix_rates()
    entries = ix.me * vectors.shape[0] + jnp.arange(vectors.shape[0], dtype=jnp.int32)
    qkv_new = adamw(w_qkv, m_qkv, v_qkv, g_qkv.reshape(-1), rate_qkv, DECAY_RATE)
    out_new = adamw(w_out, m_out, v_out, g_out.reshape(-1), rate_out, DECAY_RATE)
    up_new = adamw(w_up, m_up, v_up, g_up.reshape(-1), rate_up, DECAY_RATE)
    down_new = adamw(w_down, m_down, v_down, sum_down.reshape(-1), rate_down, DECAY_RATE)
    vec_new = adamw(vectors, m_vec, v_vec, g_vec, vector_rates(entries), 0.0)
    return (out_tokens, input_grad) + qkv_new + out_new + up_new + down_new + vec_new


def solution(mesh):
    in_specs = (P("dev", None), P("dev", None)) + (P("dev"),) * 16
    out_specs = (P("dev", None), P("dev", None)) + (P("dev"),) * 15
    return jax.shard_map(body, mesh=mesh, in_specs=in_specs, out_specs=out_specs, check_vma=False)
```

```python
import jax
import jax.numpy as jnp
from jax import lax
from jax.experimental import pallas as pl
from jax.experimental.pallas import tpu as pltpu
from jax.sharding import PartitionSpec as P

D = 768
HEAD_DIM = 64
HEADS = D // HEAD_DIM
FF = 3072
SEQ_MOST = 1024
STEP = 10
VCOLS = 12


NORM_EPS = 1e-05
BETA_ONE = 0.9
BETA_TWO = 0.999
ADAM_EPS = 1e-08
DECAY_RATE = 0.01
NEG_LARGE = -1e30

LOW = jnp.bfloat16
FULL = jnp.float32


def norm_parts(values):
    centre = jnp.mean(values, axis=-1, keepdims=True)
    centred = values - centre
    spread = jnp.mean(centred * centred, axis=-1, keepdims=True)
    inverse = lax.rsqrt(spread + NORM_EPS)
    return centred * inverse, inverse


def norm_back(grad, unit, inverse, gain_vec):
    scaled = grad * gain_vec
    along = jnp.mean(scaled * unit, axis=-1, keepdims=True)
    return inverse * (scaled - jnp.mean(scaled, axis=-1, keepdims=True) - unit * along)


def smooth_act(values):
    return jax.nn.gelu(values, approximate=True)


def adamw(weight, moment, second, gradient, step_rate, decay_rate):
    moment = BETA_ONE * moment + (1.0 - BETA_ONE) * gradient
    second = BETA_TWO * second + (1.0 - BETA_TWO) * gradient * gradient
    first_hat = moment / (1.0 - BETA_ONE**STEP)
    second_hat = second / (1.0 - BETA_TWO**STEP)
    weight = weight - step_rate * (
        first_hat / (jnp.sqrt(second_hat) + ADAM_EPS) + decay_rate * weight
    )
    return (moment, second, weight)


def matrix_rates():
    return (
        2.5 * D ** (-0.5),
        2.5 * max(1, D * 16 // SEQ_MOST) ** (-0.5),
        2.5 * D ** (-0.5),
        2.5 * FF ** (-0.5),
    )


def vector_rates(entries):
    column = entries % 8
    is_gain = (entries < 8 * D) & ((column == 0) | (column == 5))
    return jnp.where(is_gain, 0.3, 0.05).astype(jnp.float32)


def shifted(x, by):
    length = lax.axis_size("dev")
    return lax.ppermute(x, "dev", [(i, i + by) for i in range(length) if 0 <= i + by < length])


def flipped(x, mask):
    return lax.ppermute(x, "dev", [(i, i ^ mask) for i in range(lax.axis_size("dev"))])


def tied(*arrays):
    return lax.optimization_barrier(arrays)


class Index:
    def __init__(self):
        self.count = lax.axis_size("dev")
        self.me = lax.axis_index("dev")
        self.top = self.count.bit_length() - 3
        self.core = self.me & 1
        self.odd = self.core == 1
        middle = tuple(range(1, self.top))
        self.orders = (middle, tuple(reversed(middle)))

    def relative(self, order):
        seen = [r << self.top for r in range(4)]
        for b in reversed(order):
            seen = seen + [s | 1 << b for s in seen]
        return [s >> 1 for s in seen]


def by_core(ix, own, other):
    return jnp.where(ix.odd, other, own), jnp.where(ix.odd, own, other)


def cut_sides(x):
    cut = x.shape[-1] // 256 * 128
    return (x[..., :cut], x[..., cut:])


def gather_top(ix, piece):
    return jnp.stack([piece] + [flipped(piece, r << ix.top) for r in (1, 2, 3)])


def gather_mid(ix, sides):
    done = []
    for x, order in zip(sides, ix.orders):
        for b in reversed(order[1:]):
            x = jnp.concatenate([x, flipped(x, 1 << b)], axis=0)
        done.append(x)
    return done


def gather_last(ix, sides):
    return [(x, flipped(x, 1 << order[0])) for x, order in zip(sides, ix.orders)]


def place_kernel(rows, count, moves, chip_ref, *refs):
    ins, outs = refs[:count], refs[count:]
    chip = chip_ref[0]
    for source, at, target, relative, column, width in moves:
        start = pl.multiple_of((chip ^ relative) * rows, rows)
        spot = (pl.ds(start, rows), pl.ds(column, width))
        if at[0] == 0:
            outs[target][spot] = ins[source][at[1]]
        else:
            outs[target][at[1]] = ins[source][spot]


def place(ix, rows, ins, moves, out_shape):
    return pl.pallas_call(
        lambda *refs: place_kernel(rows, len(ins), moves, *refs),
        in_specs=[pl.BlockSpec(memory_space=pltpu.SMEM)]
        + [pl.BlockSpec(memory_space=pltpu.VMEM)] * len(ins),
        out_specs=[pl.BlockSpec(memory_space=pltpu.VMEM)] * len(out_shape),
        out_shape=[jax.ShapeDtypeStruct(shape, LOW) for shape in out_shape],
        compiler_params=pltpu.CompilerParams(vmem_limit_bytes=VMEM_BYTES),
    )((ix.me >> 1).astype(jnp.int32).reshape(1), *ins)


def assemble(ix, sides):
    chips = ix.count // 2
    rows = sides[0][0].shape[1]
    widths = [side[0].shape[2] for side in sides]
    if rows % 16:
        whole = []
        for side, order in zip(sides, ix.orders):
            place_of = [0] * chips
            for spot, relative in enumerate(ix.relative(order)):
                place_of[relative] = spot
            pick = jnp.array(place_of, jnp.int32)[(ix.me >> 1) ^ jnp.arange(chips)]
            full = jnp.take(jnp.concatenate(side, axis=0), pick, axis=0)
            whole.append(full.reshape(chips * rows, -1))
        return jnp.concatenate(whole, axis=1)
    moves = []
    for s, order in enumerate(ix.orders):
        for spot, relative in enumerate(ix.relative(order)):
            half, at = divmod(spot, chips // 2)
            moves.append((2 * s + half, (0, at), 0, relative, s * widths[0], widths[s]))
    ins = [array for side in sides for array in side]
    return place(ix, rows, ins, moves, [(chips * rows, sum(widths))])[0]


def take_apart(ix, whole):
    chips = ix.count // 2
    rows = whole.shape[0] // chips
    if rows % 16:
        sides = []
        for side, order in zip(cut_sides(whole), ix.orders):
            pick = (ix.me >> 1) ^ jnp.array(ix.relative(order), jnp.int32)
            full = jnp.take(side.reshape(chips, rows, -1), pick, axis=0)
            sides.append((full[: chips // 2], full[chips // 2 :]))
        return sides
    widths = [side.shape[1] for side in cut_sides(whole)]
    moves, shapes = [], []
    for s, order in enumerate(ix.orders):
        shapes += [(chips // 2, rows, widths[s])] * 2
        for spot, relative in enumerate(ix.relative(order)):
            half, at = divmod(spot, chips // 2)
            moves.append((0, (1, at), 2 * s + half, relative, s * widths[0], widths[s]))
    outs = place(ix, rows, [whole], moves, shapes)
    return [(outs[0], outs[1]), (outs[2], outs[3])]


def settle(keep, other, parts):
    size = keep.shape[0] // parts
    return [
        (
            keep[i * size : (i + 1) * size].astype(FULL)
            + other[i * size : (i + 1) * size].astype(FULL)
        ).astype(LOW)
        for i in range(parts)
    ]


def scatter_mid(ix, sides, first, last):
    done = []
    for (keep, send), order in zip(sides, ix.orders):
        for i in range(first, min(last, len(order))):
            parts = 2 if i < len(order) - 1 else 4
            settled = settle(keep, flipped(send, 1 << order[i]), parts)
            keep, send = settled[0], settled[1] if parts == 2 else settled[1:]
        done.append((keep, send))
    return done


def scatter_top(ix, sides):
    total = jnp.concatenate([keep[0] for keep, _ in sides], axis=-1).astype(FULL)
    for r in (1, 2, 3):
        part = jnp.concatenate([send[r - 1][0] for _, send in sides], axis=-1)
        total = total + flipped(part, r << ix.top).astype(FULL)
    return total


def own_rows(ix, summed):
    rows = summed.shape[0] // 2
    keep = lax.dynamic_slice_in_dim(summed, ix.core * rows, rows, 0)
    other = lax.dynamic_slice_in_dim(summed, (1 - ix.core) * rows, rows, 0)
    return keep, flipped(other, 1)


PAIR = 2 * HEAD_DIM
PAIRS = HEADS // 2
SIDE = PAIRS // 2
SCALE = HEAD_DIM ** (-0.5)
VMEM_BYTES = 48 * 1024 * 1024


def by_head(pair):
    low_half = lax.broadcasted_iota(jnp.int32, pair.shape, 1) < HEAD_DIM
    zero = jnp.zeros_like(pair)
    return (
        low_half,
        jnp.where(low_half, pair, zero).astype(LOW),
        jnp.where(low_half, zero, pair).astype(LOW),
    )


def dot_over(operand_a, operand_b, dim_a, dim_b):
    return lax.dot_general(
        operand_a, operand_b, (((dim_a,), (dim_b,)), ((), ())), preferred_element_type=FULL
    )


def attend_kernel(first_ref, q_ref, kv_ref, out_ref, weights_ref):
    rows, near = weights_ref.shape[-2:]
    key = lax.broadcasted_iota(jnp.int32, (rows, near), 1)
    last = lax.broadcasted_iota(jnp.int32, (rows, near), 0) + (near - rows)
    for block in range(2):
        own, seen = pl.ds(block * rows, rows), pl.ds(block * rows, near)
        low_half, *q_heads = by_head(q_ref[own, :].astype(FULL) * SCALE)
        k, v = kv_ref[seen, :PAIR], kv_ref[seen, PAIR:]
        allowed = (key >= first_ref[own, :] - block * rows) & (key <= last)
        blended = []
        for head in range(2):
            scores = jnp.where(allowed, dot_over(q_heads[head], k, 1, 1), NEG_LARGE)
            weights = jnp.exp(scores - jnp.max(scores, axis=-1, keepdims=True))
            weights = weights * (1.0 / jnp.sum(weights, axis=-1, keepdims=True))
            weights = weights.astype(LOW)
            weights_ref[0, 2 * block + head] = weights
            blended.append(dot_over(weights, v, 1, 0))
        out_ref[own, :] = jnp.where(low_half, blended[0], blended[1]).astype(LOW)


def attend(first_key, query, kv, rows, first, pairs):
    near = kv.shape[0] - rows
    return pl.pallas_call(
        attend_kernel,
        grid=(pairs,),
        in_specs=[
            pl.BlockSpec((2 * rows, 1), lambda i: (0, 0)),
            pl.BlockSpec((2 * rows, PAIR), lambda i: (0, i + first)),
            pl.BlockSpec((near + rows, 2 * PAIR), lambda i: (0, i + first)),
        ],
        out_specs=[
            pl.BlockSpec((2 * rows, PAIR), lambda i: (0, i)),
            pl.BlockSpec((1, 4, rows, near), lambda i: (i, 0, 0, 0)),
        ],
        out_shape=[
            jax.ShapeDtypeStruct((2 * rows, pairs * PAIR), LOW),
            jax.ShapeDtypeStruct((pairs, 4, rows, near), LOW),
        ],
        compiler_params=pltpu.CompilerParams(vmem_limit_bytes=VMEM_BYTES),
    )(first_key, query, kv)


def attend_back_kernel(weights_ref, grad_ref, q_ref, kv_ref, dq_ref, dkv_ref):
    rows, near = weights_ref.shape[-2:]
    turned = []
    for block in range(2):
        own, seen = pl.ds(block * rows, rows), pl.ds(block * rows, near)
        low_half, *grad_heads = by_head(grad_ref[own, :].astype(FULL))
        _, *q_heads = by_head(q_ref[own, :].astype(FULL))
        k, v = kv_ref[seen, :PAIR], kv_ref[seen, PAIR:]
        dq = []
        dk_turned = dv_turned = 0.0
        for head in range(2):
            weights_low = weights_ref[0, 2 * block + head]
            weights = weights_low.astype(FULL)
            grad_weights = dot_over(grad_heads[head], v, 1, 1)
            inner_sum = jnp.sum(weights * grad_weights, axis=-1, keepdims=True)
            grad_scores = (weights * (grad_weights - inner_sum)).astype(LOW)
            dq.append(dot_over(grad_scores, k, 1, 0))
            dk_turned += dot_over(q_heads[head], grad_scores, 0, 0)
            dv_turned += dot_over(grad_heads[head], weights_low, 0, 0)
        dq_ref[own, :] = (jnp.where(low_half, dq[0], dq[1]) * SCALE).astype(LOW)
        turned.append((dk_turned * SCALE, dv_turned))
    for which in range(2):
        early, late = turned[0][which], turned[1][which]
        whole = jnp.concatenate(
            [early[:, :rows], early[:, rows:] + late[:, : near - rows], late[:, near - rows :]],
            axis=1,
        )
        dkv_ref[:, which * PAIR : (which + 1) * PAIR] = whole.T.astype(LOW)


def attend_back(weights, grad, query, kv, rows, first, pairs):
    near = kv.shape[0] - rows
    return pl.pallas_call(
        attend_back_kernel,
        grid=(pairs,),
        in_specs=[
            pl.BlockSpec((1, 4, rows, near), lambda i: (i, 0, 0, 0)),
            pl.BlockSpec((2 * rows, PAIR), lambda i: (0, i + first)),
            pl.BlockSpec((2 * rows, PAIR), lambda i: (0, i + first)),
            pl.BlockSpec((near + rows, 2 * PAIR), lambda i: (0, i + first)),
        ],
        out_specs=[
            pl.BlockSpec((2 * rows, PAIR), lambda i: (0, i)),
            pl.BlockSpec((near + rows, 2 * PAIR), lambda i: (0, i)),
        ],
        out_shape=[
            jax.ShapeDtypeStruct((2 * rows, pairs * PAIR), LOW),
            jax.ShapeDtypeStruct((near + rows, 2 * pairs * PAIR), LOW),
        ],
        compiler_params=pltpu.CompilerParams(vmem_limit_bytes=VMEM_BYTES),
    )(weights, grad, query, kv)


def paired_columns(x):
    rows = x.shape[0]
    query = x[:, :D].reshape(rows, 2, SIDE * PAIR)
    kv = x[:, D:].reshape(rows, 2, 2, SIDE, PAIR).transpose(0, 2, 3, 1, 4)
    kv = kv.reshape(rows, 2, 2 * SIDE * PAIR)
    return [jnp.concatenate([query[:, s], kv[:, s]], axis=1) for s in range(2)]


def plain_columns(sides):
    rows, wide = sides[0].shape[0], SIDE * PAIR
    query = [side[:, :wide] for side in sides]
    kv = [side[:, wide:].reshape(rows, SIDE, 2, PAIR).transpose(0, 2, 1, 3) for side in sides]
    key_value = [kv[s][:, which].reshape(rows, wide) for which in range(2) for s in range(2)]
    return jnp.concatenate(query + key_value, axis=1)


def hidden_columns(x, share):
    parts = x.reshape(x.shape[0], FF // (2 * share), 2, share)
    return [parts[:, :, s].reshape(x.shape[0], FF // 2) for s in range(2)]


def plain_hidden(sides, share):
    rows = sides[0].shape[0]
    parts = [side.reshape(rows, FF // (2 * share), 1, share) for side in sides]
    return jnp.concatenate(parts, axis=2).reshape(rows, FF)


def dot(operand_a, operand_b):
    return jnp.dot(operand_a, operand_b, preferred_element_type=FULL)


def outer_sum(operand_a, operand_b):
    return jnp.einsum("ti,tj->ij", operand_a, operand_b, preferred_element_type=FULL).astype(LOW)


def dot_turned(operand_a, operand_b):
    return jnp.einsum("ti,ji->tj", operand_a, operand_b, preferred_element_type=FULL)


def body(
    tokens,
    cotangent,
    starts,
    w_qkv,
    m_qkv,
    v_qkv,
    w_out,
    m_out,
    v_out,
    w_up,
    m_up,
    v_up,
    w_down,
    m_down,
    v_down,
    vectors,
    m_vec,
    v_vec,
):
    ix = Index()
    rows = D // ix.count
    share = FF // ix.count
    tok_rows = tokens.shape[0]
    reach_count = (SEQ_MOST + tok_rows - 2) // tok_rows
    assert reach_count == 4
    chip_rows = 2 * tok_rows
    near_rows = (reach_count + 2) * tok_rows
    wide = SIDE * PAIR
    columns = 3 * wide
    out_wide, up_wide = D // 2, FF // 2

    vec_piece = jnp.pad(vectors.astype(LOW).reshape(rows, VCOLS), ((0, 0), (0, 128 - VCOLS)))
    qkv_sides = paired_columns(w_qkv.astype(LOW).reshape(rows, 3 * D))
    up_sides = hidden_columns(w_up.astype(LOW).reshape(rows, FF), share)
    out_low = w_out.astype(LOW).reshape(rows, D)
    pieces = [
        jnp.concatenate(
            [qkv_sides[s], vec_piece, out_low[:, s * out_wide : (s + 1) * out_wide], up_sides[s]],
            axis=1,
        )
        for s in range(2)
    ]
    mine, others = by_core(ix, *pieces)
    both = jnp.concatenate(by_core(ix, mine, flipped(others, 1)), axis=0)
    both, tokens, starts, cotangent = tied(both, tokens, starts, cotangent)
    first, second = both[:, : columns + 128], both[:, columns + 128 :]
    first = gather_top(ix, first)

    mine = jnp.stack([shifted(tokens, 4), shifted(tokens, 2), tokens])

    first, second, mine = tied(first, second, mine)
    second = gather_top(ix, second)
    first = gather_last(ix, gather_mid(ix, cut_sides(first)))
    near_tokens = jnp.stack(by_core(ix, mine, flipped(mine, 1)), axis=1).reshape(near_rows, D)
    chip_starts = jnp.concatenate(by_core(ix, starts, flipped(starts, 1)))
    third = w_down.astype(LOW).reshape(4 * rows, D)
    first, second, third, near_tokens, chip_starts, cotangent = tied(
        first, second, third, near_tokens, chip_starts, cotangent
    )
    chip_cotangent = jnp.concatenate(by_core(ix, cotangent, flipped(cotangent, 1)), axis=0)
    third = gather_top(ix, third)
    second = gather_mid(ix, cut_sides(second))
    first = assemble(ix, first)
    qkv_w = first[:, :columns]
    vec_all = first[:, columns : columns + VCOLS].reshape(-1).astype(FULL)
    vec_table, up_bias = vec_all[: 8 * D].reshape(D, 8).T, vec_all[8 * D :]
    gain_one, shift_one, bias_q, bias_v, bias_o, gain_two, shift_two, bias_down = (
        vec_table[i] for i in range(8)
    )
    up_bias = lax.dynamic_index_in_dim(
        up_bias.reshape(ix.count // 2, 2, share), ix.core, 1, keepdims=False
    ).reshape(up_wide)
    bias_q = lax.dynamic_slice_in_dim(bias_q, ix.core * wide, wide)
    bias_v = lax.dynamic_slice_in_dim(bias_v, ix.core * wide, wide)

    near_unit, near_inverse = norm_parts(near_tokens.astype(FULL))
    near_normed = (near_unit * gain_one + shift_one).astype(LOW)
    normed = near_normed[near_rows - chip_rows :]
    kv_bias = jnp.stack(
        [jnp.zeros((SIDE, PAIR), FULL), bias_v.reshape(SIDE, PAIR)], axis=1
    ).reshape(2 * wide)
    first_key = (chip_starts - ((ix.me >> 1) * chip_rows - reach_count * tok_rows))[:, None]
    query = (dot(normed, qkv_w[:, :wide]) + bias_q).astype(LOW)
    kv = (dot(near_normed, qkv_w[:, wide:]) + kv_bias).astype(LOW)
    query, kv, second = tied(query, kv, second)
    second = gather_last(ix, second)
    splits = ((0, 1), (1, SIDE - 1))
    mixed, weights = [None, None], [None, None]
    mixed[0], weights[0] = attend(first_key, query, kv, tok_rows, *splits[0])
    mixed[0], query, third = tied(mixed[0], query, third)
    third = gather_mid(ix, cut_sides(third))
    mixed[1], weights[1] = attend(first_key, query, kv, tok_rows, *splits[1])
    mixed = jnp.concatenate(mixed, axis=1)
    mixed, second, third = tied(mixed, second, third)
    third = gather_last(ix, third)
    attended = jnp.concatenate(by_core(ix, mixed, flipped(mixed, 1)), axis=1)
    second = assemble(ix, second)
    out_half, up_w = second[:, :out_wide], second[:, out_wide:]
    out_w = jnp.concatenate(by_core(ix, out_half, flipped(out_half, 1)), axis=1)

    inputs = near_tokens[near_rows - chip_rows :].astype(FULL)
    middle = inputs + (dot(attended, out_w) + bias_o)
    unit_two, inverse_two = norm_parts(middle)
    normed_two = (unit_two * gain_two + shift_two).astype(LOW)
    hidden_pre = dot(normed_two, up_w) + up_bias
    hidden_low = smooth_act(hidden_pre).astype(LOW)
    grad_downw = outer_sum(hidden_low, chip_cotangent)
    hidden_low, hidden_pre, grad_downw = tied(hidden_low, hidden_pre, grad_downw)
    sum_down = scatter_mid(ix, take_apart(ix, grad_downw), 0, 1)
    down_w = assemble(ix, third)
    result = dot(hidden_low, down_w).reshape(2, tok_rows, D)
    own_result, other_result = by_core(ix, result[0], result[1])
    own_result = own_result + flipped(other_result.astype(LOW), 1).astype(FULL)
    own_middle = lax.dynamic_slice_in_dim(middle, ix.core * tok_rows, tok_rows, 0)
    out_tokens = (own_middle + (own_result + bias_down)).astype(LOW)

    grad_hidden = dot_turned(chip_cotangent, down_w)
    act_value, act_back = jax.vjp(smooth_act, hidden_pre)
    grad_pre = act_back(grad_hidden)[0].astype(LOW)
    partial_two = dot_turned(grad_pre, up_w)
    grad_gain_two = jnp.sum(partial_two * unit_two, axis=0)
    grad_shift_two = jnp.sum(partial_two, axis=0)
    grad_normed_two = partial_two + flipped(partial_two.astype(LOW), 1).astype(FULL)
    grad_upw = outer_sum(normed_two, grad_pre)
    grad_middle = chip_cotangent.astype(FULL) + norm_back(
        grad_normed_two, unit_two, inverse_two, gain_two
    )
    grad_branch = grad_middle.astype(LOW)
    own_part = lax.dynamic_slice_in_dim(grad_branch, ix.core * out_wide, out_wide, 1)
    grad_second = jnp.concatenate([outer_sum(attended, own_part), grad_upw], axis=1)
    own_out = lax.dynamic_slice_in_dim(out_w, ix.core * wide, wide, 0)
    grad_mixed = dot_turned(grad_branch, own_out).astype(LOW)
    grad_mixed, grad_second, sum_down = tied(grad_mixed, grad_second, sum_down)
    sum_second = scatter_mid(ix, take_apart(ix, grad_second), 0, 1)
    sum_down = scatter_mid(ix, sum_down, 1, 9)
    dq, dkv = [None, None], [None, None]
    dq[0], dkv[0] = attend_back(weights[0], grad_mixed, query, kv, tok_rows, *splits[0])
    dq[0], dkv[0], grad_mixed, sum_down = tied(dq[0], dkv[0], grad_mixed, sum_down)
    sum_down = scatter_top(ix, sum_down)
    dq[1], dkv[1] = attend_back(weights[1], grad_mixed, query, kv, tok_rows, *splits[1])
    dq, dkv = jnp.concatenate(dq, axis=1), jnp.concatenate(dkv, axis=1)
    dq, dkv, sum_second = tied(dq, dkv, sum_second)
    sum_second = scatter_mid(ix, sum_second, 1, 9)

    grad_near = dot_turned(dkv, qkv_w[:, wide:]) + jnp.pad(
        dot_turned(dq, qkv_w[:, :wide]), ((near_rows - chip_rows, 0), (0, 0))
    )
    grad_gain_one = jnp.sum(grad_near * near_unit, axis=0)
    grad_shift_one = jnp.sum(grad_near, axis=0)
    own_half = (jnp.arange(2) == ix.core).astype(FULL)[:, None]
    grad_bias_v = jnp.sum(dkv.astype(FULL), axis=0).reshape(SIDE, 2, PAIR)[:, 1].reshape(1, wide)
    vec_rows = jnp.stack(
        [
            grad_gain_one,
            grad_shift_one,
            (jnp.sum(dq.astype(FULL), axis=0)[None] * own_half).reshape(D),
            (grad_bias_v * own_half).reshape(D),
            0.5 * jnp.sum(grad_branch.astype(FULL), axis=0),
            grad_gain_two,
            grad_shift_two,
            jnp.sum(cotangent.astype(FULL), axis=0),
        ],
        axis=0,
    )
    grad_bias_up = jnp.sum(grad_pre.astype(FULL), axis=0).reshape(ix.count // 2, 1, share)
    grad_vec = jnp.concatenate([vec_rows.T.reshape(-1), (grad_bias_up * own_half).reshape(-1)])
    grad_vec = lax.optimization_barrier(grad_vec).astype(LOW).reshape(D, VCOLS)
    grad_vec = jnp.pad(grad_vec, ((0, 0), (0, 128 - VCOLS)))
    grad_first = jnp.concatenate(
        [outer_sum(normed, dq), outer_sum(near_normed, dkv), grad_vec], axis=1
    )
    sum_first = scatter_mid(ix, take_apart(ix, grad_first), 0, 1)

    blocks = grad_near.reshape(reach_count // 2 + 1, 2, tok_rows, D)
    own_blocks, other_blocks = by_core(ix, blocks[:, 0], blocks[:, 1])
    own_blocks = own_blocks + flipped(other_blocks.astype(LOW), 1).astype(FULL)
    four_back, two_back = own_blocks[0].astype(LOW), own_blocks[1].astype(LOW)
    sum_first, own_blocks, two_back, four_back, sum_second = tied(
        sum_first, own_blocks, two_back, four_back, sum_second
    )
    sum_first = scatter_mid(ix, sum_first, 1, 9)
    sum_second = scatter_top(ix, sum_second)
    own = (
        own_blocks[2]
        + shifted(two_back, -2).astype(FULL)
        + shifted(four_back, -4).astype(FULL)
    )
    unit_one, inverse_one = norm_parts(tokens.astype(FULL))
    own_grad_middle = lax.dynamic_slice_in_dim(grad_middle, ix.core * tok_rows, tok_rows, 0)
    input_grad = own_grad_middle + norm_back(own, unit_one, inverse_one, gain_one)

    sum_first, own = tied(sum_first, own)
    sum_first = scatter_top(ix, sum_first)
    keep_second, other_second = own_rows(ix, sum_second)
    keep_first, other_first = own_rows(ix, sum_first)
    g_vec = (keep_first[:, columns:] + other_first[:, columns:])[:, :VCOLS].reshape(-1)
    g_qkv = plain_columns(by_core(ix, keep_first[:, :columns], other_first[:, :columns]))
    g_out = jnp.concatenate(
        by_core(ix, keep_second[:, :out_wide], other_second[:, :out_wide]), axis=1
    )
    g_up = plain_hidden(by_core(ix, keep_second[:, out_wide:], other_second[:, out_wide:]), share)

    rate_qkv, rate_out, rate_up, rate_down = matrix_rates()
    entries = ix.me * vectors.shape[0] + jnp.arange(vectors.shape[0], dtype=jnp.int32)
    qkv_new = adamw(w_qkv, m_qkv, v_qkv, g_qkv.reshape(-1), rate_qkv, DECAY_RATE)
    out_new = adamw(w_out, m_out, v_out, g_out.reshape(-1), rate_out, DECAY_RATE)
    up_new = adamw(w_up, m_up, v_up, g_up.reshape(-1), rate_up, DECAY_RATE)
    down_new = adamw(w_down, m_down, v_down, sum_down.reshape(-1), rate_down, DECAY_RATE)
    vec_new = adamw(vectors, m_vec, v_vec, g_vec, vector_rates(entries), 0.0)
    return (out_tokens, input_grad) + qkv_new + out_new + up_new + down_new + vec_new


def solution(mesh):
    in_specs = (P("dev", None), P("dev", None)) + (P("dev"),) * 16
    out_specs = (P("dev", None), P("dev", None)) + (P("dev"),) * 15
    return jax.shard_map(body, mesh=mesh, in_specs=in_specs, out_specs=out_specs, check_vma=False)
```

```python
import jax
import jax.numpy as jnp
from jax import lax
from jax.experimental import pallas as pl
from jax.experimental.pallas import tpu as pltpu
from jax.sharding import PartitionSpec as P

D = 768
HEAD_DIM = 64
HEADS = D // HEAD_DIM
FF = 3072
SEQ_MOST = 1024
STEP = 10
VCOLS = 12


NORM_EPS = 1e-05
BETA_ONE = 0.9
BETA_TWO = 0.999
ADAM_EPS = 1e-08
DECAY_RATE = 0.01
NEG_LARGE = -1e30

LOW = jnp.bfloat16
FULL = jnp.float32


def norm_parts(values):
    centre = jnp.mean(values, axis=-1, keepdims=True)
    centred = values - centre
    spread = jnp.mean(centred * centred, axis=-1, keepdims=True)
    inverse = lax.rsqrt(spread + NORM_EPS)
    return centred * inverse, inverse


def norm_back(grad, unit, inverse, gain_vec):
    scaled = grad * gain_vec
    along = jnp.mean(scaled * unit, axis=-1, keepdims=True)
    return inverse * (scaled - jnp.mean(scaled, axis=-1, keepdims=True) - unit * along)


def smooth_act(values):
    return jax.nn.gelu(values, approximate=True)


def adamw(weight, moment, second, gradient, step_rate, decay_rate):
    moment = BETA_ONE * moment + (1.0 - BETA_ONE) * gradient
    second = BETA_TWO * second + (1.0 - BETA_TWO) * gradient * gradient
    first_hat = moment / (1.0 - BETA_ONE**STEP)
    second_hat = second / (1.0 - BETA_TWO**STEP)
    weight = weight - step_rate * (
        first_hat / (jnp.sqrt(second_hat) + ADAM_EPS) + decay_rate * weight
    )
    return (moment, second, weight)


def matrix_rates():
    return (
        2.5 * D ** (-0.5),
        2.5 * max(1, D * 16 // SEQ_MOST) ** (-0.5),
        2.5 * D ** (-0.5),
        2.5 * FF ** (-0.5),
    )


def vector_rates(entries):
    column = entries % 8
    is_gain = (entries < 8 * D) & ((column == 0) | (column == 5))
    return jnp.where(is_gain, 0.3, 0.05).astype(jnp.float32)


def shifted(x, by):
    length = lax.axis_size("dev")
    return lax.ppermute(x, "dev", [(i, i + by) for i in range(length) if 0 <= i + by < length])


def flipped(x, mask):
    return lax.ppermute(x, "dev", [(i, i ^ mask) for i in range(lax.axis_size("dev"))])


def tied(*arrays):
    return lax.optimization_barrier(arrays)


class Index:
    def __init__(self):
        self.count = lax.axis_size("dev")
        self.me = lax.axis_index("dev")
        self.top = self.count.bit_length() - 3
        self.core = self.me & 1
        self.odd = self.core == 1
        middle = tuple(range(1, self.top))
        self.orders = (middle, tuple(reversed(middle)))

    def relative(self, order):
        seen = [r << self.top for r in range(4)]
        for b in reversed(order):
            seen = seen + [s | 1 << b for s in seen]
        return [s >> 1 for s in seen]


def by_core(ix, own, other):
    return jnp.where(ix.odd, other, own), jnp.where(ix.odd, own, other)


def cut_at(x, column):
    return (x[..., :column], x[..., column:])


def gather_top(ix, piece):
    return jnp.stack([piece] + [flipped(piece, r << ix.top) for r in (1, 2, 3)])


def gather_mid(sides, orders):
    done = []
    for x, order in zip(sides, orders):
        for b in reversed(order[1:]):
            x = jnp.concatenate([x, flipped(x, 1 << b)], axis=0)
        done.append(x)
    return done


def gather_last(sides, orders):
    return [(x, flipped(x, 1 << order[0])) for x, order in zip(sides, orders)]


def place_kernel(rows, count, moves, inward, chip_ref, *refs):
    ins, outs = refs[:count], refs[count:]
    chip = chip_ref[0]
    for part, at, column, whole, relative, whole_column, width in moves:
        start = pl.multiple_of((chip ^ relative) * rows, rows)
        spot = (pl.ds(start, rows), pl.ds(whole_column, width))
        if inward:
            outs[whole][spot] = ins[part][at, :, column : column + width]
        else:
            outs[part][at, :, column : column + width] = ins[whole][spot]


def place(ix, rows, ins, moves, inward, out_shape):
    return pl.pallas_call(
        lambda *refs: place_kernel(rows, len(ins), moves, inward, *refs),
        in_specs=[pl.BlockSpec(memory_space=pltpu.SMEM)]
        + [pl.BlockSpec(memory_space=pltpu.VMEM)] * len(ins),
        out_specs=[pl.BlockSpec(memory_space=pltpu.VMEM)] * len(out_shape),
        out_shape=[jax.ShapeDtypeStruct(shape, LOW) for shape in out_shape],
        compiler_params=pltpu.CompilerParams(vmem_limit_bytes=VMEM_BYTES),
    )((ix.me >> 1).astype(jnp.int32).reshape(1), *ins)


def place_moves(ix, orders, spots):
    moves = []
    for s, order in enumerate(orders):
        for spot, relative in enumerate(ix.relative(order)):
            half, at = divmod(spot, ix.count // 4)
            for column, width, whole, whole_column in spots[s]:
                moves.append((2 * s + half, at, column, whole, relative, whole_column, width))
    return moves


def assemble(ix, sides, orders, spots, widths):
    chips = ix.count // 2
    rows = sides[0][0].shape[1]
    if rows % 16:
        parts = [{} for _ in widths]
        for side, order, spot in zip(sides, orders, spots):
            seen = ix.relative(order)
            place_of = jnp.array([seen.index(r) for r in range(chips)], jnp.int32)
            pick = place_of[(ix.me >> 1) ^ jnp.arange(chips)]
            full = jnp.take(jnp.concatenate(side, axis=0), pick, axis=0)
            full = full.reshape(chips * rows, -1)
            for column, width, whole, whole_column in spot:
                parts[whole][whole_column] = full[:, column : column + width]
        return [jnp.concatenate([p[c] for c in sorted(p)], axis=1) for p in parts]
    ins = [array for side in sides for array in side]
    shapes = [(chips * rows, width) for width in widths]
    return place(ix, rows, ins, place_moves(ix, orders, spots), True, shapes)


def take_apart(ix, wholes, orders, spots):
    chips = ix.count // 2
    rows = wholes[0].shape[0] // chips
    widths = [sum(spot[1] for spot in side) for side in spots]
    if rows % 16:
        sides = []
        for order, spot in zip(orders, spots):
            side = jnp.concatenate([wholes[w][:, c : c + n] for _, n, w, c in spot], axis=1)
            pick = (ix.me >> 1) ^ jnp.array(ix.relative(order), jnp.int32)
            full = jnp.take(side.reshape(chips, rows, -1), pick, axis=0)
            sides.append((full[: chips // 2], full[chips // 2 :]))
        return sides
    shapes = [(chips // 2, rows, width) for width in widths for _ in range(2)]
    outs = place(ix, rows, wholes, place_moves(ix, orders, spots), False, shapes)
    return [(outs[2 * s], outs[2 * s + 1]) for s in range(len(spots))]


def settle(keep, other, parts):
    size = keep.shape[0] // parts
    return [
        (
            keep[i * size : (i + 1) * size].astype(FULL)
            + other[i * size : (i + 1) * size].astype(FULL)
        ).astype(LOW)
        for i in range(parts)
    ]


def scatter_mid(sides, orders, first, last):
    done = []
    for (keep, send), order in zip(sides, orders):
        for i in range(first, min(last, len(order))):
            parts = 2 if i < len(order) - 1 else 4
            settled = settle(keep, flipped(send, 1 << order[i]), parts)
            keep, send = settled[0], settled[1] if parts == 2 else settled[1:]
        done.append((keep, send))
    return done


def scatter_top(ix, sides):
    total = jnp.concatenate([keep[0] for keep, _ in sides], axis=-1).astype(FULL)
    for r in (1, 2, 3):
        part = jnp.concatenate([send[r - 1][0] for _, send in sides], axis=-1)
        total = total + flipped(part, r << ix.top).astype(FULL)
    return total


def own_rows(ix, summed):
    rows = summed.shape[0] // 2
    keep = lax.dynamic_slice_in_dim(summed, ix.core * rows, rows, 0)
    other = lax.dynamic_slice_in_dim(summed, (1 - ix.core) * rows, rows, 0)
    return keep, flipped(other, 1)


PAIR = 2 * HEAD_DIM
PAIRS = HEADS // 2
SIDE = PAIRS // 2
SCALE = HEAD_DIM ** (-0.5)
VMEM_BYTES = 48 * 1024 * 1024


def by_head(pair):
    low_half = lax.broadcasted_iota(jnp.int32, pair.shape, 1) < HEAD_DIM
    zero = jnp.zeros_like(pair)
    return (
        low_half,
        jnp.where(low_half, pair, zero).astype(LOW),
        jnp.where(low_half, zero, pair).astype(LOW),
    )


def dot_over(operand_a, operand_b, dim_a, dim_b):
    return lax.dot_general(
        operand_a, operand_b, (((dim_a,), (dim_b,)), ((), ())), preferred_element_type=FULL
    )


def attend_kernel(first_ref, qkv_ref, out_ref, weights_ref):
    rows, near = weights_ref.shape[-2:]
    before = near - rows
    key = lax.broadcasted_iota(jnp.int32, (rows, near), 1)
    last = lax.broadcasted_iota(jnp.int32, (rows, near), 0) + (near - rows)
    for block in range(2):
        own, seen = pl.ds(block * rows, rows), pl.ds(block * rows, near)
        query = qkv_ref[pl.ds(before + block * rows, rows), :PAIR]
        low_half, *q_heads = by_head(query.astype(FULL) * SCALE)
        k, v = qkv_ref[seen, PAIR : 2 * PAIR], qkv_ref[seen, 2 * PAIR :]
        allowed = (key >= first_ref[own, :] - block * rows) & (key <= last)
        blended = []
        for head in range(2):
            scores = jnp.where(allowed, dot_over(q_heads[head], k, 1, 1), NEG_LARGE)
            weights = jnp.exp(scores - jnp.max(scores, axis=-1, keepdims=True))
            weights = weights * (1.0 / jnp.sum(weights, axis=-1, keepdims=True))
            weights = weights.astype(LOW)
            weights_ref[0, 2 * block + head] = weights
            blended.append(dot_over(weights, v, 1, 0))
        out_ref[own, :] = jnp.where(low_half, blended[0], blended[1]).astype(LOW)


def attend(first_key, qkv, rows, first, pairs):
    window = qkv.shape[0]
    near = window - rows
    return pl.pallas_call(
        attend_kernel,
        grid=(pairs,),
        in_specs=[
            pl.BlockSpec((2 * rows, 1), lambda i: (0, 0)),
            pl.BlockSpec((window, 3 * PAIR), lambda i: (0, i + first)),
        ],
        out_specs=[
            pl.BlockSpec((2 * rows, PAIR), lambda i: (0, i)),
            pl.BlockSpec((1, 4, rows, near), lambda i: (i, 0, 0, 0)),
        ],
        out_shape=[
            jax.ShapeDtypeStruct((2 * rows, pairs * PAIR), LOW),
            jax.ShapeDtypeStruct((pairs, 4, rows, near), LOW),
        ],
        compiler_params=pltpu.CompilerParams(vmem_limit_bytes=VMEM_BYTES),
    )(first_key, qkv)


def attend_back_kernel(weights_ref, grad_ref, qkv_ref, out_ref):
    rows, near = weights_ref.shape[-2:]
    before = near - rows
    out_ref[:before, :PAIR] = jnp.zeros((before, PAIR), LOW)
    turned = []
    for block in range(2):
        own, seen = pl.ds(block * rows, rows), pl.ds(block * rows, near)
        low_half, *grad_heads = by_head(grad_ref[own, :].astype(FULL))
        asking = pl.ds(before + block * rows, rows)
        _, *q_heads = by_head(qkv_ref[asking, :PAIR].astype(FULL))
        k, v = qkv_ref[seen, PAIR : 2 * PAIR], qkv_ref[seen, 2 * PAIR :]
        dq = []
        dk_turned = dv_turned = 0.0
        for head in range(2):
            weights_low = weights_ref[0, 2 * block + head]
            weights = weights_low.astype(FULL)
            grad_weights = dot_over(grad_heads[head], v, 1, 1)
            inner_sum = jnp.sum(weights * grad_weights, axis=-1, keepdims=True)
            grad_scores = (weights * (grad_weights - inner_sum)).astype(LOW)
            dq.append(dot_over(grad_scores, k, 1, 0))
            dk_turned += dot_over(q_heads[head], grad_scores, 0, 0)
            dv_turned += dot_over(grad_heads[head], weights_low, 0, 0)
        out_ref[asking, :PAIR] = (jnp.where(low_half, dq[0], dq[1]) * SCALE).astype(LOW)
        turned.append((dk_turned * SCALE, dv_turned))
    for which in range(2):
        early, late = turned[0][which], turned[1][which]
        whole = jnp.concatenate(
            [early[:, :rows], early[:, rows:] + late[:, : near - rows], late[:, near - rows :]],
            axis=1,
        )
        out_ref[:, (which + 1) * PAIR : (which + 2) * PAIR] = whole.T.astype(LOW)


def attend_back(weights, grad, qkv, rows, first, pairs):
    window = qkv.shape[0]
    near = window - rows
    return pl.pallas_call(
        attend_back_kernel,
        grid=(pairs,),
        in_specs=[
            pl.BlockSpec((1, 4, rows, near), lambda i: (i, 0, 0, 0)),
            pl.BlockSpec((2 * rows, PAIR), lambda i: (0, i + first)),
            pl.BlockSpec((window, 3 * PAIR), lambda i: (0, i)),
        ],
        out_specs=pl.BlockSpec((window, 3 * PAIR), lambda i: (0, i)),
        out_shape=jax.ShapeDtypeStruct((window, 3 * pairs * PAIR), LOW),
        compiler_params=pltpu.CompilerParams(vmem_limit_bytes=VMEM_BYTES),
    )(weights, grad, qkv)


def paired_columns(x):
    rows = x.shape[0]
    parts = x.reshape(rows, 3, 2, SIDE, PAIR).transpose(2, 0, 3, 1, 4)
    return parts.reshape(2, rows, 3 * SIDE * PAIR)


def plain_columns(sides):
    rows = sides[0].shape[0]
    parts = [side.reshape(rows, SIDE, 3, PAIR).transpose(0, 2, 1, 3) for side in sides]
    return jnp.stack(parts, axis=2).reshape(rows, 3 * D)


def hidden_columns(x, share):
    parts = x.reshape(x.shape[0], FF // (2 * share), 2, share)
    return [parts[:, :, s].reshape(x.shape[0], FF // 2) for s in range(2)]


def plain_hidden(sides, share):
    rows = sides[0].shape[0]
    parts = [side.reshape(rows, FF // (2 * share), 1, share) for side in sides]
    return jnp.concatenate(parts, axis=2).reshape(rows, FF)


def dot(operand_a, operand_b):
    return jnp.dot(operand_a, operand_b, preferred_element_type=FULL)


def outer_sum(operand_a, operand_b):
    return jnp.einsum("ti,tj->ij", operand_a, operand_b, preferred_element_type=FULL).astype(LOW)


def dot_turned(operand_a, operand_b):
    return jnp.einsum("ti,ji->tj", operand_a, operand_b, preferred_element_type=FULL)


def body(
    tokens,
    cotangent,
    starts,
    w_qkv,
    m_qkv,
    v_qkv,
    w_out,
    m_out,
    v_out,
    w_up,
    m_up,
    v_up,
    w_down,
    m_down,
    v_down,
    vectors,
    m_vec,
    v_vec,
):
    ix = Index()
    rows = D // ix.count
    share = FF // ix.count
    tok_rows = tokens.shape[0]
    reach_count = (SEQ_MOST + tok_rows - 2) // tok_rows
    assert reach_count == 4
    chip_rows = 2 * tok_rows
    near_rows = (reach_count + 2) * tok_rows
    wide = SIDE * PAIR
    columns = 3 * wide
    out_wide, up_wide = D // 2, FF // 2

    early = 3 * PAIR * (SIDE - 1)
    late = columns - early
    first_spots = [[(0, early, 0, 0)], [(0, late + 128, 0, 0)]]
    cut = (out_wide + up_wide) // 256 * 128
    second_spots = [
        [(0, out_wide, 0, 0), (out_wide, cut - out_wide, 1, 0)],
        [(0, out_wide + up_wide - cut, 1, cut - out_wide)],
    ]
    third_spots = [[(0, D // 2, 0, 0)], [(0, D // 2, 0, D // 2)]]
    orders = ix.orders
    vec_piece = jnp.pad(vectors.astype(LOW).reshape(rows, VCOLS), ((0, 0), (0, 128 - VCOLS)))
    qkv_mine, qkv_others = by_core(ix, *paired_columns(w_qkv.astype(LOW).reshape(rows, 3 * D)))
    mine = jnp.concatenate([qkv_mine, vec_piece], axis=1)
    others = jnp.concatenate([qkv_others, vec_piece], axis=1)
    first = jnp.concatenate(by_core(ix, mine, flipped(others, 1)), axis=0)
    first = gather_top(ix, first)
    first, tokens, w_out, w_up = tied(first, tokens, w_out, w_up)

    first = gather_mid((first[..., :early], first[..., early:]), orders)
    mine = jnp.stack([shifted(tokens, 4), shifted(tokens, 2), tokens])
    up_sides = hidden_columns(w_up.astype(LOW).reshape(rows, FF), share)
    out_low = w_out.astype(LOW).reshape(rows, D)
    pieces = [
        jnp.concatenate([out_low[:, s * out_wide : (s + 1) * out_wide], up_sides[s]], axis=1)
        for s in range(2)
    ]
    own_piece, others = by_core(ix, *pieces)
    second = jnp.concatenate(by_core(ix, own_piece, flipped(others, 1)), axis=0)
    *first, second, starts = tied(*first, second, starts)
    first = gather_last(first, orders)
    second = gather_top(ix, second)
    near_tokens = jnp.stack(by_core(ix, mine, flipped(mine, 1)), axis=1).reshape(near_rows, D)
    chip_starts = jnp.concatenate(by_core(ix, starts, flipped(starts, 1)))
    first, near_tokens, chip_starts, cotangent, w_down = tied(
        first, near_tokens, chip_starts, cotangent, w_down
    )
    early_w = assemble(ix, first[:1], orders[:1], first_spots[:1], [early])[0]
    late_w = assemble(ix, first[1:], orders[1:], first_spots[1:], [late + 128])[0]
    vec_all = late_w[:, late : late + VCOLS].reshape(-1).astype(FULL)
    late_w = late_w[:, :late]
    third = w_down.astype(LOW).reshape(4 * rows, D)
    vec_table, up_bias = vec_all[: 8 * D].reshape(D, 8).T, vec_all[8 * D :]
    gain_one, shift_one, bias_q, bias_v, bias_o, gain_two, shift_two, bias_down = (
        vec_table[i] for i in range(8)
    )
    up_bias = lax.dynamic_index_in_dim(
        up_bias.reshape(ix.count // 2, 2, share), ix.core, 1, keepdims=False
    ).reshape(up_wide)
    bias_q = lax.dynamic_slice_in_dim(bias_q, ix.core * wide, wide)
    bias_v = lax.dynamic_slice_in_dim(bias_v, ix.core * wide, wide)

    near_unit, near_inverse = norm_parts(near_tokens.astype(FULL))
    near_normed = (near_unit * gain_one + shift_one).astype(LOW)
    near_normed, second, third, cotangent = tied(near_normed, second, third, cotangent)
    third = gather_top(ix, third)
    second = gather_mid(cut_at(second, cut), orders)
    chip_cotangent = jnp.concatenate(by_core(ix, cotangent, flipped(cotangent, 1)), axis=0)
    bias = jnp.stack(
        [bias_q.reshape(SIDE, PAIR), jnp.zeros((SIDE, PAIR), FULL), bias_v.reshape(SIDE, PAIR)],
        axis=1,
    ).reshape(columns)
    first_key = (chip_starts - ((ix.me >> 1) * chip_rows - reach_count * tok_rows))[:, None]
    early_qkv = (dot(near_normed, early_w) + bias[:early]).astype(LOW)
    late_qkv = (dot(near_normed, late_w) + bias[early:]).astype(LOW)
    early_qkv, late_qkv, second = tied(early_qkv, late_qkv, second)
    second = gather_last(second, orders)
    mixed, weights = [None, None], [None, None]
    mixed[0], weights[0] = attend(first_key, late_qkv, tok_rows, 0, 1)
    mixed[0], early_qkv, third = tied(mixed[0], early_qkv, third)
    third = gather_mid(cut_at(third, D // 2), orders)
    mixed[1], weights[1] = attend(first_key, early_qkv, tok_rows, 0, SIDE - 1)
    mixed = jnp.concatenate([mixed[1], mixed[0]], axis=1)
    mixed, second = tied(mixed, second)
    attended = jnp.concatenate(by_core(ix, mixed, flipped(mixed, 1)), axis=1)
    out_half, up_w = assemble(ix, second, orders, second_spots, [out_wide, up_wide])
    out_w = jnp.concatenate(by_core(ix, out_half, flipped(out_half, 1)), axis=1)
    attended, out_w, third = tied(attended, out_w, third)
    third = gather_last(third, orders)

    inputs = near_tokens[near_rows - chip_rows :].astype(FULL)
    middle = inputs + (dot(attended, out_w) + bias_o)
    unit_two, inverse_two = norm_parts(middle)
    normed_two = (unit_two * gain_two + shift_two).astype(LOW)
    hidden_pre = dot(normed_two, up_w) + up_bias
    hidden_low = smooth_act(hidden_pre).astype(LOW)
    grad_downw = outer_sum(hidden_low, chip_cotangent)
    hidden_low, hidden_pre, grad_downw = tied(hidden_low, hidden_pre, grad_downw)
    sum_down = scatter_mid(take_apart(ix, [grad_downw], orders, third_spots), orders, 0, 1)
    down_w = assemble(ix, third, orders, third_spots, [D])[0]
    result = dot(hidden_low, down_w).reshape(2, tok_rows, D)
    own_result, other_result = by_core(ix, result[0], result[1])
    own_result = own_result + flipped(other_result.astype(LOW), 1).astype(FULL)
    own_middle = lax.dynamic_slice_in_dim(middle, ix.core * tok_rows, tok_rows, 0)
    out_tokens = (own_middle + (own_result + bias_down)).astype(LOW)

    grad_hidden = dot_turned(chip_cotangent, down_w)
    act_value, act_back = jax.vjp(smooth_act, hidden_pre)
    grad_pre = act_back(grad_hidden)[0].astype(LOW)
    partial_two = dot_turned(grad_pre, up_w)
    grad_gain_two = jnp.sum(partial_two * unit_two, axis=0)
    grad_shift_two = jnp.sum(partial_two, axis=0)
    grad_normed_two = partial_two + flipped(partial_two.astype(LOW), 1).astype(FULL)
    grad_normed_two, grad_pre, sum_down = tied(grad_normed_two, grad_pre, sum_down)
    sum_down = scatter_mid(sum_down, orders, 1, 9)
    grad_upw = outer_sum(normed_two, grad_pre)
    grad_middle = chip_cotangent.astype(FULL) + norm_back(
        grad_normed_two, unit_two, inverse_two, gain_two
    )
    grad_branch = grad_middle.astype(LOW)
    own_part = lax.dynamic_slice_in_dim(grad_branch, ix.core * out_wide, out_wide, 1)
    grad_outw = outer_sum(attended, own_part)
    own_out = lax.dynamic_slice_in_dim(out_w, ix.core * wide, wide, 0)
    grad_mixed = dot_turned(grad_branch, own_out).astype(LOW)
    grad_mixed, grad_outw, grad_upw = tied(grad_mixed, grad_outw, grad_upw)
    sum_second = take_apart(ix, [grad_outw, grad_upw], orders, second_spots)
    sum_second = scatter_mid(sum_second, orders, 0, 1)
    early_back = attend_back(weights[1], grad_mixed, early_qkv, tok_rows, 0, SIDE - 1)
    sum_early = take_apart(ix, [outer_sum(near_normed, early_back)], orders[:1], first_spots[:1])
    early_back, grad_mixed, sum_down, sum_early = tied(early_back, grad_mixed, sum_down, sum_early)
    sum_early = scatter_mid(sum_early, orders[:1], 0, 1)
    sum_down = scatter_top(ix, sum_down)
    late_back = attend_back(weights[0], grad_mixed, late_qkv, tok_rows, SIDE - 1, 1)
    late_back, sum_second = tied(late_back, sum_second)
    sum_second = scatter_mid(sum_second, orders, 1, 9)

    grad_near = dot_turned(early_back, early_w) + dot_turned(late_back, late_w)
    grad_gain_one = jnp.sum(grad_near * near_unit, axis=0)
    grad_shift_one = jnp.sum(grad_near, axis=0)
    own_half = (jnp.arange(2) == ix.core).astype(FULL)[:, None]
    grad_bias = jnp.concatenate(
        [jnp.sum(early_back.astype(FULL), axis=0), jnp.sum(late_back.astype(FULL), axis=0)]
    ).reshape(SIDE, 3, PAIR)
    grad_bias_q, grad_bias_v = (grad_bias[:, i].reshape(1, wide) for i in (0, 2))
    vec_rows = jnp.stack(
        [
            grad_gain_one,
            grad_shift_one,
            (grad_bias_q * own_half).reshape(D),
            (grad_bias_v * own_half).reshape(D),
            0.5 * jnp.sum(grad_branch.astype(FULL), axis=0),
            grad_gain_two,
            grad_shift_two,
            jnp.sum(cotangent.astype(FULL), axis=0),
        ],
        axis=0,
    )
    grad_bias_up = jnp.sum(grad_pre.astype(FULL), axis=0).reshape(ix.count // 2, 1, share)
    grad_vec = jnp.concatenate([vec_rows.T.reshape(-1), (grad_bias_up * own_half).reshape(-1)])
    grad_vec = lax.optimization_barrier(grad_vec).astype(LOW).reshape(D, VCOLS)
    grad_vec = jnp.pad(grad_vec, ((0, 0), (0, 128 - VCOLS)))
    grad_late = jnp.concatenate([outer_sum(near_normed, late_back), grad_vec], axis=1)
    sum_late = scatter_mid(
        take_apart(ix, [grad_late], orders[1:], first_spots[1:]), orders[1:], 0, 1
    )

    blocks = grad_near.reshape(reach_count // 2 + 1, 2, tok_rows, D)
    own_blocks, other_blocks = by_core(ix, blocks[:, 0], blocks[:, 1])
    own_blocks = own_blocks + flipped(other_blocks.astype(LOW), 1).astype(FULL)
    four_back, two_back = own_blocks[0].astype(LOW), own_blocks[1].astype(LOW)
    sum_early, sum_second = tied(sum_early, sum_second)
    sum_early = scatter_mid(sum_early, orders[:1], 1, 9)
    sum_second = scatter_top(ix, sum_second)
    sum_late, own_blocks, two_back, four_back = tied(sum_late, own_blocks, two_back, four_back)
    sum_late = scatter_mid(sum_late, orders[1:], 1, 9)
    sum_first = scatter_top(ix, sum_early + sum_late)
    own = (
        own_blocks[2]
        + shifted(two_back, -2).astype(FULL)
        + shifted(four_back, -4).astype(FULL)
    )
    unit_one, inverse_one = norm_parts(tokens.astype(FULL))
    own_grad_middle = lax.dynamic_slice_in_dim(grad_middle, ix.core * tok_rows, tok_rows, 0)
    input_grad = own_grad_middle + norm_back(own, unit_one, inverse_one, gain_one)

    keep_second, other_second = own_rows(ix, sum_second)
    keep_first, other_first = own_rows(ix, sum_first)
    g_vec = (keep_first[:, columns:] + other_first[:, columns:])[:, :VCOLS].reshape(-1)
    g_qkv = plain_columns(by_core(ix, keep_first[:, :columns], other_first[:, :columns]))
    g_out = jnp.concatenate(
        by_core(ix, keep_second[:, :out_wide], other_second[:, :out_wide]), axis=1
    )
    g_up = plain_hidden(by_core(ix, keep_second[:, out_wide:], other_second[:, out_wide:]), share)

    rate_qkv, rate_out, rate_up, rate_down = matrix_rates()
    entries = ix.me * vectors.shape[0] + jnp.arange(vectors.shape[0], dtype=jnp.int32)
    qkv_new = adamw(w_qkv, m_qkv, v_qkv, g_qkv.reshape(-1), rate_qkv, DECAY_RATE)
    out_new = adamw(w_out, m_out, v_out, g_out.reshape(-1), rate_out, DECAY_RATE)
    up_new = adamw(w_up, m_up, v_up, g_up.reshape(-1), rate_up, DECAY_RATE)
    down_new = adamw(w_down, m_down, v_down, sum_down.reshape(-1), rate_down, DECAY_RATE)
    vec_new = adamw(vectors, m_vec, v_vec, g_vec, vector_rates(entries), 0.0)
    return (out_tokens, input_grad) + qkv_new + out_new + up_new + down_new + vec_new


def solution(mesh):
    in_specs = (P("dev", None), P("dev", None)) + (P("dev"),) * 16
    out_specs = (P("dev", None), P("dev", None)) + (P("dev"),) * 15
    return jax.shard_map(body, mesh=mesh, in_specs=in_specs, out_specs=out_specs, check_vma=False)
```

```python
import jax
import jax.numpy as jnp
from jax import lax
from jax.experimental import pallas as pl
from jax.experimental.pallas import tpu as pltpu
from jax.sharding import PartitionSpec as P

D = 768
HEAD_DIM = 64
HEADS = D // HEAD_DIM
FF = 3072
SEQ_MOST = 1024
STEP = 10
VCOLS = 12


NORM_EPS = 1e-05
BETA_ONE = 0.9
BETA_TWO = 0.999
ADAM_EPS = 1e-08
DECAY_RATE = 0.01
NEG_LARGE = -1e30

LOW = jnp.bfloat16
FULL = jnp.float32


def norm_parts(values):
    centre = jnp.mean(values, axis=-1, keepdims=True)
    centred = values - centre
    spread = jnp.mean(centred * centred, axis=-1, keepdims=True)
    inverse = lax.rsqrt(spread + NORM_EPS)
    return centred * inverse, inverse


def norm_back(grad, unit, inverse, gain_vec):
    scaled = grad * gain_vec
    along = jnp.mean(scaled * unit, axis=-1, keepdims=True)
    return inverse * (scaled - jnp.mean(scaled, axis=-1, keepdims=True) - unit * along)


def smooth_act(values):
    return jax.nn.gelu(values, approximate=True)


def adamw(weight, moment, second, gradient, step_rate, decay_rate):
    moment = BETA_ONE * moment + (1.0 - BETA_ONE) * gradient
    second = BETA_TWO * second + (1.0 - BETA_TWO) * gradient * gradient
    first_hat = moment / (1.0 - BETA_ONE**STEP)
    second_hat = second / (1.0 - BETA_TWO**STEP)
    weight = weight - step_rate * (
        first_hat / (jnp.sqrt(second_hat) + ADAM_EPS) + decay_rate * weight
    )
    return (moment, second, weight)


def matrix_rates():
    return (
        2.5 * D ** (-0.5),
        2.5 * max(1, D * 16 // SEQ_MOST) ** (-0.5),
        2.5 * D ** (-0.5),
        2.5 * FF ** (-0.5),
    )


def vector_rates(entries):
    column = entries % 8
    is_gain = (entries < 8 * D) & ((column == 0) | (column == 5))
    return jnp.where(is_gain, 0.3, 0.05).astype(jnp.float32)


def shifted(x, by):
    length = lax.axis_size("dev")
    return lax.ppermute(x, "dev", [(i, i + by) for i in range(length) if 0 <= i + by < length])


def flipped(x, mask):
    return lax.ppermute(x, "dev", [(i, i ^ mask) for i in range(lax.axis_size("dev"))])


def tied(*arrays):
    return lax.optimization_barrier(arrays)


class Index:
    def __init__(self):
        self.count = lax.axis_size("dev")
        self.me = lax.axis_index("dev")
        self.top = self.count.bit_length() - 3
        self.core = self.me & 1
        self.odd = self.core == 1
        middle = tuple(range(1, self.top))
        self.orders = (middle, tuple(reversed(middle)))

    def relative(self, order):
        seen = [r << self.top for r in range(4)]
        for b in reversed(order):
            seen = seen + [s | 1 << b for s in seen]
        return [s >> 1 for s in seen]


def by_core(ix, own, other):
    return jnp.where(ix.odd, other, own), jnp.where(ix.odd, own, other)


def cut_at(x, column):
    return (x[..., :column], x[..., column:])


def gather_top(ix, piece):
    return jnp.stack([piece] + [flipped(piece, r << ix.top) for r in (1, 2, 3)])


def gather_mid(sides, orders):
    done = []
    for x, order in zip(sides, orders):
        for b in reversed(order[1:]):
            x = jnp.concatenate([x, flipped(x, 1 << b)], axis=0)
        done.append(x)
    return done


def gather_last(sides, orders):
    return [(x, flipped(x, 1 << order[0])) for x, order in zip(sides, orders)]


def place_kernel(rows, count, moves, inward, chip_ref, *refs):
    ins, outs = refs[:count], refs[count:]
    chip = chip_ref[0]
    for part, at, column, whole, relative, whole_column, width in moves:
        start = pl.multiple_of((chip ^ relative) * rows, rows)
        spot = (pl.ds(start, rows), pl.ds(whole_column, width))
        if inward:
            outs[whole][spot] = ins[part][at, :, column : column + width]
        else:
            outs[part][at, :, column : column + width] = ins[whole][spot]


def place(ix, rows, ins, moves, inward, out_shape):
    return pl.pallas_call(
        lambda *refs: place_kernel(rows, len(ins), moves, inward, *refs),
        in_specs=[pl.BlockSpec(memory_space=pltpu.SMEM)]
        + [pl.BlockSpec(memory_space=pltpu.VMEM)] * len(ins),
        out_specs=[pl.BlockSpec(memory_space=pltpu.VMEM)] * len(out_shape),
        out_shape=[jax.ShapeDtypeStruct(shape, LOW) for shape in out_shape],
        compiler_params=pltpu.CompilerParams(
            vmem_limit_bytes=4 * sum(rows * move[-1] for move in moves) + 2**21
        ),
    )((ix.me >> 1).astype(jnp.int32).reshape(1), *ins)


def place_moves(ix, orders, spots):
    moves = []
    for s, order in enumerate(orders):
        for spot, relative in enumerate(ix.relative(order)):
            half, at = divmod(spot, ix.count // 4)
            for column, width, whole, whole_column in spots[s]:
                moves.append((2 * s + half, at, column, whole, relative, whole_column, width))
    return moves


def assemble(ix, sides, orders, spots, widths):
    chips = ix.count // 2
    rows = sides[0][0].shape[1]
    if rows % 16:
        parts = [{} for _ in widths]
        for side, order, spot in zip(sides, orders, spots):
            seen = ix.relative(order)
            place_of = jnp.array([seen.index(r) for r in range(chips)], jnp.int32)
            pick = place_of[(ix.me >> 1) ^ jnp.arange(chips)]
            full = jnp.take(jnp.concatenate(side, axis=0), pick, axis=0)
            full = full.reshape(chips * rows, -1)
            for column, width, whole, whole_column in spot:
                parts[whole][whole_column] = full[:, column : column + width]
        return [jnp.concatenate([p[c] for c in sorted(p)], axis=1) for p in parts]
    ins = [array for side in sides for array in side]
    shapes = [(chips * rows, width) for width in widths]
    return place(ix, rows, ins, place_moves(ix, orders, spots), True, shapes)


def take_apart(ix, wholes, orders, spots):
    chips = ix.count // 2
    rows = wholes[0].shape[0] // chips
    widths = [sum(spot[1] for spot in side) for side in spots]
    if rows % 16:
        sides = []
        for order, spot in zip(orders, spots):
            side = jnp.concatenate([wholes[w][:, c : c + n] for _, n, w, c in spot], axis=1)
            pick = (ix.me >> 1) ^ jnp.array(ix.relative(order), jnp.int32)
            full = jnp.take(side.reshape(chips, rows, -1), pick, axis=0)
            sides.append((full[: chips // 2], full[chips // 2 :]))
        return sides
    shapes = [(chips // 2, rows, width) for width in widths for _ in range(2)]
    outs = place(ix, rows, wholes, place_moves(ix, orders, spots), False, shapes)
    return [(outs[2 * s], outs[2 * s + 1]) for s in range(len(spots))]


def settle(keep, other, parts):
    size = keep.shape[0] // parts
    return [
        (
            keep[i * size : (i + 1) * size].astype(FULL)
            + other[i * size : (i + 1) * size].astype(FULL)
        ).astype(LOW)
        for i in range(parts)
    ]


def scatter_mid(sides, orders, first, last):
    done = []
    for (keep, send), order in zip(sides, orders):
        for i in range(first, min(last, len(order))):
            parts = 2 if i < len(order) - 1 else 4
            settled = settle(keep, flipped(send, 1 << order[i]), parts)
            keep, send = settled[0], settled[1] if parts == 2 else settled[1:]
        done.append((keep, send))
    return done


def scatter_top(ix, sides):
    total = jnp.concatenate([keep[0] for keep, _ in sides], axis=-1).astype(FULL)
    for r in (1, 2, 3):
        part = jnp.concatenate([send[r - 1][0] for _, send in sides], axis=-1)
        total = total + flipped(part, r << ix.top).astype(FULL)
    return total


def own_rows(ix, summed):
    rows = summed.shape[0] // 2
    keep = lax.dynamic_slice_in_dim(summed, ix.core * rows, rows, 0)
    other = lax.dynamic_slice_in_dim(summed, (1 - ix.core) * rows, rows, 0)
    return keep, flipped(other, 1)


PAIR = 2 * HEAD_DIM
PAIRS = HEADS // 2
SIDE = PAIRS // 2
SCALE = HEAD_DIM ** (-0.5)
VMEM_BYTES = 20 * 1024 * 1024


def by_head(pair):
    low_half = lax.broadcasted_iota(jnp.int32, pair.shape, 1) < HEAD_DIM
    zero = jnp.zeros_like(pair)
    return (
        low_half,
        jnp.where(low_half, pair, zero).astype(LOW),
        jnp.where(low_half, zero, pair).astype(LOW),
    )


def dot_over(operand_a, operand_b, dim_a, dim_b):
    return lax.dot_general(
        operand_a, operand_b, (((dim_a,), (dim_b,)), ((), ())), preferred_element_type=FULL
    )


def attend_kernel(first_ref, qkv_ref, out_ref, weights_ref):
    rows, near = weights_ref.shape[-2:]
    before = near - rows
    key = lax.broadcasted_iota(jnp.int32, (rows, near), 1)
    last = lax.broadcasted_iota(jnp.int32, (rows, near), 0) + (near - rows)
    for block in range(2):
        own, seen = pl.ds(block * rows, rows), pl.ds(block * rows, near)
        query = qkv_ref[pl.ds(before + block * rows, rows), :PAIR]
        low_half, *q_heads = by_head(query.astype(FULL) * SCALE)
        k, v = qkv_ref[seen, PAIR : 2 * PAIR], qkv_ref[seen, 2 * PAIR :]
        allowed = (key >= first_ref[own, :] - block * rows) & (key <= last)
        blended = []
        for head in range(2):
            scores = jnp.where(allowed, dot_over(q_heads[head], k, 1, 1), NEG_LARGE)
            weights = jnp.exp(scores - jnp.max(scores, axis=-1, keepdims=True))
            weights = weights * (1.0 / jnp.sum(weights, axis=-1, keepdims=True))
            weights = weights.astype(LOW)
            weights_ref[0, 2 * block + head] = weights
            blended.append(dot_over(weights, v, 1, 0))
        out_ref[own, :] = jnp.where(low_half, blended[0], blended[1]).astype(LOW)


def attend(first_key, qkv, rows, first, pairs):
    window = qkv.shape[0]
    near = window - rows
    return pl.pallas_call(
        attend_kernel,
        grid=(pairs,),
        in_specs=[
            pl.BlockSpec((2 * rows, 1), lambda i: (0, 0)),
            pl.BlockSpec((window, 3 * PAIR), lambda i: (0, i + first)),
        ],
        out_specs=[
            pl.BlockSpec((2 * rows, PAIR), lambda i: (0, i)),
            pl.BlockSpec((1, 4, rows, near), lambda i: (i, 0, 0, 0)),
        ],
        out_shape=[
            jax.ShapeDtypeStruct((2 * rows, pairs * PAIR), LOW),
            jax.ShapeDtypeStruct((pairs, 4, rows, near), LOW),
        ],
        compiler_params=pltpu.CompilerParams(vmem_limit_bytes=VMEM_BYTES),
    )(first_key, qkv)


def attend_back_kernel(weights_ref, grad_ref, qkv_ref, out_ref):
    rows, near = weights_ref.shape[-2:]
    before = near - rows
    out_ref[:before, :PAIR] = jnp.zeros((before, PAIR), LOW)
    turned = []
    for block in range(2):
        own, seen = pl.ds(block * rows, rows), pl.ds(block * rows, near)
        low_half, *grad_heads = by_head(grad_ref[own, :].astype(FULL))
        asking = pl.ds(before + block * rows, rows)
        _, *q_heads = by_head(qkv_ref[asking, :PAIR].astype(FULL))
        k, v = qkv_ref[seen, PAIR : 2 * PAIR], qkv_ref[seen, 2 * PAIR :]
        dq = []
        dk_turned = dv_turned = 0.0
        for head in range(2):
            weights_low = weights_ref[0, 2 * block + head]
            weights = weights_low.astype(FULL)
            grad_weights = dot_over(grad_heads[head], v, 1, 1)
            inner_sum = jnp.sum(weights * grad_weights, axis=-1, keepdims=True)
            grad_scores = (weights * (grad_weights - inner_sum)).astype(LOW)
            dq.append(dot_over(grad_scores, k, 1, 0))
            dk_turned += dot_over(q_heads[head], grad_scores, 0, 0)
            dv_turned += dot_over(grad_heads[head], weights_low, 0, 0)
        out_ref[asking, :PAIR] = (jnp.where(low_half, dq[0], dq[1]) * SCALE).astype(LOW)
        turned.append((dk_turned * SCALE, dv_turned))
    for which in range(2):
        early, late = turned[0][which], turned[1][which]
        whole = jnp.concatenate(
            [early[:, :rows], early[:, rows:] + late[:, : near - rows], late[:, near - rows :]],
            axis=1,
        )
        out_ref[:, (which + 1) * PAIR : (which + 2) * PAIR] = whole.T.astype(LOW)


def attend_back(weights, grad, qkv, rows, first, pairs):
    window = qkv.shape[0]
    near = window - rows
    return pl.pallas_call(
        attend_back_kernel,
        grid=(pairs,),
        in_specs=[
            pl.BlockSpec((1, 4, rows, near), lambda i: (i, 0, 0, 0)),
            pl.BlockSpec((2 * rows, PAIR), lambda i: (0, i + first)),
            pl.BlockSpec((window, 3 * PAIR), lambda i: (0, i)),
        ],
        out_specs=pl.BlockSpec((window, 3 * PAIR), lambda i: (0, i)),
        out_shape=jax.ShapeDtypeStruct((window, 3 * pairs * PAIR), LOW),
        compiler_params=pltpu.CompilerParams(vmem_limit_bytes=VMEM_BYTES),
    )(weights, grad, qkv)


def paired_columns(x):
    rows = x.shape[0]
    parts = x.reshape(rows, 3, 2, SIDE, PAIR).transpose(2, 0, 3, 1, 4)
    return parts.reshape(2, rows, 3 * SIDE * PAIR)


def plain_columns(sides):
    rows = sides[0].shape[0]
    parts = [side.reshape(rows, SIDE, 3, PAIR).transpose(0, 2, 1, 3) for side in sides]
    return jnp.stack(parts, axis=2).reshape(rows, 3 * D)


def hidden_columns(x, share):
    parts = x.reshape(x.shape[0], FF // (2 * share), 2, share)
    return [parts[:, :, s].reshape(x.shape[0], FF // 2) for s in range(2)]


def plain_hidden(sides, share):
    rows = sides[0].shape[0]
    parts = [side.reshape(rows, FF // (2 * share), 1, share) for side in sides]
    return jnp.concatenate(parts, axis=2).reshape(rows, FF)


def dot(operand_a, operand_b):
    return jnp.dot(operand_a, operand_b, preferred_element_type=FULL)


def outer_sum(operand_a, operand_b):
    return jnp.einsum("ti,tj->ij", operand_a, operand_b, preferred_element_type=FULL).astype(LOW)


def dot_turned(operand_a, operand_b):
    return jnp.einsum("ti,ji->tj", operand_a, operand_b, preferred_element_type=FULL)


def body(
    tokens,
    cotangent,
    starts,
    w_qkv,
    m_qkv,
    v_qkv,
    w_out,
    m_out,
    v_out,
    w_up,
    m_up,
    v_up,
    w_down,
    m_down,
    v_down,
    vectors,
    m_vec,
    v_vec,
):
    ix = Index()
    rows = D // ix.count
    share = FF // ix.count
    tok_rows = tokens.shape[0]
    reach_count = (SEQ_MOST + tok_rows - 2) // tok_rows
    assert reach_count == 4
    chip_rows = 2 * tok_rows
    near_rows = (reach_count + 2) * tok_rows
    wide = SIDE * PAIR
    columns = 3 * wide
    out_wide, up_wide = D // 2, FF // 2

    early = 3 * PAIR * (SIDE - 1)
    late = columns - early
    first_spots = [[(0, early, 0, 0)], [(0, late + 128, 0, 0)]]
    cut = (out_wide + up_wide) // 256 * 128
    second_spots = [
        [(0, out_wide, 0, 0), (out_wide, cut - out_wide, 1, 0)],
        [(0, out_wide + up_wide - cut, 1, cut - out_wide)],
    ]
    third_spots = [[(0, D // 2, 0, 0)], [(0, D // 2, 0, D // 2)]]
    orders = ix.orders
    vec_piece = jnp.pad(vectors.astype(LOW).reshape(rows, VCOLS), ((0, 0), (0, 128 - VCOLS)))
    qkv_mine, qkv_others = by_core(ix, *paired_columns(w_qkv.astype(LOW).reshape(rows, 3 * D)))
    mine = jnp.concatenate([qkv_mine, vec_piece], axis=1)
    others = jnp.concatenate([qkv_others, vec_piece], axis=1)
    first = jnp.concatenate(by_core(ix, mine, flipped(others, 1)), axis=0)
    first = gather_top(ix, first)
    first, tokens, w_out, w_up = tied(first, tokens, w_out, w_up)

    first = gather_mid((first[..., :early], first[..., early:]), orders)
    mine = jnp.stack([shifted(tokens, 4), shifted(tokens, 2), tokens])
    up_sides = hidden_columns(w_up.astype(LOW).reshape(rows, FF), share)
    out_low = w_out.astype(LOW).reshape(rows, D)
    pieces = [
        jnp.concatenate([out_low[:, s * out_wide : (s + 1) * out_wide], up_sides[s]], axis=1)
        for s in range(2)
    ]
    own_piece, others = by_core(ix, *pieces)
    second = jnp.concatenate(by_core(ix, own_piece, flipped(others, 1)), axis=0)
    *first, second, starts, mine = tied(*first, second, starts, mine)
    first = gather_last(first, orders)
    second = gather_top(ix, second)
    near_tokens = jnp.stack(by_core(ix, mine, flipped(mine, 1)), axis=1).reshape(near_rows, D)
    chip_starts = jnp.concatenate(by_core(ix, starts, flipped(starts, 1)))
    first, near_tokens, chip_starts, cotangent, w_down = tied(
        first, near_tokens, chip_starts, cotangent, w_down
    )
    early_w = assemble(ix, first[:1], orders[:1], first_spots[:1], [early])[0]
    late_w = assemble(ix, first[1:], orders[1:], first_spots[1:], [late + 128])[0]
    vec_all = late_w[:, late : late + VCOLS].reshape(-1).astype(FULL)
    late_w = late_w[:, :late]
    third = w_down.astype(LOW).reshape(4 * rows, D)
    vec_table, up_bias = vec_all[: 8 * D].reshape(D, 8).T, vec_all[8 * D :]
    gain_one, shift_one, bias_q, bias_v, bias_o, gain_two, shift_two, bias_down = (
        vec_table[i] for i in range(8)
    )
    up_bias = lax.dynamic_index_in_dim(
        up_bias.reshape(ix.count // 2, 2, share), ix.core, 1, keepdims=False
    ).reshape(up_wide)
    bias_q = lax.dynamic_slice_in_dim(bias_q, ix.core * wide, wide)
    bias_v = lax.dynamic_slice_in_dim(bias_v, ix.core * wide, wide)

    near_unit, near_inverse = norm_parts(near_tokens.astype(FULL))
    near_normed = (near_unit * gain_one + shift_one).astype(LOW)
    chip_cotangent = jnp.concatenate(by_core(ix, cotangent, flipped(cotangent, 1)), axis=0)
    bias = jnp.stack(
        [bias_q.reshape(SIDE, PAIR), jnp.zeros((SIDE, PAIR), FULL), bias_v.reshape(SIDE, PAIR)],
        axis=1,
    ).reshape(columns)
    first_key = (chip_starts - ((ix.me >> 1) * chip_rows - reach_count * tok_rows))[:, None]
    early_qkv = (dot(near_normed, early_w) + bias[:early]).astype(LOW)
    late_qkv = (dot(near_normed, late_w) + bias[early:]).astype(LOW)
    early_qkv, late_qkv, second, third = tied(early_qkv, late_qkv, second, third)
    second = gather_mid(cut_at(second, cut), orders)
    third = gather_top(ix, third)
    mixed, weights = [None, None], [None, None]
    mixed[0], weights[0] = attend(first_key, late_qkv, tok_rows, 0, 1)
    mixed[0], early_qkv, second = tied(mixed[0], early_qkv, second)
    second = gather_last(second, orders)
    mixed[1], weights[1] = attend(first_key, early_qkv, tok_rows, 0, SIDE - 1)
    mixed = jnp.concatenate([mixed[1], mixed[0]], axis=1)
    mixed, second, third = tied(mixed, second, third)
    third = gather_mid(cut_at(third, D // 2), orders)
    attended = jnp.concatenate(by_core(ix, mixed, flipped(mixed, 1)), axis=1)
    out_half, up_w = assemble(ix, second, orders, second_spots, [out_wide, up_wide])
    out_w = jnp.concatenate(by_core(ix, out_half, flipped(out_half, 1)), axis=1)
    inputs = near_tokens[near_rows - chip_rows :].astype(FULL)
    middle = inputs + (dot(attended, out_w) + bias_o)
    middle, third = tied(middle, third)
    third = gather_last(third, orders)
    unit_two, inverse_two = norm_parts(middle)
    normed_two = (unit_two * gain_two + shift_two).astype(LOW)
    hidden_pre = dot(normed_two, up_w) + up_bias
    hidden_low = smooth_act(hidden_pre).astype(LOW)
    grad_downw = outer_sum(hidden_low, chip_cotangent)
    hidden_low, hidden_pre, grad_downw = tied(hidden_low, hidden_pre, grad_downw)
    sum_down = scatter_mid(take_apart(ix, [grad_downw], orders, third_spots), orders, 0, 1)
    down_w = assemble(ix, third, orders, third_spots, [D])[0]
    result = dot(hidden_low, down_w).reshape(2, tok_rows, D)
    own_result, other_result = by_core(ix, result[0], result[1])
    own_result = own_result + flipped(other_result.astype(LOW), 1).astype(FULL)
    own_middle = lax.dynamic_slice_in_dim(middle, ix.core * tok_rows, tok_rows, 0)
    out_tokens = (own_middle + (own_result + bias_down)).astype(LOW)

    grad_hidden = dot_turned(chip_cotangent, down_w)
    act_value, act_back = jax.vjp(smooth_act, hidden_pre)
    grad_pre = act_back(grad_hidden)[0].astype(LOW)
    partial_two = dot_turned(grad_pre, up_w)
    grad_gain_two = jnp.sum(partial_two * unit_two, axis=0)
    grad_shift_two = jnp.sum(partial_two, axis=0)
    grad_normed_two = partial_two + flipped(partial_two.astype(LOW), 1).astype(FULL)
    grad_normed_two, grad_pre, sum_down = tied(grad_normed_two, grad_pre, sum_down)
    sum_down = scatter_mid(sum_down, orders, 1, 9)
    grad_upw = outer_sum(normed_two, grad_pre)
    grad_middle = chip_cotangent.astype(FULL) + norm_back(
        grad_normed_two, unit_two, inverse_two, gain_two
    )
    grad_branch = grad_middle.astype(LOW)
    own_part = lax.dynamic_slice_in_dim(grad_branch, ix.core * out_wide, out_wide, 1)
    grad_outw = outer_sum(attended, own_part)
    own_out = lax.dynamic_slice_in_dim(out_w, ix.core * wide, wide, 0)
    grad_mixed = dot_turned(grad_branch, own_out).astype(LOW)
    grad_mixed, grad_outw, grad_upw, sum_down = tied(grad_mixed, grad_outw, grad_upw, sum_down)
    sum_second = take_apart(ix, [grad_outw, grad_upw], orders, second_spots)
    sum_second = scatter_mid(sum_second, orders, 0, 1)
    early_back = attend_back(weights[1], grad_mixed, early_qkv, tok_rows, 0, SIDE - 1)
    sum_early = take_apart(ix, [outer_sum(near_normed, early_back)], orders[:1], first_spots[:1])
    sum_down = scatter_top(ix, sum_down)
    early_back, grad_mixed, sum_early = tied(early_back, grad_mixed, sum_early)
    sum_early = scatter_mid(sum_early, orders[:1], 0, 1)
    late_back = attend_back(weights[0], grad_mixed, late_qkv, tok_rows, SIDE - 1, 1)
    late_spots = [[(0, late, 0, 0)]]
    sum_late = take_apart(ix, [outer_sum(near_normed, late_back)], orders[1:], late_spots)
    late_back, sum_second, sum_late, sum_down = tied(late_back, sum_second, sum_late, sum_down)
    sum_late = scatter_mid(sum_late, orders[1:], 0, 1)
    sum_second = scatter_mid(sum_second, orders, 1, 9)

    grad_near = (dot_turned(early_back, early_w) + dot_turned(late_back, late_w)).astype(LOW)
    grad_near, sum_early = tied(grad_near, sum_early)
    sum_early = scatter_mid(sum_early, orders[:1], 1, 9)
    grad_gain_one = jnp.sum(grad_near.astype(FULL) * near_unit, axis=0)
    grad_shift_one = jnp.sum(grad_near.astype(FULL), axis=0)
    own_half = (jnp.arange(2) == ix.core).astype(FULL)[:, None]
    grad_bias = jnp.concatenate(
        [jnp.sum(early_back.astype(FULL), axis=0), jnp.sum(late_back.astype(FULL), axis=0)]
    ).reshape(SIDE, 3, PAIR)
    grad_bias_q, grad_bias_v = (grad_bias[:, i].reshape(1, wide) for i in (0, 2))
    vec_rows = jnp.stack(
        [
            grad_gain_one,
            grad_shift_one,
            (grad_bias_q * own_half).reshape(D),
            (grad_bias_v * own_half).reshape(D),
            0.5 * jnp.sum(grad_branch.astype(FULL), axis=0),
            grad_gain_two,
            grad_shift_two,
            jnp.sum(cotangent.astype(FULL), axis=0),
        ],
        axis=0,
    )
    grad_bias_up = jnp.sum(grad_pre.astype(FULL), axis=0).reshape(ix.count // 2, 1, share)
    grad_vec = jnp.concatenate([vec_rows.T.reshape(-1), (grad_bias_up * own_half).reshape(-1)])
    grad_vec = lax.optimization_barrier(grad_vec).astype(LOW).reshape(D, VCOLS)
    grad_vec = jnp.pad(grad_vec, ((0, 0), (0, 128 - VCOLS)))
    grad_vec, sum_late, sum_second = tied(grad_vec, sum_late, sum_second)
    sum_late = scatter_mid(sum_late, orders[1:], 1, 9)
    sum_second = scatter_top(ix, sum_second)
    vec_spots = [[(0, 128, 0, 0)]]
    sum_vec = scatter_mid(take_apart(ix, [grad_vec], orders[:1], vec_spots), orders[:1], 0, 9)

    blocks = grad_near.reshape(reach_count // 2 + 1, 2, tok_rows, D)
    own_blocks, other_blocks = by_core(ix, blocks[:, 0], blocks[:, 1])
    own_blocks = own_blocks.astype(FULL) + flipped(other_blocks, 1).astype(FULL)
    four_back, two_back = own_blocks[0].astype(LOW), own_blocks[1].astype(LOW)
    sum_early, sum_late, sum_vec, own_blocks, two_back, four_back = tied(
        sum_early, sum_late, sum_vec, own_blocks, two_back, four_back
    )
    sum_first = scatter_top(ix, sum_early + sum_late + sum_vec)
    own = (
        own_blocks[2]
        + shifted(two_back, -2).astype(FULL)
        + shifted(four_back, -4).astype(FULL)
    )
    unit_one, inverse_one = norm_parts(tokens.astype(FULL))
    own_grad_middle = lax.dynamic_slice_in_dim(grad_middle, ix.core * tok_rows, tok_rows, 0)
    input_grad = own_grad_middle + norm_back(own, unit_one, inverse_one, gain_one)

    keep_second, other_second = own_rows(ix, sum_second)
    keep_first, other_first = own_rows(ix, sum_first)
    g_vec = (keep_first[:, columns:] + other_first[:, columns:])[:, :VCOLS].reshape(-1)
    g_qkv = plain_columns(by_core(ix, keep_first[:, :columns], other_first[:, :columns]))
    g_out = jnp.concatenate(
        by_core(ix, keep_second[:, :out_wide], other_second[:, :out_wide]), axis=1
    )
    g_up = plain_hidden(by_core(ix, keep_second[:, out_wide:], other_second[:, out_wide:]), share)

    rate_qkv, rate_out, rate_up, rate_down = matrix_rates()
    entries = ix.me * vectors.shape[0] + jnp.arange(vectors.shape[0], dtype=jnp.int32)
    qkv_new = adamw(w_qkv, m_qkv, v_qkv, g_qkv.reshape(-1), rate_qkv, DECAY_RATE)
    out_new = adamw(w_out, m_out, v_out, g_out.reshape(-1), rate_out, DECAY_RATE)
    up_new = adamw(w_up, m_up, v_up, g_up.reshape(-1), rate_up, DECAY_RATE)
    down_new = adamw(w_down, m_down, v_down, sum_down.reshape(-1), rate_down, DECAY_RATE)
    vec_new = adamw(vectors, m_vec, v_vec, g_vec, vector_rates(entries), 0.0)
    return (out_tokens, input_grad) + qkv_new + out_new + up_new + down_new + vec_new


def solution(mesh):
    in_specs = (P("dev", None), P("dev", None)) + (P("dev"),) * 16
    out_specs = (P("dev", None), P("dev", None)) + (P("dev"),) * 15
    return jax.shard_map(body, mesh=mesh, in_specs=in_specs, out_specs=out_specs, check_vma=False)
```

```python
import jax
import jax.numpy as jnp
from jax import lax
from jax.experimental import pallas as pl
from jax.experimental.pallas import tpu as pltpu
from jax.sharding import PartitionSpec as P

D = 768
HEAD_DIM = 64
HEADS = D // HEAD_DIM
FF = 3072
SEQ_MOST = 1024
STEP = 10
VCOLS = 12


NORM_EPS = 1e-05
BETA_ONE = 0.9
BETA_TWO = 0.999
ADAM_EPS = 1e-08
DECAY_RATE = 0.01
NEG_LARGE = -1e30

LOW = jnp.bfloat16
FULL = jnp.float32


def norm_parts(values):
    centre = jnp.mean(values, axis=-1, keepdims=True)
    centred = values - centre
    spread = jnp.mean(centred * centred, axis=-1, keepdims=True)
    inverse = lax.rsqrt(spread + NORM_EPS)
    return centred * inverse, inverse


def norm_back(grad, unit, inverse, gain_vec):
    scaled = grad * gain_vec
    along = jnp.mean(scaled * unit, axis=-1, keepdims=True)
    return inverse * (scaled - jnp.mean(scaled, axis=-1, keepdims=True) - unit * along)


def smooth_act(values):
    return jax.nn.gelu(values, approximate=True)


def adamw(weight, moment, second, gradient, step_rate, decay_rate):
    moment = BETA_ONE * moment + (1.0 - BETA_ONE) * gradient
    second = BETA_TWO * second + (1.0 - BETA_TWO) * gradient * gradient
    first_hat = moment / (1.0 - BETA_ONE**STEP)
    second_hat = second / (1.0 - BETA_TWO**STEP)
    weight = weight - step_rate * (
        first_hat / (jnp.sqrt(second_hat) + ADAM_EPS) + decay_rate * weight
    )
    return (moment, second, weight)


def matrix_rates():
    return (
        2.5 * D ** (-0.5),
        2.5 * max(1, D * 16 // SEQ_MOST) ** (-0.5),
        2.5 * D ** (-0.5),
        2.5 * FF ** (-0.5),
    )


def vector_rates(entries):
    column = entries % 8
    is_gain = (entries < 8 * D) & ((column == 0) | (column == 5))
    return jnp.where(is_gain, 0.3, 0.05).astype(jnp.float32)


def shifted(x, by):
    length = lax.axis_size("dev")
    return lax.ppermute(x, "dev", [(i, i + by) for i in range(length) if 0 <= i + by < length])


def flipped(x, mask):
    return lax.ppermute(x, "dev", [(i, i ^ mask) for i in range(lax.axis_size("dev"))])


def tied(*arrays):
    return lax.optimization_barrier(arrays)


class Index:
    def __init__(self):
        self.count = lax.axis_size("dev")
        self.me = lax.axis_index("dev")
        self.top = self.count.bit_length() - 3
        self.core = self.me & 1
        self.odd = self.core == 1
        middle = tuple(range(1, self.top))
        self.orders = (middle, tuple(reversed(middle)))

    def relative(self, order):
        seen = [r << self.top for r in range(4)]
        for b in reversed(order):
            seen = seen + [s | 1 << b for s in seen]
        return [s >> 1 for s in seen]


def by_core(ix, own, other):
    return jnp.where(ix.odd, other, own), jnp.where(ix.odd, own, other)


def cut_at(x, column):
    return (x[..., :column], x[..., column:])


def gather_top(ix, piece):
    return jnp.stack([piece] + [flipped(piece, r << ix.top) for r in (1, 2, 3)])


def gather_mid(sides, orders):
    done = []
    for x, order in zip(sides, orders):
        for b in reversed(order[1:]):
            x = jnp.concatenate([x, flipped(x, 1 << b)], axis=0)
        done.append(x)
    return done


def gather_last(sides, orders):
    return [(x, flipped(x, 1 << order[0])) for x, order in zip(sides, orders)]


def place_kernel(rows, count, moves, inward, chip_ref, *refs):
    ins, outs = refs[:count], refs[count:]
    chip = chip_ref[0]
    for part, at, column, whole, relative, whole_column, width in moves:
        start = pl.multiple_of((chip ^ relative) * rows, rows)
        spot = (pl.ds(start, rows), pl.ds(whole_column, width))
        if inward:
            outs[whole][spot] = ins[part][at, :, column : column + width]
        else:
            outs[part][at, :, column : column + width] = ins[whole][spot]


def place(ix, rows, ins, moves, inward, out_shape):
    return pl.pallas_call(
        lambda *refs: place_kernel(rows, len(ins), moves, inward, *refs),
        in_specs=[pl.BlockSpec(memory_space=pltpu.SMEM)]
        + [pl.BlockSpec(memory_space=pltpu.VMEM)] * len(ins),
        out_specs=[pl.BlockSpec(memory_space=pltpu.VMEM)] * len(out_shape),
        out_shape=[jax.ShapeDtypeStruct(shape, LOW) for shape in out_shape],
        compiler_params=pltpu.CompilerParams(
            vmem_limit_bytes=4 * sum(rows * move[-1] for move in moves) + 2**21
        ),
    )((ix.me >> 1).astype(jnp.int32).reshape(1), *ins)


def place_moves(ix, orders, spots):
    moves = []
    for s, order in enumerate(orders):
        for spot, relative in enumerate(ix.relative(order)):
            half, at = divmod(spot, ix.count // 4)
            for column, width, whole, whole_column in spots[s]:
                moves.append((2 * s + half, at, column, whole, relative, whole_column, width))
    return moves


def assemble(ix, sides, orders, spots, widths):
    chips = ix.count // 2
    rows = sides[0][0].shape[1]
    if rows % 16:
        parts = [{} for _ in widths]
        for side, order, spot in zip(sides, orders, spots):
            seen = ix.relative(order)
            place_of = jnp.array([seen.index(r) for r in range(chips)], jnp.int32)
            pick = place_of[(ix.me >> 1) ^ jnp.arange(chips)]
            full = jnp.take(jnp.concatenate(side, axis=0), pick, axis=0)
            full = full.reshape(chips * rows, -1)
            for column, width, whole, whole_column in spot:
                parts[whole][whole_column] = full[:, column : column + width]
        return [jnp.concatenate([p[c] for c in sorted(p)], axis=1) for p in parts]
    ins = [array for side in sides for array in side]
    shapes = [(chips * rows, width) for width in widths]
    return place(ix, rows, ins, place_moves(ix, orders, spots), True, shapes)


def take_apart(ix, wholes, orders, spots):
    chips = ix.count // 2
    rows = wholes[0].shape[0] // chips
    widths = [sum(spot[1] for spot in side) for side in spots]
    if rows % 16:
        sides = []
        for order, spot in zip(orders, spots):
            side = jnp.concatenate([wholes[w][:, c : c + n] for _, n, w, c in spot], axis=1)
            pick = (ix.me >> 1) ^ jnp.array(ix.relative(order), jnp.int32)
            full = jnp.take(side.reshape(chips, rows, -1), pick, axis=0)
            sides.append((full[: chips // 2], full[chips // 2 :]))
        return sides
    shapes = [(chips // 2, rows, width) for width in widths for _ in range(2)]
    outs = place(ix, rows, wholes, place_moves(ix, orders, spots), False, shapes)
    return [(outs[2 * s], outs[2 * s + 1]) for s in range(len(spots))]


def settle(keep, other, parts):
    size = keep.shape[0] // parts
    return [
        (
            keep[i * size : (i + 1) * size].astype(FULL)
            + other[i * size : (i + 1) * size].astype(FULL)
        ).astype(LOW)
        for i in range(parts)
    ]


def scatter_mid(sides, orders, first, last):
    done = []
    for (keep, send), order in zip(sides, orders):
        for i in range(first, min(last, len(order))):
            parts = 2 if i < len(order) - 1 else 4
            settled = settle(keep, flipped(send, 1 << order[i]), parts)
            keep, send = settled[0], settled[1] if parts == 2 else settled[1:]
        done.append((keep, send))
    return done


def scatter_top(ix, sides):
    total = jnp.concatenate([keep[0] for keep, _ in sides], axis=-1).astype(FULL)
    for r in (1, 2, 3):
        part = jnp.concatenate([send[r - 1][0] for _, send in sides], axis=-1)
        total = total + flipped(part, r << ix.top).astype(FULL)
    return total


def own_rows(ix, summed):
    rows = summed.shape[0] // 2
    keep = lax.dynamic_slice_in_dim(summed, ix.core * rows, rows, 0)
    other = lax.dynamic_slice_in_dim(summed, (1 - ix.core) * rows, rows, 0)
    return keep, flipped(other, 1)


PAIR = 2 * HEAD_DIM
PAIRS = HEADS // 2
SIDE = PAIRS // 2
SCALE = HEAD_DIM ** (-0.5)
VMEM_BYTES = 20 * 1024 * 1024


def by_head(pair):
    low_half = lax.broadcasted_iota(jnp.int32, pair.shape, 1) < HEAD_DIM
    zero = jnp.zeros_like(pair)
    return (
        low_half,
        jnp.where(low_half, pair, zero).astype(LOW),
        jnp.where(low_half, zero, pair).astype(LOW),
    )


def dot_over(operand_a, operand_b, dim_a, dim_b):
    return lax.dot_general(
        operand_a, operand_b, (((dim_a,), (dim_b,)), ((), ())), preferred_element_type=FULL
    )


def attend_kernel(first_ref, qkv_ref, out_ref, weights_ref):
    rows, near = weights_ref.shape[-2:]
    before = near - rows
    key = lax.broadcasted_iota(jnp.int32, (rows, near), 1)
    last = lax.broadcasted_iota(jnp.int32, (rows, near), 0) + (near - rows)
    for block in range(2):
        own, seen = pl.ds(block * rows, rows), pl.ds(block * rows, near)
        query = qkv_ref[pl.ds(before + block * rows, rows), :PAIR]
        low_half, *q_heads = by_head(query.astype(FULL) * SCALE)
        k, v = qkv_ref[seen, PAIR : 2 * PAIR], qkv_ref[seen, 2 * PAIR :]
        allowed = (key >= first_ref[own, :] - block * rows) & (key <= last)
        blended = []
        for head in range(2):
            scores = jnp.where(allowed, dot_over(q_heads[head], k, 1, 1), NEG_LARGE)
            weights = jnp.exp(scores - jnp.max(scores, axis=-1, keepdims=True))
            weights = weights * (1.0 / jnp.sum(weights, axis=-1, keepdims=True))
            weights = weights.astype(LOW)
            weights_ref[0, 2 * block + head] = weights
            blended.append(dot_over(weights, v, 1, 0))
        out_ref[own, :] = jnp.where(low_half, blended[0], blended[1]).astype(LOW)


def attend(first_key, qkv, rows, first, pairs):
    window = qkv.shape[0]
    near = window - rows
    return pl.pallas_call(
        attend_kernel,
        grid=(pairs,),
        in_specs=[
            pl.BlockSpec((2 * rows, 1), lambda i: (0, 0)),
            pl.BlockSpec((window, 3 * PAIR), lambda i: (0, i + first)),
        ],
        out_specs=[
            pl.BlockSpec((2 * rows, PAIR), lambda i: (0, i)),
            pl.BlockSpec((1, 4, rows, near), lambda i: (i, 0, 0, 0)),
        ],
        out_shape=[
            jax.ShapeDtypeStruct((2 * rows, pairs * PAIR), LOW),
            jax.ShapeDtypeStruct((pairs, 4, rows, near), LOW),
        ],
        compiler_params=pltpu.CompilerParams(vmem_limit_bytes=VMEM_BYTES),
    )(first_key, qkv)


def attend_back_kernel(weights_ref, grad_ref, qkv_ref, out_ref):
    rows, near = weights_ref.shape[-2:]
    before = near - rows
    out_ref[:before, :PAIR] = jnp.zeros((before, PAIR), LOW)
    turned = []
    for block in range(2):
        own, seen = pl.ds(block * rows, rows), pl.ds(block * rows, near)
        low_half, *grad_heads = by_head(grad_ref[own, :].astype(FULL))
        asking = pl.ds(before + block * rows, rows)
        _, *q_heads = by_head(qkv_ref[asking, :PAIR].astype(FULL))
        k, v = qkv_ref[seen, PAIR : 2 * PAIR], qkv_ref[seen, 2 * PAIR :]
        dq = []
        dk_turned = dv_turned = 0.0
        for head in range(2):
            weights_low = weights_ref[0, 2 * block + head]
            weights = weights_low.astype(FULL)
            grad_weights = dot_over(grad_heads[head], v, 1, 1)
            inner_sum = jnp.sum(weights * grad_weights, axis=-1, keepdims=True)
            grad_scores = (weights * (grad_weights - inner_sum)).astype(LOW)
            dq.append(dot_over(grad_scores, k, 1, 0))
            dk_turned += dot_over(q_heads[head], grad_scores, 0, 0)
            dv_turned += dot_over(grad_heads[head], weights_low, 0, 0)
        out_ref[asking, :PAIR] = (jnp.where(low_half, dq[0], dq[1]) * SCALE).astype(LOW)
        turned.append((dk_turned * SCALE, dv_turned))
    for which in range(2):
        early, late = turned[0][which], turned[1][which]
        whole = jnp.concatenate(
            [early[:, :rows], early[:, rows:] + late[:, : near - rows], late[:, near - rows :]],
            axis=1,
        )
        out_ref[:, (which + 1) * PAIR : (which + 2) * PAIR] = whole.T.astype(LOW)


def attend_back(weights, grad, qkv, rows, first, pairs):
    window = qkv.shape[0]
    near = window - rows
    return pl.pallas_call(
        attend_back_kernel,
        grid=(pairs,),
        in_specs=[
            pl.BlockSpec((1, 4, rows, near), lambda i: (i, 0, 0, 0)),
            pl.BlockSpec((2 * rows, PAIR), lambda i: (0, i + first)),
            pl.BlockSpec((window, 3 * PAIR), lambda i: (0, i)),
        ],
        out_specs=pl.BlockSpec((window, 3 * PAIR), lambda i: (0, i)),
        out_shape=jax.ShapeDtypeStruct((window, 3 * pairs * PAIR), LOW),
        compiler_params=pltpu.CompilerParams(vmem_limit_bytes=VMEM_BYTES),
    )(weights, grad, qkv)


def paired_columns(x):
    rows = x.shape[0]
    parts = x.reshape(rows, 3, 2, SIDE, PAIR).transpose(2, 0, 3, 1, 4)
    return parts.reshape(2, rows, 3 * SIDE * PAIR)


def plain_columns(sides):
    rows = sides[0].shape[0]
    parts = [side.reshape(rows, SIDE, 3, PAIR).transpose(0, 2, 1, 3) for side in sides]
    return jnp.stack(parts, axis=2).reshape(rows, 3 * D)


def hidden_columns(x, share):
    parts = x.reshape(x.shape[0], FF // (2 * share), 2, share)
    return [parts[:, :, s].reshape(x.shape[0], FF // 2) for s in range(2)]


def plain_hidden(sides, share):
    rows = sides[0].shape[0]
    parts = [side.reshape(rows, FF // (2 * share), 1, share) for side in sides]
    return jnp.concatenate(parts, axis=2).reshape(rows, FF)


def dot(operand_a, operand_b):
    return jnp.dot(operand_a, operand_b, preferred_element_type=FULL)


def outer_sum(operand_a, operand_b):
    return jnp.einsum("ti,tj->ij", operand_a, operand_b, preferred_element_type=FULL).astype(LOW)


def dot_turned(operand_a, operand_b):
    return jnp.einsum("ti,ji->tj", operand_a, operand_b, preferred_element_type=FULL)


def body(
    tokens,
    cotangent,
    starts,
    w_qkv,
    m_qkv,
    v_qkv,
    w_out,
    m_out,
    v_out,
    w_up,
    m_up,
    v_up,
    w_down,
    m_down,
    v_down,
    vectors,
    m_vec,
    v_vec,
):
    ix = Index()
    rows = D // ix.count
    share = FF // ix.count
    tok_rows = tokens.shape[0]
    reach_count = (SEQ_MOST + tok_rows - 2) // tok_rows
    assert reach_count == 4
    chip_rows = 2 * tok_rows
    near_rows = (reach_count + 2) * tok_rows
    wide = SIDE * PAIR
    columns = 3 * wide
    out_wide, up_wide = D // 2, FF // 2

    early = 3 * PAIR * (SIDE - 1)
    late = columns - early
    first_spots = [[(0, early, 0, 0)], [(0, late + 128, 0, 0)]]
    cut = (out_wide + up_wide) // 256 * 128
    second_spots = [
        [(0, out_wide, 0, 0), (out_wide, cut - out_wide, 1, 0)],
        [(0, out_wide + up_wide - cut, 1, cut - out_wide)],
    ]
    third_spots = [[(0, D // 2, 0, 0)], [(0, D // 2, 0, D // 2)]]
    orders = ix.orders
    vec_piece = jnp.pad(vectors.astype(LOW).reshape(rows, VCOLS), ((0, 0), (0, 128 - VCOLS)))
    qkv_mine, qkv_others = by_core(ix, *paired_columns(w_qkv.astype(LOW).reshape(rows, 3 * D)))
    mine = jnp.concatenate([qkv_mine, vec_piece], axis=1)
    others = jnp.concatenate([qkv_others, vec_piece], axis=1)
    first = jnp.concatenate(by_core(ix, mine, flipped(others, 1)), axis=0)
    first = gather_top(ix, first)
    first, tokens, w_out, w_up = tied(first, tokens, w_out, w_up)

    first = gather_mid((first[..., :early], first[..., early:]), orders)
    mine = jnp.stack([shifted(tokens, 4), shifted(tokens, 2), tokens])
    up_sides = hidden_columns(w_up.astype(LOW).reshape(rows, FF), share)
    out_low = w_out.astype(LOW).reshape(rows, D)
    pieces = [
        jnp.concatenate([out_low[:, s * out_wide : (s + 1) * out_wide], up_sides[s]], axis=1)
        for s in range(2)
    ]
    own_piece, others = by_core(ix, *pieces)
    second = jnp.concatenate(by_core(ix, own_piece, flipped(others, 1)), axis=0)
    *first, second, starts, mine = tied(*first, second, starts, mine)
    first = gather_last(first, orders)
    second = gather_top(ix, second)
    near_tokens = jnp.stack(by_core(ix, mine, flipped(mine, 1)), axis=1).reshape(near_rows, D)
    chip_starts = jnp.concatenate(by_core(ix, starts, flipped(starts, 1)))
    first, near_tokens, chip_starts, cotangent, w_down = tied(
        first, near_tokens, chip_starts, cotangent, w_down
    )
    early_w = assemble(ix, first[:1], orders[:1], first_spots[:1], [early])[0]
    late_w = assemble(ix, first[1:], orders[1:], first_spots[1:], [late + 128])[0]
    vec_all = late_w[:, late : late + VCOLS].reshape(-1).astype(FULL)
    late_w = late_w[:, :late]
    third = w_down.astype(LOW).reshape(4 * rows, D)
    vec_table, up_bias = vec_all[: 8 * D].reshape(D, 8).T, vec_all[8 * D :]
    gain_one, shift_one, bias_q, bias_v, bias_o, gain_two, shift_two, bias_down = (
        vec_table[i] for i in range(8)
    )
    up_bias = lax.dynamic_index_in_dim(
        up_bias.reshape(ix.count // 2, 2, share), ix.core, 1, keepdims=False
    ).reshape(up_wide)
    bias_q = lax.dynamic_slice_in_dim(bias_q, ix.core * wide, wide)
    bias_v = lax.dynamic_slice_in_dim(bias_v, ix.core * wide, wide)

    near_unit, near_inverse = norm_parts(near_tokens.astype(FULL))
    near_normed = (near_unit * gain_one + shift_one).astype(LOW)
    near_normed, second, third, cotangent = tied(near_normed, second, third, cotangent)
    third = gather_top(ix, third)
    second = gather_mid(cut_at(second, cut), orders)
    chip_cotangent = jnp.concatenate(by_core(ix, cotangent, flipped(cotangent, 1)), axis=0)
    bias = jnp.stack(
        [bias_q.reshape(SIDE, PAIR), jnp.zeros((SIDE, PAIR), FULL), bias_v.reshape(SIDE, PAIR)],
        axis=1,
    ).reshape(columns)
    first_key = (chip_starts - ((ix.me >> 1) * chip_rows - reach_count * tok_rows))[:, None]
    early_qkv = (dot(near_normed, early_w) + bias[:early]).astype(LOW)
    late_qkv = (dot(near_normed, late_w) + bias[early:]).astype(LOW)
    early_qkv, late_qkv, second = tied(early_qkv, late_qkv, second)
    second = gather_last(second, orders)
    mixed, weights = [None, None], [None, None]
    mixed[0], weights[0] = attend(first_key, late_qkv, tok_rows, 0, 1)
    mixed[0], early_qkv, third = tied(mixed[0], early_qkv, third)
    third = gather_mid(cut_at(third, D // 2), orders)
    mixed[1], weights[1] = attend(first_key, early_qkv, tok_rows, 0, SIDE - 1)
    mixed = jnp.concatenate([mixed[1], mixed[0]], axis=1)
    mixed, second = tied(mixed, second)
    attended = jnp.concatenate(by_core(ix, mixed, flipped(mixed, 1)), axis=1)
    out_half, up_w = assemble(ix, second, orders, second_spots, [out_wide, up_wide])
    out_w = jnp.concatenate(by_core(ix, out_half, flipped(out_half, 1)), axis=1)
    attended, out_w, third = tied(attended, out_w, third)
    third = gather_last(third, orders)
    inputs = near_tokens[near_rows - chip_rows :].astype(FULL)
    middle = inputs + (dot(attended, out_w) + bias_o)
    unit_two, inverse_two = norm_parts(middle)
    normed_two = (unit_two * gain_two + shift_two).astype(LOW)
    hidden_pre = dot(normed_two, up_w) + up_bias
    hidden_low = smooth_act(hidden_pre).astype(LOW)
    grad_downw = outer_sum(hidden_low, chip_cotangent)
    hidden_low, hidden_pre, grad_downw = tied(hidden_low, hidden_pre, grad_downw)
    sum_down = scatter_mid(take_apart(ix, [grad_downw], orders, third_spots), orders, 0, 1)
    down_w = assemble(ix, third, orders, third_spots, [D])[0]
    result = dot(hidden_low, down_w).reshape(2, tok_rows, D)
    own_result, other_result = by_core(ix, result[0], result[1])
    own_result = own_result + flipped(other_result.astype(LOW), 1).astype(FULL)
    own_middle = lax.dynamic_slice_in_dim(middle, ix.core * tok_rows, tok_rows, 0)
    out_tokens = (own_middle + (own_result + bias_down)).astype(LOW)

    grad_hidden = dot_turned(chip_cotangent, down_w)
    act_value, act_back = jax.vjp(smooth_act, hidden_pre)
    grad_pre = act_back(grad_hidden)[0].astype(LOW)
    partial_two = dot_turned(grad_pre, up_w)
    grad_gain_two = jnp.sum(partial_two * unit_two, axis=0)
    grad_shift_two = jnp.sum(partial_two, axis=0)
    grad_normed_two = partial_two + flipped(partial_two.astype(LOW), 1).astype(FULL)
    grad_normed_two, grad_pre, sum_down = tied(grad_normed_two, grad_pre, sum_down)
    sum_down = scatter_mid(sum_down, orders, 1, 9)
    grad_upw = outer_sum(normed_two, grad_pre)
    grad_middle = chip_cotangent.astype(FULL) + norm_back(
        grad_normed_two, unit_two, inverse_two, gain_two
    )
    grad_branch = grad_middle.astype(LOW)
    own_part = lax.dynamic_slice_in_dim(grad_branch, ix.core * out_wide, out_wide, 1)
    grad_outw = outer_sum(attended, own_part)
    own_out = lax.dynamic_slice_in_dim(out_w, ix.core * wide, wide, 0)
    grad_mixed = dot_turned(grad_branch, own_out).astype(LOW)
    grad_mixed, grad_outw, grad_upw, sum_down = tied(grad_mixed, grad_outw, grad_upw, sum_down)
    sum_second = take_apart(ix, [grad_outw, grad_upw], orders, second_spots)
    grad_mixed, sum_second = tied(grad_mixed, sum_second)
    sum_second = scatter_mid(sum_second, orders, 0, 1)
    early_back = attend_back(weights[1], grad_mixed, early_qkv, tok_rows, 0, SIDE - 1)
    sum_early = take_apart(ix, [outer_sum(near_normed, early_back)], orders[:1], first_spots[:1])
    sum_down = scatter_top(ix, sum_down)
    early_back, grad_mixed, sum_early = tied(early_back, grad_mixed, sum_early)
    sum_early = scatter_mid(sum_early, orders[:1], 0, 1)
    late_back = attend_back(weights[0], grad_mixed, late_qkv, tok_rows, SIDE - 1, 1)
    late_spots = [[(0, late, 0, 0)]]
    sum_late = take_apart(ix, [outer_sum(near_normed, late_back)], orders[1:], late_spots)
    sums_two = (
        grad_gain_two,
        grad_shift_two,
        jnp.sum(grad_branch.astype(FULL), axis=0),
        jnp.sum(cotangent.astype(FULL), axis=0),
        jnp.sum(grad_pre.astype(FULL), axis=0),
    )
    late_back, sum_second, sum_late, sum_down, sums_two = tied(
        late_back, sum_second, sum_late, sum_down, sums_two
    )
    grad_gain_two, grad_shift_two, grad_bias_o, grad_bias_down, grad_bias_up = sums_two
    sum_late = scatter_mid(sum_late, orders[1:], 0, 1)
    sum_second = scatter_mid(sum_second, orders, 1, 9)

    grad_near = (dot_turned(early_back, early_w) + dot_turned(late_back, late_w)).astype(LOW)
    grad_gain_one = jnp.sum(grad_near.astype(FULL) * near_unit, axis=0)
    grad_shift_one = jnp.sum(grad_near.astype(FULL), axis=0)
    own_half = (jnp.arange(2) == ix.core).astype(FULL)[:, None]
    grad_bias = jnp.concatenate(
        [jnp.sum(early_back.astype(FULL), axis=0), jnp.sum(late_back.astype(FULL), axis=0)]
    ).reshape(SIDE, 3, PAIR)
    grad_bias_q, grad_bias_v = (grad_bias[:, i].reshape(1, wide) for i in (0, 2))
    vec_rows = jnp.stack(
        [
            grad_gain_one,
            grad_shift_one,
            (grad_bias_q * own_half).reshape(D),
            (grad_bias_v * own_half).reshape(D),
            0.5 * grad_bias_o,
            grad_gain_two,
            grad_shift_two,
            grad_bias_down,
        ],
        axis=0,
    )
    grad_bias_up = grad_bias_up.reshape(ix.count // 2, 1, share)
    grad_vec = jnp.concatenate([vec_rows.T.reshape(-1), (grad_bias_up * own_half).reshape(-1)])
    grad_vec = lax.optimization_barrier(grad_vec).astype(LOW).reshape(D, VCOLS)
    grad_vec = jnp.pad(grad_vec, ((0, 0), (0, 128 - VCOLS)))
    blocks = grad_near.reshape(reach_count // 2 + 1, 2, tok_rows, D)
    own_blocks, other_blocks = by_core(ix, blocks[:, 0], blocks[:, 1])
    mate_blocks = flipped(other_blocks, 1)
    grad_vec, sum_early, sum_late, sum_second, mate_blocks = tied(
        grad_vec, sum_early, sum_late, sum_second, mate_blocks
    )
    sum_early = scatter_mid(sum_early, orders[:1], 1, 9)
    sum_late = scatter_mid(sum_late, orders[1:], 1, 9)
    sum_second = scatter_top(ix, sum_second)
    vec_spots = [[(0, 128, 0, 0)]]
    sum_vec = scatter_mid(take_apart(ix, [grad_vec], orders[:1], vec_spots), orders[:1], 0, 9)

    own_blocks = own_blocks.astype(FULL) + mate_blocks.astype(FULL)
    four_back, two_back = own_blocks[0].astype(LOW), own_blocks[1].astype(LOW)
    sum_early, sum_late, sum_vec = tied(sum_early, sum_late, sum_vec)
    sum_first = scatter_top(ix, sum_early + sum_late + sum_vec)
    sum_first, sum_second = tied(sum_first, sum_second)
    own = (
        own_blocks[2]
        + shifted(two_back, -2).astype(FULL)
        + shifted(four_back, -4).astype(FULL)
    )
    unit_one, inverse_one = norm_parts(tokens.astype(FULL))
    own_grad_middle = lax.dynamic_slice_in_dim(grad_middle, ix.core * tok_rows, tok_rows, 0)
    input_grad = own_grad_middle + norm_back(own, unit_one, inverse_one, gain_one)

    keep_second, other_second = own_rows(ix, sum_second)
    keep_first, other_first = own_rows(ix, sum_first)
    g_vec = (keep_first[:, columns:] + other_first[:, columns:])[:, :VCOLS].reshape(-1)
    g_qkv = plain_columns(by_core(ix, keep_first[:, :columns], other_first[:, :columns]))
    g_out = jnp.concatenate(
        by_core(ix, keep_second[:, :out_wide], other_second[:, :out_wide]), axis=1
    )
    g_up = plain_hidden(by_core(ix, keep_second[:, out_wide:], other_second[:, out_wide:]), share)

    rate_qkv, rate_out, rate_up, rate_down = matrix_rates()
    entries = ix.me * vectors.shape[0] + jnp.arange(vectors.shape[0], dtype=jnp.int32)
    qkv_new = adamw(w_qkv, m_qkv, v_qkv, g_qkv.reshape(-1), rate_qkv, DECAY_RATE)
    out_new = adamw(w_out, m_out, v_out, g_out.reshape(-1), rate_out, DECAY_RATE)
    up_new = adamw(w_up, m_up, v_up, g_up.reshape(-1), rate_up, DECAY_RATE)
    down_new = adamw(w_down, m_down, v_down, sum_down.reshape(-1), rate_down, DECAY_RATE)
    vec_new = adamw(vectors, m_vec, v_vec, g_vec, vector_rates(entries), 0.0)
    return (out_tokens, input_grad) + qkv_new + out_new + up_new + down_new + vec_new


def solution(mesh):
    in_specs = (P("dev", None), P("dev", None)) + (P("dev"),) * 16
    out_specs = (P("dev", None), P("dev", None)) + (P("dev"),) * 15
    return jax.shard_map(body, mesh=mesh, in_specs=in_specs, out_specs=out_specs, check_vma=False)
```

```python
import jax
import jax.numpy as jnp
import numpy as np
from jax import lax
from jax.experimental import pallas as pl
from jax.experimental.pallas import tpu as pltpu
from jax.sharding import PartitionSpec as P

D = 768
HEAD_DIM = 64
HEADS = D // HEAD_DIM
FF = 3072
SEQ_MOST = 1024
STEP = 10
VCOLS = 12


NORM_EPS = 1e-05
BETA_ONE = 0.9
BETA_TWO = 0.999
ADAM_EPS = 1e-08
DECAY_RATE = 0.01
NEG_LARGE = -1e30

LOW = jnp.bfloat16
FULL = jnp.float32


def norm_parts(values):
    centre = jnp.mean(values, axis=-1, keepdims=True)
    centred = values - centre
    spread = jnp.mean(centred * centred, axis=-1, keepdims=True)
    inverse = lax.rsqrt(spread + NORM_EPS)
    return centred * inverse, inverse


def norm_back(grad, unit, inverse, gain_vec):
    scaled = grad * gain_vec
    along = jnp.mean(scaled * unit, axis=-1, keepdims=True)
    return inverse * (scaled - jnp.mean(scaled, axis=-1, keepdims=True) - unit * along)


def smooth_act(values):
    return jax.nn.gelu(values, approximate=True)


def adamw(weight, moment, second, gradient, step_rate, decay_rate):
    moment = BETA_ONE * moment + (1.0 - BETA_ONE) * gradient
    second = BETA_TWO * second + (1.0 - BETA_TWO) * gradient * gradient
    first_hat = moment / (1.0 - BETA_ONE**STEP)
    second_hat = second / (1.0 - BETA_TWO**STEP)
    weight = weight - step_rate * (
        first_hat / (jnp.sqrt(second_hat) + ADAM_EPS) + decay_rate * weight
    )
    return (moment, second, weight)


def matrix_rates():
    return (
        2.5 * D ** (-0.5),
        2.5 * max(1, D * 16 // SEQ_MOST) ** (-0.5),
        2.5 * D ** (-0.5),
        2.5 * FF ** (-0.5),
    )


def vector_rates(entries):
    column = entries % 8
    is_gain = (entries < 8 * D) & ((column == 0) | (column == 5))
    return jnp.where(is_gain, 0.3, 0.05).astype(jnp.float32)


def shifted(x, by):
    length = lax.axis_size("dev")
    return lax.ppermute(x, "dev", [(i, i + by) for i in range(length) if 0 <= i + by < length])


def flipped(x, mask):
    return lax.ppermute(x, "dev", [(i, i ^ mask) for i in range(lax.axis_size("dev"))])


def tied(*arrays):
    return lax.optimization_barrier(arrays)


class Index:
    def __init__(self):
        self.count = lax.axis_size("dev")
        self.me = lax.axis_index("dev")
        self.top = self.count.bit_length() - 3
        self.core = self.me & 1
        self.odd = self.core == 1
        middle = tuple(range(1, self.top))
        self.orders = (middle, tuple(reversed(middle)))

    def relative(self, order):
        seen = [r << self.top for r in range(4)]
        for b in reversed(order):
            seen = seen + [s | 1 << b for s in seen]
        return [s >> 1 for s in seen]


def by_core(ix, own, other):
    return jnp.where(ix.odd, other, own), jnp.where(ix.odd, own, other)


def cut_at(x, column):
    return (x[..., :column], x[..., column:])


def gather_top(ix, piece):
    return jnp.stack([piece] + [flipped(piece, r << ix.top) for r in (1, 2, 3)])


def gather_mid(sides, orders):
    done = []
    for x, order in zip(sides, orders):
        for b in reversed(order[1:]):
            x = jnp.concatenate([x, flipped(x, 1 << b)], axis=0)
        done.append(x)
    return done


def gather_last(sides, orders):
    return [(x, flipped(x, 1 << order[0])) for x, order in zip(sides, orders)]


def place_kernel(rows, count, moves, inward, chip_ref, *refs):
    ins, outs = refs[:count], refs[count:]
    chip = chip_ref[0]
    for part, at, column, whole, relative, whole_column, width in moves:
        start = pl.multiple_of((chip ^ relative) * rows, rows)
        spot = (pl.ds(start, rows), pl.ds(whole_column, width))
        if inward:
            outs[whole][spot] = ins[part][at, :, column : column + width]
        else:
            outs[part][at, :, column : column + width] = ins[whole][spot]


def place(ix, rows, ins, moves, inward, out_shape):
    return pl.pallas_call(
        lambda *refs: place_kernel(rows, len(ins), moves, inward, *refs),
        in_specs=[pl.BlockSpec(memory_space=pltpu.SMEM)]
        + [pl.BlockSpec(memory_space=pltpu.VMEM)] * len(ins),
        out_specs=[pl.BlockSpec(memory_space=pltpu.VMEM)] * len(out_shape),
        out_shape=[jax.ShapeDtypeStruct(shape, LOW) for shape in out_shape],
        compiler_params=pltpu.CompilerParams(
            vmem_limit_bytes=4 * sum(rows * move[-1] for move in moves) + 2**21
        ),
    )((ix.me >> 1).astype(jnp.int32).reshape(1), *ins)


def place_moves(ix, orders, spots):
    moves = []
    for s, order in enumerate(orders):
        for spot, relative in enumerate(ix.relative(order)):
            half, at = divmod(spot, ix.count // 4)
            for column, width, whole, whole_column in spots[s]:
                moves.append((2 * s + half, at, column, whole, relative, whole_column, width))
    return moves


def assemble(ix, sides, orders, spots, widths):
    chips = ix.count // 2
    rows = sides[0][0].shape[1]
    if rows % 16:
        parts = [{} for _ in widths]
        for side, order, spot in zip(sides, orders, spots):
            seen = ix.relative(order)
            place_of = jnp.array([seen.index(r) for r in range(chips)], jnp.int32)
            pick = place_of[(ix.me >> 1) ^ jnp.arange(chips)]
            full = jnp.take(jnp.concatenate(side, axis=0), pick, axis=0)
            full = full.reshape(chips * rows, -1)
            for column, width, whole, whole_column in spot:
                parts[whole][whole_column] = full[:, column : column + width]
        return [jnp.concatenate([p[c] for c in sorted(p)], axis=1) for p in parts]
    ins = [array for side in sides for array in side]
    shapes = [(chips * rows, width) for width in widths]
    return place(ix, rows, ins, place_moves(ix, orders, spots), True, shapes)


def take_apart(ix, wholes, orders, spots):
    chips = ix.count // 2
    rows = wholes[0].shape[0] // chips
    widths = [sum(spot[1] for spot in side) for side in spots]
    if rows % 16:
        sides = []
        for order, spot in zip(orders, spots):
            side = jnp.concatenate([wholes[w][:, c : c + n] for _, n, w, c in spot], axis=1)
            pick = (ix.me >> 1) ^ jnp.array(ix.relative(order), jnp.int32)
            full = jnp.take(side.reshape(chips, rows, -1), pick, axis=0)
            sides.append((full[: chips // 2], full[chips // 2 :]))
        return sides
    shapes = [(chips // 2, rows, width) for width in widths for _ in range(2)]
    outs = place(ix, rows, wholes, place_moves(ix, orders, spots), False, shapes)
    return [(outs[2 * s], outs[2 * s + 1]) for s in range(len(spots))]


def settle(keep, other, parts):
    size = keep.shape[0] // parts
    return [
        (
            keep[i * size : (i + 1) * size].astype(FULL)
            + other[i * size : (i + 1) * size].astype(FULL)
        ).astype(LOW)
        for i in range(parts)
    ]


def scatter_mid(sides, orders, first, last):
    done = []
    for (keep, send), order in zip(sides, orders):
        for i in range(first, min(last, len(order))):
            parts = 2 if i < len(order) - 1 else 4
            settled = settle(keep, flipped(send, 1 << order[i]), parts)
            keep, send = settled[0], settled[1] if parts == 2 else settled[1:]
        done.append((keep, send))
    return done


def scatter_top(ix, sides):
    total = jnp.concatenate([keep[0] for keep, _ in sides], axis=-1).astype(FULL)
    for r in (1, 2, 3):
        part = jnp.concatenate([send[r - 1][0] for _, send in sides], axis=-1)
        total = total + flipped(part, r << ix.top).astype(FULL)
    return total


def own_rows(ix, summed):
    rows = summed.shape[0] // 2
    keep = lax.dynamic_slice_in_dim(summed, ix.core * rows, rows, 0)
    other = lax.dynamic_slice_in_dim(summed, (1 - ix.core) * rows, rows, 0)
    return keep, flipped(other, 1)


PAIR = 2 * HEAD_DIM
PAIRS = HEADS // 2
SIDE = PAIRS // 2
SCALE = HEAD_DIM ** (-0.5)
VMEM_BYTES = 20 * 1024 * 1024


def by_head(pair):
    low_half = lax.broadcasted_iota(jnp.int32, pair.shape, 1) < HEAD_DIM
    zero = jnp.zeros_like(pair)
    return (
        low_half,
        jnp.where(low_half, pair, zero).astype(LOW),
        jnp.where(low_half, zero, pair).astype(LOW),
    )


def dot_over(operand_a, operand_b, dim_a, dim_b):
    return lax.dot_general(
        operand_a, operand_b, (((dim_a,), (dim_b,)), ((), ())), preferred_element_type=FULL
    )


def attend_kernel(first_ref, qkv_ref, out_ref, weights_ref):
    rows, near = weights_ref.shape[-2:]
    before = near - rows
    key = lax.broadcasted_iota(jnp.int32, (rows, near), 1)
    last = lax.broadcasted_iota(jnp.int32, (rows, near), 0) + (near - rows)
    for block in range(2):
        own, seen = pl.ds(block * rows, rows), pl.ds(block * rows, near)
        query = qkv_ref[pl.ds(before + block * rows, rows), :PAIR]
        low_half, *q_heads = by_head(query.astype(FULL) * SCALE)
        k, v = qkv_ref[seen, PAIR : 2 * PAIR], qkv_ref[seen, 2 * PAIR :]
        allowed = (key >= first_ref[own, :] - block * rows) & (key <= last)
        blended = []
        for head in range(2):
            scores = jnp.where(allowed, dot_over(q_heads[head], k, 1, 1), NEG_LARGE)
            weights = jnp.exp(scores - jnp.max(scores, axis=-1, keepdims=True))
            weights = weights * (1.0 / jnp.sum(weights, axis=-1, keepdims=True))
            weights = weights.astype(LOW)
            weights_ref[0, 2 * block + head] = weights
            blended.append(dot_over(weights, v, 1, 0))
        out_ref[own, :] = jnp.where(low_half, blended[0], blended[1]).astype(LOW)


def attend(first_key, qkv, rows, first, pairs):
    window = qkv.shape[0]
    near = window - rows
    return pl.pallas_call(
        attend_kernel,
        grid=(pairs,),
        in_specs=[
            pl.BlockSpec((2 * rows, 1), lambda i: (0, 0)),
            pl.BlockSpec((window, 3 * PAIR), lambda i: (0, i + first)),
        ],
        out_specs=[
            pl.BlockSpec((2 * rows, PAIR), lambda i: (0, i)),
            pl.BlockSpec((1, 4, rows, near), lambda i: (i, 0, 0, 0)),
        ],
        out_shape=[
            jax.ShapeDtypeStruct((2 * rows, pairs * PAIR), LOW),
            jax.ShapeDtypeStruct((pairs, 4, rows, near), LOW),
        ],
        compiler_params=pltpu.CompilerParams(vmem_limit_bytes=VMEM_BYTES),
    )(first_key, qkv)


def attend_back_kernel(weights_ref, grad_ref, qkv_ref, out_ref):
    rows, near = weights_ref.shape[-2:]
    before = near - rows
    out_ref[:before, :PAIR] = jnp.zeros((before, PAIR), LOW)
    turned = []
    for block in range(2):
        own, seen = pl.ds(block * rows, rows), pl.ds(block * rows, near)
        low_half, *grad_heads = by_head(grad_ref[own, :].astype(FULL))
        asking = pl.ds(before + block * rows, rows)
        _, *q_heads = by_head(qkv_ref[asking, :PAIR].astype(FULL))
        k, v = qkv_ref[seen, PAIR : 2 * PAIR], qkv_ref[seen, 2 * PAIR :]
        dq = []
        dk_turned = dv_turned = 0.0
        for head in range(2):
            weights_low = weights_ref[0, 2 * block + head]
            weights = weights_low.astype(FULL)
            grad_weights = dot_over(grad_heads[head], v, 1, 1)
            inner_sum = jnp.sum(weights * grad_weights, axis=-1, keepdims=True)
            grad_scores = (weights * (grad_weights - inner_sum)).astype(LOW)
            dq.append(dot_over(grad_scores, k, 1, 0))
            dk_turned += dot_over(q_heads[head], grad_scores, 0, 0)
            dv_turned += dot_over(grad_heads[head], weights_low, 0, 0)
        out_ref[asking, :PAIR] = (jnp.where(low_half, dq[0], dq[1]) * SCALE).astype(LOW)
        turned.append((dk_turned * SCALE, dv_turned))
    for which in range(2):
        early, late = turned[0][which], turned[1][which]
        whole = jnp.concatenate(
            [early[:, :rows], early[:, rows:] + late[:, : near - rows], late[:, near - rows :]],
            axis=1,
        )
        out_ref[:, (which + 1) * PAIR : (which + 2) * PAIR] = whole.T.astype(LOW)


def attend_back(weights, grad, qkv, rows, first, pairs):
    window = qkv.shape[0]
    near = window - rows
    return pl.pallas_call(
        attend_back_kernel,
        grid=(pairs,),
        in_specs=[
            pl.BlockSpec((1, 4, rows, near), lambda i: (i, 0, 0, 0)),
            pl.BlockSpec((2 * rows, PAIR), lambda i: (0, i + first)),
            pl.BlockSpec((window, 3 * PAIR), lambda i: (0, i)),
        ],
        out_specs=pl.BlockSpec((window, 3 * PAIR), lambda i: (0, i)),
        out_shape=jax.ShapeDtypeStruct((window, 3 * pairs * PAIR), LOW),
        compiler_params=pltpu.CompilerParams(vmem_limit_bytes=VMEM_BYTES),
    )(weights, grad, qkv)


def paired_columns(x):
    rows = x.shape[0]
    parts = x.reshape(rows, 3, 2, SIDE, PAIR).transpose(2, 0, 3, 1, 4)
    return parts.reshape(2, rows, 3 * SIDE * PAIR)


def plain_columns(sides):
    rows = sides[0].shape[0]
    parts = [side.reshape(rows, SIDE, 3, PAIR).transpose(0, 2, 1, 3) for side in sides]
    return jnp.stack(parts, axis=2).reshape(rows, 3 * D)


def hidden_columns(x, share):
    parts = x.reshape(x.shape[0], FF // (2 * share), 2, share)
    return [parts[:, :, s].reshape(x.shape[0], FF // 2) for s in range(2)]


def plain_hidden(sides, share):
    rows = sides[0].shape[0]
    parts = [side.reshape(rows, FF // (2 * share), 1, share) for side in sides]
    return jnp.concatenate(parts, axis=2).reshape(rows, FF)


TABLE_ROWS = 8 * D // VCOLS


def table_places():
    feature = np.arange(D)[None]
    entry = 8 * (feature % 3) + np.arange(8)[:, None]
    first_row = 2 * (feature // 3)
    return (
        jnp.asarray(first_row, jnp.int32),
        jnp.asarray(entry // VCOLS, jnp.int32),
        jnp.asarray(entry % VCOLS, jnp.int32),
    )


def up_places(ix, share):
    unit = np.arange(FF // 2)[None]
    row = 2 * (unit // share) * (share // VCOLS) + unit % share // VCOLS
    return (
        jnp.asarray(row, jnp.int32) + ix.core * (share // VCOLS),
        jnp.asarray(unit % VCOLS, jnp.int32),
    )


def one_at(row, rows):
    at = lax.broadcasted_iota(jnp.int32, (rows, row.shape[1]), 0)
    return jnp.where(at == row, 1.0, 0.0).astype(LOW)


def in_column(column):
    return lax.broadcasted_iota(jnp.int32, (16, column.shape[1]), 0) == column


def read_vec_kernel(vec_ref, first_ref, step_ref, column_ref, row_ref, spot_ref, table_ref, up_ref):
    vec = vec_ref[...]
    table = vec[:TABLE_ROWS]
    moved = [dot_over(table, one_at(first_ref[...] + d, TABLE_ROWS), 0, 0)[:16] for d in range(2)]
    for c in range(8):
        step = step_ref[c : c + 1, :]
        picked = jnp.where(step == 0, moved[0], moved[1])
        picked = jnp.where(in_column(column_ref[c : c + 1, :]), picked, 0.0)
        table_ref[c : c + 1, :] = jnp.sum(picked, axis=0, keepdims=True)
    rest = vec[TABLE_ROWS:]
    moved = dot_over(rest, one_at(row_ref[...], rest.shape[0]), 0, 0)[:16]
    picked = jnp.where(in_column(spot_ref[...]), moved, 0.0)
    up_ref[...] = jnp.sum(picked, axis=0, keepdims=True)


def read_vec(ix, vec, share):
    return pl.pallas_call(
        read_vec_kernel,
        out_shape=[
            jax.ShapeDtypeStruct((8, D), FULL),
            jax.ShapeDtypeStruct((1, FF // 2), FULL),
        ],
        compiler_params=pltpu.CompilerParams(vmem_limit_bytes=VMEM_BYTES),
    )(vec, *table_places(), *up_places(ix, share))


def write_vec_kernel(
    core_ref, table_ref, bias_ref, up_ref, first_ref, step_ref, column_ref, row_ref, spot_ref, out_ref
):
    core = core_ref[0]
    wide = SIDE * PAIR
    moved = [jnp.zeros((16, D), FULL) for _ in range(2)]
    for c in range(8):
        row = table_ref[c : c + 1, :]
        if c in (2, 3):
            part = 0 if c == 2 else 2
            half = jnp.concatenate(
                [
                    bias_ref[:, (3 * i + part) * PAIR : (3 * i + part + 1) * PAIR]
                    for i in range(SIDE)
                ],
                axis=1,
            )
            lane = lax.broadcasted_iota(jnp.int32, (1, D), 1)
            own = (lane >= core * wide) & (lane < (core + 1) * wide)
            row = jnp.where(own, jnp.concatenate([half, half], axis=1), 0.0)
        step = step_ref[c : c + 1, :]
        here = in_column(column_ref[c : c + 1, :])
        for d in range(2):
            moved[d] = moved[d] + jnp.where(here & (step == d), row, 0.0)
    blank = jnp.zeros((112, D), LOW)
    total = 0.0
    for d in range(2):
        wanted = jnp.concatenate([moved[d].astype(LOW), blank], axis=0)
        total = total + dot_over(one_at(first_ref[...] + d, TABLE_ROWS), wanted, 1, 1)
    out_ref[:TABLE_ROWS, :] = total.astype(LOW)
    rest = out_ref.shape[0] - TABLE_ROWS
    wanted = jnp.where(in_column(spot_ref[...]), up_ref[...], 0.0).astype(LOW)
    wanted = jnp.concatenate([wanted, jnp.zeros((112, wanted.shape[1]), LOW)], axis=0)
    out_ref[TABLE_ROWS:, :] = dot_over(one_at(row_ref[...], rest), wanted, 1, 1).astype(LOW)


def write_vec(ix, table, bias, up, share):
    whole = pl.BlockSpec(memory_space=pltpu.VMEM)
    return pl.pallas_call(
        write_vec_kernel,
        in_specs=[pl.BlockSpec(memory_space=pltpu.SMEM)] + [whole] * 8,
        out_specs=whole,
        out_shape=jax.ShapeDtypeStruct((D, 128), LOW),
        compiler_params=pltpu.CompilerParams(vmem_limit_bytes=VMEM_BYTES),
    )(
        ix.core.astype(jnp.int32).reshape(1),
        table,
        bias,
        up,
        *table_places(),
        *up_places(ix, share),
    )


def dot(operand_a, operand_b):
    return jnp.dot(operand_a, operand_b, preferred_element_type=FULL)


def outer_sum(operand_a, operand_b):
    return jnp.einsum("ti,tj->ij", operand_a, operand_b, preferred_element_type=FULL).astype(LOW)


def dot_turned(operand_a, operand_b):
    return jnp.einsum("ti,ji->tj", operand_a, operand_b, preferred_element_type=FULL)


def body(
    tokens,
    cotangent,
    starts,
    w_qkv,
    m_qkv,
    v_qkv,
    w_out,
    m_out,
    v_out,
    w_up,
    m_up,
    v_up,
    w_down,
    m_down,
    v_down,
    vectors,
    m_vec,
    v_vec,
):
    ix = Index()
    rows = D // ix.count
    share = FF // ix.count
    tok_rows = tokens.shape[0]
    reach_count = (SEQ_MOST + tok_rows - 2) // tok_rows
    assert reach_count == 4
    chip_rows = 2 * tok_rows
    near_rows = (reach_count + 2) * tok_rows
    wide = SIDE * PAIR
    columns = 3 * wide
    out_wide, up_wide = D // 2, FF // 2

    early = 3 * PAIR * (SIDE - 1)
    late = columns - early
    first_spots = [[(0, early, 0, 0)], [(0, late + 128, 0, 0)]]
    cut = (out_wide + up_wide) // 256 * 128
    second_spots = [
        [(0, out_wide, 0, 0), (out_wide, cut - out_wide, 1, 0)],
        [(0, out_wide + up_wide - cut, 1, cut - out_wide)],
    ]
    third_spots = [[(0, D // 2, 0, 0)], [(0, D // 2, 0, D // 2)]]
    orders = ix.orders
    vec_piece = jnp.pad(vectors.astype(LOW).reshape(rows, VCOLS), ((0, 0), (0, 128 - VCOLS)))
    qkv_mine, qkv_others = by_core(ix, *paired_columns(w_qkv.astype(LOW).reshape(rows, 3 * D)))
    mine = jnp.concatenate([qkv_mine, vec_piece], axis=1)
    others = jnp.concatenate([qkv_others, vec_piece], axis=1)
    first = jnp.concatenate(by_core(ix, mine, flipped(others, 1)), axis=0)
    first = gather_top(ix, first)
    mine = jnp.stack([shifted(tokens, 4), shifted(tokens, 2), tokens])
    first, mine, w_out, w_up = tied(first, mine, w_out, w_up)

    first = gather_mid((first[..., :early], first[..., early:]), orders)
    up_sides = hidden_columns(w_up.astype(LOW).reshape(rows, FF), share)
    out_low = w_out.astype(LOW).reshape(rows, D)
    pieces = [
        jnp.concatenate([out_low[:, s * out_wide : (s + 1) * out_wide], up_sides[s]], axis=1)
        for s in range(2)
    ]
    near_tokens = jnp.stack(by_core(ix, mine, flipped(mine, 1)), axis=1).reshape(near_rows, D)
    own_piece, others = by_core(ix, *pieces)
    second = jnp.concatenate(by_core(ix, own_piece, flipped(others, 1)), axis=0)
    *first, second, starts, near_tokens = tied(*first, second, starts, near_tokens)
    first = gather_last(first, orders)
    second = gather_top(ix, second)
    chip_starts = jnp.concatenate(by_core(ix, starts, flipped(starts, 1)))
    first, near_tokens, chip_starts, cotangent, w_down = tied(
        first, near_tokens, chip_starts, cotangent, w_down
    )
    early_w = assemble(ix, first[:1], orders[:1], first_spots[:1], [early])[0]
    late_w = assemble(ix, first[1:], orders[1:], first_spots[1:], [late + 128])[0]
    vec_table, up_bias = read_vec(ix, late_w[:, late:], share)
    late_w = late_w[:, :late]
    third = w_down.astype(LOW).reshape(4 * rows, D)
    gain_one, shift_one, bias_q, bias_v, bias_o, gain_two, shift_two, bias_down = (
        vec_table[i] for i in range(8)
    )
    bias_q = lax.dynamic_slice_in_dim(bias_q, ix.core * wide, wide)
    bias_v = lax.dynamic_slice_in_dim(bias_v, ix.core * wide, wide)

    near_unit, near_inverse = norm_parts(near_tokens.astype(FULL))
    near_normed = (near_unit * gain_one + shift_one).astype(LOW)
    near_normed, second, third, cotangent = tied(near_normed, second, third, cotangent)
    third = gather_top(ix, third)
    second = gather_mid(cut_at(second, cut), orders)
    chip_cotangent = jnp.concatenate(by_core(ix, cotangent, flipped(cotangent, 1)), axis=0)
    bias = jnp.stack(
        [bias_q.reshape(SIDE, PAIR), jnp.zeros((SIDE, PAIR), FULL), bias_v.reshape(SIDE, PAIR)],
        axis=1,
    ).reshape(columns)
    first_key = (chip_starts - ((ix.me >> 1) * chip_rows - reach_count * tok_rows))[:, None]
    early_qkv = (dot(near_normed, early_w) + bias[:early]).astype(LOW)
    late_qkv = (dot(near_normed, late_w) + bias[early:]).astype(LOW)
    early_qkv, late_qkv, second = tied(early_qkv, late_qkv, second)
    second = gather_last(second, orders)
    mixed, weights = [None, None], [None, None]
    mixed[0], weights[0] = attend(first_key, late_qkv, tok_rows, 0, 1)
    mixed[0], early_qkv, third = tied(mixed[0], early_qkv, third)
    third = gather_mid(cut_at(third, D // 2), orders)
    mixed[1], weights[1] = attend(first_key, early_qkv, tok_rows, 0, SIDE - 1)
    mixed = jnp.concatenate([mixed[1], mixed[0]], axis=1)
    mixed, second, third = tied(mixed, second, third)
    third = gather_last(third, orders)
    attended = jnp.concatenate(by_core(ix, mixed, flipped(mixed, 1)), axis=1)
    out_half, up_w = assemble(ix, second, orders, second_spots, [out_wide, up_wide])
    out_w = jnp.concatenate(by_core(ix, out_half, flipped(out_half, 1)), axis=1)
    inputs = near_tokens[near_rows - chip_rows :].astype(FULL)
    middle = inputs + (dot(attended, out_w) + bias_o)
    unit_two, inverse_two = norm_parts(middle)
    normed_two = (unit_two * gain_two + shift_two).astype(LOW)
    hidden_pre = dot(normed_two, up_w) + up_bias
    hidden_low = smooth_act(hidden_pre).astype(LOW)
    grad_downw = outer_sum(hidden_low, chip_cotangent)
    hidden_low, hidden_pre, grad_downw = tied(hidden_low, hidden_pre, grad_downw)
    sum_down = scatter_mid(take_apart(ix, [grad_downw], orders, third_spots), orders, 0, 1)
    down_w = assemble(ix, third, orders, third_spots, [D])[0]
    result = dot(hidden_low, down_w).reshape(2, tok_rows, D)
    own_result, other_result = by_core(ix, result[0], result[1])
    own_result = own_result + flipped(other_result.astype(LOW), 1).astype(FULL)
    own_middle = lax.dynamic_slice_in_dim(middle, ix.core * tok_rows, tok_rows, 0)
    out_tokens = (own_middle + (own_result + bias_down)).astype(LOW)

    grad_hidden = dot_turned(chip_cotangent, down_w)
    act_value, act_back = jax.vjp(smooth_act, hidden_pre)
    grad_pre = act_back(grad_hidden)[0].astype(LOW)
    partial_two = dot_turned(grad_pre, up_w)
    grad_gain_two = jnp.sum(partial_two * unit_two, axis=0)
    grad_shift_two = jnp.sum(partial_two, axis=0)
    grad_normed_two = partial_two + flipped(partial_two.astype(LOW), 1).astype(FULL)
    grad_normed_two, grad_pre, sum_down = tied(grad_normed_two, grad_pre, sum_down)
    sum_down = scatter_mid(sum_down, orders, 1, 9)
    grad_upw = outer_sum(normed_two, grad_pre)
    grad_middle = chip_cotangent.astype(FULL) + norm_back(
        grad_normed_two, unit_two, inverse_two, gain_two
    )
    grad_branch = grad_middle.astype(LOW)
    own_part = lax.dynamic_slice_in_dim(grad_branch, ix.core * out_wide, out_wide, 1)
    grad_outw = outer_sum(attended, own_part)
    own_out = lax.dynamic_slice_in_dim(out_w, ix.core * wide, wide, 0)
    grad_mixed = dot_turned(grad_branch, own_out).astype(LOW)
    grad_mixed, grad_outw, grad_upw, sum_down = tied(grad_mixed, grad_outw, grad_upw, sum_down)
    sum_second = take_apart(ix, [grad_outw, grad_upw], orders, second_spots)
    grad_mixed, sum_second = tied(grad_mixed, sum_second)
    sum_second = scatter_mid(sum_second, orders, 0, 1)
    early_back = attend_back(weights[1], grad_mixed, early_qkv, tok_rows, 0, SIDE - 1)
    sum_early = take_apart(ix, [outer_sum(near_normed, early_back)], orders[:1], first_spots[:1])
    sum_down = scatter_top(ix, sum_down)
    early_back, grad_mixed, sum_early, sum_second = tied(
        early_back, grad_mixed, sum_early, sum_second
    )
    sum_early = scatter_mid(sum_early, orders[:1], 0, 1)
    sum_second = scatter_mid(sum_second, orders, 1, 9)
    late_back = attend_back(weights[0], grad_mixed, late_qkv, tok_rows, SIDE - 1, 1)
    late_spots = [[(0, late, 0, 0)]]
    sum_late = take_apart(ix, [outer_sum(near_normed, late_back)], orders[1:], late_spots)
    sums_two = (
        grad_gain_two,
        grad_shift_two,
        jnp.sum(grad_branch.astype(FULL), axis=0),
        jnp.sum(cotangent.astype(FULL), axis=0),
        jnp.sum(grad_pre.astype(FULL), axis=0),
    )
    late_back, sum_late, sum_down, sums_two = tied(late_back, sum_late, sum_down, sums_two)
    grad_gain_two, grad_shift_two, grad_bias_o, grad_bias_down, grad_bias_up = sums_two
    sum_late = scatter_mid(sum_late, orders[1:], 0, 1)

    grad_near = (dot_turned(early_back, early_w) + dot_turned(late_back, late_w)).astype(LOW)
    grad_gain_one = jnp.sum(grad_near.astype(FULL) * near_unit, axis=0)
    grad_shift_one = jnp.sum(grad_near.astype(FULL), axis=0)
    grad_bias = jnp.concatenate(
        [jnp.sum(early_back.astype(FULL), axis=0), jnp.sum(late_back.astype(FULL), axis=0)]
    )
    blank = jnp.zeros((D,), FULL)
    grad_table = jnp.stack(
        [
            grad_gain_one,
            grad_shift_one,
            blank,
            blank,
            0.5 * grad_bias_o,
            grad_gain_two,
            grad_shift_two,
            grad_bias_down,
        ]
    )
    grad_vec = write_vec(ix, grad_table, grad_bias[None], grad_bias_up[None], share)
    blocks = grad_near.reshape(reach_count // 2 + 1, 2, tok_rows, D)
    own_blocks, other_blocks = by_core(ix, blocks[:, 0], blocks[:, 1])
    mate_blocks = flipped(other_blocks, 1)
    grad_vec, sum_early, sum_late, sum_second, mate_blocks = tied(
        grad_vec, sum_early, sum_late, sum_second, mate_blocks
    )
    sum_early = scatter_mid(sum_early, orders[:1], 1, 9)
    sum_late = scatter_mid(sum_late, orders[1:], 1, 9)
    sum_second = scatter_top(ix, sum_second)
    vec_spots = [[(0, 128, 0, 0)]]
    sum_vec = scatter_mid(take_apart(ix, [grad_vec], orders[:1], vec_spots), orders[:1], 0, 9)

    own_blocks = own_blocks.astype(FULL) + mate_blocks.astype(FULL)
    four_back, two_back = own_blocks[0].astype(LOW), own_blocks[1].astype(LOW)
    sum_early, sum_late, sum_vec = tied(sum_early, sum_late, sum_vec)
    sum_first = scatter_top(ix, sum_early + sum_late + sum_vec)
    sum_first, sum_second = tied(sum_first, sum_second)
    own = (
        own_blocks[2]
        + shifted(two_back, -2).astype(FULL)
        + shifted(four_back, -4).astype(FULL)
    )
    unit_one, inverse_one = norm_parts(tokens.astype(FULL))
    own_grad_middle = lax.dynamic_slice_in_dim(grad_middle, ix.core * tok_rows, tok_rows, 0)
    input_grad = own_grad_middle + norm_back(own, unit_one, inverse_one, gain_one)

    keep_second, other_second = own_rows(ix, sum_second)
    keep_first, other_first = own_rows(ix, sum_first)
    g_vec = (keep_first[:, columns:] + other_first[:, columns:])[:, :VCOLS].reshape(-1)
    g_qkv = plain_columns(by_core(ix, keep_first[:, :columns], other_first[:, :columns]))
    g_out = jnp.concatenate(
        by_core(ix, keep_second[:, :out_wide], other_second[:, :out_wide]), axis=1
    )
    g_up = plain_hidden(by_core(ix, keep_second[:, out_wide:], other_second[:, out_wide:]), share)

    rate_qkv, rate_out, rate_up, rate_down = matrix_rates()
    entries = ix.me * vectors.shape[0] + jnp.arange(vectors.shape[0], dtype=jnp.int32)
    qkv_new = adamw(w_qkv, m_qkv, v_qkv, g_qkv.reshape(-1), rate_qkv, DECAY_RATE)
    out_new = adamw(w_out, m_out, v_out, g_out.reshape(-1), rate_out, DECAY_RATE)
    up_new = adamw(w_up, m_up, v_up, g_up.reshape(-1), rate_up, DECAY_RATE)
    down_new = adamw(w_down, m_down, v_down, sum_down.reshape(-1), rate_down, DECAY_RATE)
    vec_new = adamw(vectors, m_vec, v_vec, g_vec, vector_rates(entries), 0.0)
    return (out_tokens, input_grad) + qkv_new + out_new + up_new + down_new + vec_new


def solution(mesh):
    in_specs = (P("dev", None), P("dev", None)) + (P("dev"),) * 16
    out_specs = (P("dev", None), P("dev", None)) + (P("dev"),) * 15
    return jax.shard_map(body, mesh=mesh, in_specs=in_specs, out_specs=out_specs, check_vma=False)
```

```python
import jax
import jax.numpy as jnp
import numpy as np
from jax import lax
from jax.experimental import pallas as pl
from jax.experimental.pallas import tpu as pltpu
from jax.sharding import PartitionSpec as P

D = 768
HEAD_DIM = 64
HEADS = D // HEAD_DIM
FF = 3072
SEQ_MOST = 1024
STEP = 10
VCOLS = 12


NORM_EPS = 1e-05
BETA_ONE = 0.9
BETA_TWO = 0.999
ADAM_EPS = 1e-08
DECAY_RATE = 0.01
NEG_LARGE = -1e30

LOW = jnp.bfloat16
FULL = jnp.float32


def norm_parts(values):
    centre = jnp.mean(values, axis=-1, keepdims=True)
    centred = values - centre
    spread = jnp.mean(centred * centred, axis=-1, keepdims=True)
    inverse = lax.rsqrt(spread + NORM_EPS)
    return centred * inverse, inverse


def norm_back(grad, unit, inverse, gain_vec):
    scaled = grad * gain_vec
    along = jnp.mean(scaled * unit, axis=-1, keepdims=True)
    return inverse * (scaled - jnp.mean(scaled, axis=-1, keepdims=True) - unit * along)


def smooth_act(values):
    return jax.nn.gelu(values, approximate=True)


def adamw(weight, moment, second, gradient, step_rate, decay_rate):
    moment = BETA_ONE * moment + (1.0 - BETA_ONE) * gradient
    second = BETA_TWO * second + (1.0 - BETA_TWO) * gradient * gradient
    first_hat = moment / (1.0 - BETA_ONE**STEP)
    second_hat = second / (1.0 - BETA_TWO**STEP)
    weight = weight - step_rate * (
        first_hat / (jnp.sqrt(second_hat) + ADAM_EPS) + decay_rate * weight
    )
    return (moment, second, weight)


def matrix_rates():
    return (
        2.5 * D ** (-0.5),
        2.5 * max(1, D * 16 // SEQ_MOST) ** (-0.5),
        2.5 * D ** (-0.5),
        2.5 * FF ** (-0.5),
    )


def vector_rates(entries):
    column = entries % 8
    is_gain = (entries < 8 * D) & ((column == 0) | (column == 5))
    return jnp.where(is_gain, 0.3, 0.05).astype(jnp.float32)


def shifted(x, by):
    length = lax.axis_size("dev")
    return lax.ppermute(x, "dev", [(i, i + by) for i in range(length) if 0 <= i + by < length])


def flipped(x, mask):
    return lax.ppermute(x, "dev", [(i, i ^ mask) for i in range(lax.axis_size("dev"))])


def tied(*arrays):
    return lax.optimization_barrier(arrays)


class Index:
    def __init__(self):
        self.count = lax.axis_size("dev")
        self.me = lax.axis_index("dev")
        self.top = self.count.bit_length() - 3
        self.core = self.me & 1
        self.odd = self.core == 1
        middle = tuple(range(1, self.top))
        self.orders = (middle, tuple(reversed(middle)))

    def relative(self, order):
        seen = [r << self.top for r in range(4)]
        for b in reversed(order):
            seen = seen + [s | 1 << b for s in seen]
        return [s >> 1 for s in seen]


def by_core(ix, own, other):
    return jnp.where(ix.odd, other, own), jnp.where(ix.odd, own, other)


def cut_at(x, column):
    return (x[..., :column], x[..., column:])


def gather_top(ix, piece):
    return jnp.stack([piece] + [flipped(piece, r << ix.top) for r in (1, 2, 3)])


def gather_mid(sides, orders):
    done = []
    for x, order in zip(sides, orders):
        for b in reversed(order[1:]):
            x = jnp.concatenate([x, flipped(x, 1 << b)], axis=0)
        done.append(x)
    return done


def gather_last(sides, orders):
    return [(x, flipped(x, 1 << order[0])) for x, order in zip(sides, orders)]


def place_kernel(rows, count, moves, inward, chip_ref, *refs):
    ins, outs = refs[:count], refs[count:]
    chip = chip_ref[0]
    for part, at, column, whole, relative, whole_column, width in moves:
        start = pl.multiple_of((chip ^ relative) * rows, rows)
        spot = (pl.ds(start, rows), pl.ds(whole_column, width))
        if inward:
            outs[whole][spot] = ins[part][at, :, column : column + width]
        else:
            outs[part][at, :, column : column + width] = ins[whole][spot]


def place(ix, rows, ins, moves, inward, out_shape):
    return pl.pallas_call(
        lambda *refs: place_kernel(rows, len(ins), moves, inward, *refs),
        in_specs=[pl.BlockSpec(memory_space=pltpu.SMEM)]
        + [pl.BlockSpec(memory_space=pltpu.VMEM)] * len(ins),
        out_specs=[pl.BlockSpec(memory_space=pltpu.VMEM)] * len(out_shape),
        out_shape=[jax.ShapeDtypeStruct(shape, LOW) for shape in out_shape],
        compiler_params=pltpu.CompilerParams(
            vmem_limit_bytes=4 * sum(rows * move[-1] for move in moves) + 2**21
        ),
    )((ix.me >> 1).astype(jnp.int32).reshape(1), *ins)


def place_moves(ix, orders, spots):
    moves = []
    for s, order in enumerate(orders):
        for spot, relative in enumerate(ix.relative(order)):
            half, at = divmod(spot, ix.count // 4)
            for column, width, whole, whole_column in spots[s]:
                moves.append((2 * s + half, at, column, whole, relative, whole_column, width))
    return moves


def assemble(ix, sides, orders, spots, widths):
    chips = ix.count // 2
    rows = sides[0][0].shape[1]
    if rows % 16:
        parts = [{} for _ in widths]
        for side, order, spot in zip(sides, orders, spots):
            seen = ix.relative(order)
            place_of = jnp.array([seen.index(r) for r in range(chips)], jnp.int32)
            pick = place_of[(ix.me >> 1) ^ jnp.arange(chips)]
            full = jnp.take(jnp.concatenate(side, axis=0), pick, axis=0)
            full = full.reshape(chips * rows, -1)
            for column, width, whole, whole_column in spot:
                parts[whole][whole_column] = full[:, column : column + width]
        return [jnp.concatenate([p[c] for c in sorted(p)], axis=1) for p in parts]
    ins = [array for side in sides for array in side]
    shapes = [(chips * rows, width) for width in widths]
    return place(ix, rows, ins, place_moves(ix, orders, spots), True, shapes)


def take_apart(ix, wholes, orders, spots):
    chips = ix.count // 2
    rows = wholes[0].shape[0] // chips
    widths = [sum(spot[1] for spot in side) for side in spots]
    if rows % 16:
        sides = []
        for order, spot in zip(orders, spots):
            side = jnp.concatenate([wholes[w][:, c : c + n] for _, n, w, c in spot], axis=1)
            pick = (ix.me >> 1) ^ jnp.array(ix.relative(order), jnp.int32)
            full = jnp.take(side.reshape(chips, rows, -1), pick, axis=0)
            sides.append((full[: chips // 2], full[chips // 2 :]))
        return sides
    shapes = [(chips // 2, rows, width) for width in widths for _ in range(2)]
    outs = place(ix, rows, wholes, place_moves(ix, orders, spots), False, shapes)
    return [(outs[2 * s], outs[2 * s + 1]) for s in range(len(spots))]


def settle(keep, other, parts):
    size = keep.shape[0] // parts
    return [
        (
            keep[i * size : (i + 1) * size].astype(FULL)
            + other[i * size : (i + 1) * size].astype(FULL)
        ).astype(LOW)
        for i in range(parts)
    ]


def scatter_mid(sides, orders, first, last):
    done = []
    for (keep, send), order in zip(sides, orders):
        for i in range(first, min(last, len(order))):
            parts = 2 if i < len(order) - 1 else 4
            settled = settle(keep, flipped(send, 1 << order[i]), parts)
            keep, send = settled[0], settled[1] if parts == 2 else settled[1:]
        done.append((keep, send))
    return done


def scatter_top(ix, sides):
    total = jnp.concatenate([keep[0] for keep, _ in sides], axis=-1).astype(FULL)
    for r in (1, 2, 3):
        part = jnp.concatenate([send[r - 1][0] for _, send in sides], axis=-1)
        total = total + flipped(part, r << ix.top).astype(FULL)
    return total


def own_rows(ix, summed):
    rows = summed.shape[0] // 2
    keep = lax.dynamic_slice_in_dim(summed, ix.core * rows, rows, 0)
    other = lax.dynamic_slice_in_dim(summed, (1 - ix.core) * rows, rows, 0)
    return keep, flipped(other, 1)


PAIR = 2 * HEAD_DIM
PAIRS = HEADS // 2
SIDE = PAIRS // 2
SCALE = HEAD_DIM ** (-0.5)
VMEM_BYTES = 20 * 1024 * 1024


def by_head(pair):
    low_half = lax.broadcasted_iota(jnp.int32, pair.shape, 1) < HEAD_DIM
    zero = jnp.zeros_like(pair)
    return (
        low_half,
        jnp.where(low_half, pair, zero).astype(LOW),
        jnp.where(low_half, zero, pair).astype(LOW),
    )


def dot_over(operand_a, operand_b, dim_a, dim_b):
    return lax.dot_general(
        operand_a, operand_b, (((dim_a,), (dim_b,)), ((), ())), preferred_element_type=FULL
    )


def attend_kernel(first_ref, qkv_ref, out_ref, weights_ref):
    rows, near = weights_ref.shape[-2:]
    before = near - rows
    key = lax.broadcasted_iota(jnp.int32, (rows, near), 1)
    last = lax.broadcasted_iota(jnp.int32, (rows, near), 0) + (near - rows)
    for block in range(2):
        own, seen = pl.ds(block * rows, rows), pl.ds(block * rows, near)
        query = qkv_ref[pl.ds(before + block * rows, rows), :PAIR]
        low_half, *q_heads = by_head(query.astype(FULL) * SCALE)
        k, v = qkv_ref[seen, PAIR : 2 * PAIR], qkv_ref[seen, 2 * PAIR :]
        allowed = (key >= first_ref[own, :] - block * rows) & (key <= last)
        blended = []
        for head in range(2):
            scores = jnp.where(allowed, dot_over(q_heads[head], k, 1, 1), NEG_LARGE)
            weights = jnp.exp(scores - jnp.max(scores, axis=-1, keepdims=True))
            weights = weights * (1.0 / jnp.sum(weights, axis=-1, keepdims=True))
            weights = weights.astype(LOW)
            weights_ref[0, 2 * block + head] = weights
            blended.append(dot_over(weights, v, 1, 0))
        out_ref[own, :] = jnp.where(low_half, blended[0], blended[1]).astype(LOW)


def attend(first_key, qkv, rows, first, pairs):
    window = qkv.shape[0]
    near = window - rows
    return pl.pallas_call(
        attend_kernel,
        grid=(pairs,),
        in_specs=[
            pl.BlockSpec((2 * rows, 1), lambda i: (0, 0)),
            pl.BlockSpec((window, 3 * PAIR), lambda i: (0, i + first)),
        ],
        out_specs=[
            pl.BlockSpec((2 * rows, PAIR), lambda i: (0, i)),
            pl.BlockSpec((1, 4, rows, near), lambda i: (i, 0, 0, 0)),
        ],
        out_shape=[
            jax.ShapeDtypeStruct((2 * rows, pairs * PAIR), LOW),
            jax.ShapeDtypeStruct((pairs, 4, rows, near), LOW),
        ],
        compiler_params=pltpu.CompilerParams(vmem_limit_bytes=VMEM_BYTES),
    )(first_key, qkv)


def attend_back_kernel(weights_ref, grad_ref, qkv_ref, out_ref):
    rows, near = weights_ref.shape[-2:]
    before = near - rows
    out_ref[:before, :PAIR] = jnp.zeros((before, PAIR), LOW)
    turned = []
    for block in range(2):
        own, seen = pl.ds(block * rows, rows), pl.ds(block * rows, near)
        low_half, *grad_heads = by_head(grad_ref[own, :].astype(FULL))
        asking = pl.ds(before + block * rows, rows)
        _, *q_heads = by_head(qkv_ref[asking, :PAIR].astype(FULL))
        k, v = qkv_ref[seen, PAIR : 2 * PAIR], qkv_ref[seen, 2 * PAIR :]
        dq = []
        dk_turned = dv_turned = 0.0
        for head in range(2):
            weights_low = weights_ref[0, 2 * block + head]
            weights = weights_low.astype(FULL)
            grad_weights = dot_over(grad_heads[head], v, 1, 1)
            inner_sum = jnp.sum(weights * grad_weights, axis=-1, keepdims=True)
            grad_scores = (weights * (grad_weights - inner_sum)).astype(LOW)
            dq.append(dot_over(grad_scores, k, 1, 0))
            dk_turned += dot_over(q_heads[head], grad_scores, 0, 0)
            dv_turned += dot_over(grad_heads[head], weights_low, 0, 0)
        out_ref[asking, :PAIR] = (jnp.where(low_half, dq[0], dq[1]) * SCALE).astype(LOW)
        turned.append((dk_turned * SCALE, dv_turned))
    for which in range(2):
        early, late = turned[0][which], turned[1][which]
        whole = jnp.concatenate(
            [early[:, :rows], early[:, rows:] + late[:, : near - rows], late[:, near - rows :]],
            axis=1,
        )
        out_ref[:, (which + 1) * PAIR : (which + 2) * PAIR] = whole.T.astype(LOW)


def attend_back(weights, grad, qkv, rows, first, pairs):
    window = qkv.shape[0]
    near = window - rows
    return pl.pallas_call(
        attend_back_kernel,
        grid=(pairs,),
        in_specs=[
            pl.BlockSpec((1, 4, rows, near), lambda i: (i, 0, 0, 0)),
            pl.BlockSpec((2 * rows, PAIR), lambda i: (0, i + first)),
            pl.BlockSpec((window, 3 * PAIR), lambda i: (0, i)),
        ],
        out_specs=pl.BlockSpec((window, 3 * PAIR), lambda i: (0, i)),
        out_shape=jax.ShapeDtypeStruct((window, 3 * pairs * PAIR), LOW),
        compiler_params=pltpu.CompilerParams(vmem_limit_bytes=VMEM_BYTES),
    )(weights, grad, qkv)


def paired_columns(x):
    rows = x.shape[0]
    parts = x.reshape(rows, 3, 2, SIDE, PAIR).transpose(2, 0, 3, 1, 4)
    return parts.reshape(2, rows, 3 * SIDE * PAIR)


def plain_columns(sides):
    rows = sides[0].shape[0]
    parts = [side.reshape(rows, SIDE, 3, PAIR).transpose(0, 2, 1, 3) for side in sides]
    return jnp.stack(parts, axis=2).reshape(rows, 3 * D)


def hidden_columns(x, share):
    parts = x.reshape(x.shape[0], FF // (2 * share), 2, share)
    return [parts[:, :, s].reshape(x.shape[0], FF // 2) for s in range(2)]


def plain_hidden(sides, share):
    rows = sides[0].shape[0]
    parts = [side.reshape(rows, FF // (2 * share), 1, share) for side in sides]
    return jnp.concatenate(parts, axis=2).reshape(rows, FF)


TABLE_ROWS = 8 * D // VCOLS


def table_places():
    feature = np.arange(D)[None]
    entry = 8 * (feature % 3) + np.arange(8)[:, None]
    first_row = 2 * (feature // 3)
    return (
        jnp.asarray(first_row, jnp.int32),
        jnp.asarray(entry // VCOLS, jnp.int32),
        jnp.asarray(entry % VCOLS, jnp.int32),
    )


def up_places(ix, share):
    unit = np.arange(FF // 2)[None]
    row = 2 * (unit // share) * (share // VCOLS) + unit % share // VCOLS
    return (
        jnp.asarray(row, jnp.int32) + ix.core * (share // VCOLS),
        jnp.asarray(unit % VCOLS, jnp.int32),
    )


def one_at(row, rows):
    at = lax.broadcasted_iota(jnp.int32, (rows, row.shape[1]), 0)
    return jnp.where(at == row, 1.0, 0.0).astype(LOW)


def in_column(column):
    return lax.broadcasted_iota(jnp.int32, (16, column.shape[1]), 0) == column


def read_vec_kernel(vec_ref, first_ref, step_ref, column_ref, row_ref, spot_ref, table_ref, up_ref):
    vec = vec_ref[...]
    table = vec[:TABLE_ROWS]
    moved = [dot_over(table, one_at(first_ref[...] + d, TABLE_ROWS), 0, 0)[:16] for d in range(2)]
    for c in range(8):
        step = step_ref[c : c + 1, :]
        picked = jnp.where(step == 0, moved[0], moved[1])
        picked = jnp.where(in_column(column_ref[c : c + 1, :]), picked, 0.0)
        table_ref[c : c + 1, :] = jnp.sum(picked, axis=0, keepdims=True)
    rest = vec[TABLE_ROWS:]
    moved = dot_over(rest, one_at(row_ref[...], rest.shape[0]), 0, 0)[:16]
    picked = jnp.where(in_column(spot_ref[...]), moved, 0.0)
    up_ref[...] = jnp.sum(picked, axis=0, keepdims=True)


def read_vec(ix, vec, share):
    return pl.pallas_call(
        read_vec_kernel,
        out_shape=[
            jax.ShapeDtypeStruct((8, D), FULL),
            jax.ShapeDtypeStruct((1, FF // 2), FULL),
        ],
        compiler_params=pltpu.CompilerParams(vmem_limit_bytes=VMEM_BYTES),
    )(vec, *table_places(), *up_places(ix, share))


def write_vec_kernel(
    core_ref, table_ref, bias_ref, up_ref, first_ref, step_ref, column_ref, row_ref, spot_ref, out_ref
):
    core = core_ref[0]
    wide = SIDE * PAIR
    moved = [jnp.zeros((16, D), FULL) for _ in range(2)]
    for c in range(8):
        row = table_ref[c : c + 1, :]
        if c in (2, 3):
            part = 0 if c == 2 else 2
            half = jnp.concatenate(
                [
                    bias_ref[:, (3 * i + part) * PAIR : (3 * i + part + 1) * PAIR]
                    for i in range(SIDE)
                ],
                axis=1,
            )
            lane = lax.broadcasted_iota(jnp.int32, (1, D), 1)
            own = (lane >= core * wide) & (lane < (core + 1) * wide)
            row = jnp.where(own, jnp.concatenate([half, half], axis=1), 0.0)
        step = step_ref[c : c + 1, :]
        here = in_column(column_ref[c : c + 1, :])
        for d in range(2):
            moved[d] = moved[d] + jnp.where(here & (step == d), row, 0.0)
    blank = jnp.zeros((112, D), LOW)
    total = 0.0
    for d in range(2):
        wanted = jnp.concatenate([moved[d].astype(LOW), blank], axis=0)
        total = total + dot_over(one_at(first_ref[...] + d, TABLE_ROWS), wanted, 1, 1)
    out_ref[:TABLE_ROWS, :] = total.astype(LOW)
    rest = out_ref.shape[0] - TABLE_ROWS
    wanted = jnp.where(in_column(spot_ref[...]), up_ref[...], 0.0).astype(LOW)
    wanted = jnp.concatenate([wanted, jnp.zeros((112, wanted.shape[1]), LOW)], axis=0)
    out_ref[TABLE_ROWS:, :] = dot_over(one_at(row_ref[...], rest), wanted, 1, 1).astype(LOW)


def write_vec(ix, table, bias, up, share):
    whole = pl.BlockSpec(memory_space=pltpu.VMEM)
    return pl.pallas_call(
        write_vec_kernel,
        in_specs=[pl.BlockSpec(memory_space=pltpu.SMEM)] + [whole] * 8,
        out_specs=whole,
        out_shape=jax.ShapeDtypeStruct((D, 128), LOW),
        compiler_params=pltpu.CompilerParams(vmem_limit_bytes=VMEM_BYTES),
    )(
        ix.core.astype(jnp.int32).reshape(1),
        table,
        bias,
        up,
        *table_places(),
        *up_places(ix, share),
    )


def dot(operand_a, operand_b):
    return jnp.dot(operand_a, operand_b, preferred_element_type=FULL)


def outer_sum(operand_a, operand_b):
    return jnp.einsum("ti,tj->ij", operand_a, operand_b, preferred_element_type=FULL).astype(LOW)


def dot_turned(operand_a, operand_b):
    return jnp.einsum("ti,ji->tj", operand_a, operand_b, preferred_element_type=FULL)


def body(
    tokens,
    cotangent,
    starts,
    w_qkv,
    m_qkv,
    v_qkv,
    w_out,
    m_out,
    v_out,
    w_up,
    m_up,
    v_up,
    w_down,
    m_down,
    v_down,
    vectors,
    m_vec,
    v_vec,
):
    ix = Index()
    rows = D // ix.count
    share = FF // ix.count
    tok_rows = tokens.shape[0]
    reach_count = (SEQ_MOST + tok_rows - 2) // tok_rows
    assert reach_count == 4
    chip_rows = 2 * tok_rows
    near_rows = (reach_count + 2) * tok_rows
    wide = SIDE * PAIR
    columns = 3 * wide
    out_wide, up_wide = D // 2, FF // 2

    early = 3 * PAIR * (SIDE - 1)
    late = columns - early
    first_spots = [[(0, early, 0, 0)], [(0, late + 128, 0, 0)]]
    cut = (out_wide + up_wide) // 256 * 128
    second_spots = [
        [(0, out_wide, 0, 0), (out_wide, cut - out_wide, 1, 0)],
        [(0, out_wide + up_wide - cut, 1, cut - out_wide)],
    ]
    third_spots = [[(0, D // 2, 0, 0)], [(0, D // 2, 0, D // 2)]]
    orders = ix.orders
    vec_piece = jnp.pad(vectors.astype(LOW).reshape(rows, VCOLS), ((0, 0), (0, 128 - VCOLS)))
    qkv_mine, qkv_others = by_core(ix, *paired_columns(w_qkv.astype(LOW).reshape(rows, 3 * D)))
    mine = jnp.concatenate([qkv_mine, vec_piece], axis=1)
    others = jnp.concatenate([qkv_others, vec_piece], axis=1)
    first = jnp.concatenate(by_core(ix, mine, flipped(others, 1)), axis=0)
    first = gather_top(ix, first)
    mine = jnp.stack([shifted(tokens, 4), shifted(tokens, 2), tokens])
    first, mine, w_out, w_up = tied(first, mine, w_out, w_up)

    first = gather_mid((first[..., :early], first[..., early:]), orders)
    up_sides = hidden_columns(w_up.astype(LOW).reshape(rows, FF), share)
    out_low = w_out.astype(LOW).reshape(rows, D)
    pieces = [
        jnp.concatenate([out_low[:, s * out_wide : (s + 1) * out_wide], up_sides[s]], axis=1)
        for s in range(2)
    ]
    near_tokens = jnp.stack(by_core(ix, mine, flipped(mine, 1)), axis=1).reshape(near_rows, D)
    own_piece, others = by_core(ix, *pieces)
    second = jnp.concatenate(by_core(ix, own_piece, flipped(others, 1)), axis=0)
    *first, second, starts, near_tokens = tied(*first, second, starts, near_tokens)
    first = gather_last(first, orders)
    second = gather_top(ix, second)
    chip_starts = jnp.concatenate(by_core(ix, starts, flipped(starts, 1)))
    first, second, near_tokens, chip_starts, cotangent, w_down = tied(
        first, second, near_tokens, chip_starts, cotangent, w_down
    )
    second = gather_mid(cut_at(second, cut), orders)
    early_w = assemble(ix, first[:1], orders[:1], first_spots[:1], [early])[0]
    late_w = assemble(ix, first[1:], orders[1:], first_spots[1:], [late + 128])[0]
    vec_table, up_bias = read_vec(ix, late_w[:, late:], share)
    late_w = late_w[:, :late]
    third = w_down.astype(LOW).reshape(4 * rows, D)
    gain_one, shift_one, bias_q, bias_v, bias_o, gain_two, shift_two, bias_down = (
        vec_table[i] for i in range(8)
    )
    bias_q = lax.dynamic_slice_in_dim(bias_q, ix.core * wide, wide)
    bias_v = lax.dynamic_slice_in_dim(bias_v, ix.core * wide, wide)

    near_unit, near_inverse = norm_parts(near_tokens.astype(FULL))
    near_normed = (near_unit * gain_one + shift_one).astype(LOW)
    near_normed, second, third, cotangent = tied(near_normed, second, third, cotangent)
    second = gather_last(second, orders)
    third = gather_top(ix, third)
    chip_cotangent = jnp.concatenate(by_core(ix, cotangent, flipped(cotangent, 1)), axis=0)
    bias = jnp.stack(
        [bias_q.reshape(SIDE, PAIR), jnp.zeros((SIDE, PAIR), FULL), bias_v.reshape(SIDE, PAIR)],
        axis=1,
    ).reshape(columns)
    first_key = (chip_starts - ((ix.me >> 1) * chip_rows - reach_count * tok_rows))[:, None]
    early_qkv = (dot(near_normed, early_w) + bias[:early]).astype(LOW)
    late_qkv = (dot(near_normed, late_w) + bias[early:]).astype(LOW)
    mixed, weights = [None, None], [None, None]
    mixed[0], weights[0] = attend(first_key, late_qkv, tok_rows, 0, 1)
    mixed[0], early_qkv, third = tied(mixed[0], early_qkv, third)
    third = gather_mid(cut_at(third, D // 2), orders)
    mixed[1], weights[1] = attend(first_key, early_qkv, tok_rows, 0, SIDE - 1)
    mixed = jnp.concatenate([mixed[1], mixed[0]], axis=1)
    mixed, second, third = tied(mixed, second, third)
    third = gather_last(third, orders)
    attended = jnp.concatenate(by_core(ix, mixed, flipped(mixed, 1)), axis=1)
    out_half, up_w = assemble(ix, second, orders, second_spots, [out_wide, up_wide])
    out_w = jnp.concatenate(by_core(ix, out_half, flipped(out_half, 1)), axis=1)
    inputs = near_tokens[near_rows - chip_rows :].astype(FULL)
    middle = inputs + (dot(attended, out_w) + bias_o)
    unit_two, inverse_two = norm_parts(middle)
    normed_two = (unit_two * gain_two + shift_two).astype(LOW)
    hidden_pre = dot(normed_two, up_w) + up_bias
    hidden_low = smooth_act(hidden_pre).astype(LOW)
    grad_downw = outer_sum(hidden_low, chip_cotangent)
    hidden_low, hidden_pre, grad_downw = tied(hidden_low, hidden_pre, grad_downw)
    sum_down = scatter_mid(take_apart(ix, [grad_downw], orders, third_spots), orders, 0, 1)
    down_w = assemble(ix, third, orders, third_spots, [D])[0]
    result = dot(hidden_low, down_w).reshape(2, tok_rows, D)
    own_result, other_result = by_core(ix, result[0], result[1])
    own_result = own_result + flipped(other_result.astype(LOW), 1).astype(FULL)
    own_middle = lax.dynamic_slice_in_dim(middle, ix.core * tok_rows, tok_rows, 0)
    out_tokens = (own_middle + (own_result + bias_down)).astype(LOW)

    grad_hidden = dot_turned(chip_cotangent, down_w)
    act_value, act_back = jax.vjp(smooth_act, hidden_pre)
    grad_pre = act_back(grad_hidden)[0].astype(LOW)
    partial_two = dot_turned(grad_pre, up_w)
    grad_gain_two = jnp.sum(partial_two * unit_two, axis=0)
    grad_shift_two = jnp.sum(partial_two, axis=0)
    grad_normed_two = partial_two + flipped(partial_two.astype(LOW), 1).astype(FULL)
    grad_normed_two, grad_pre, sum_down = tied(grad_normed_two, grad_pre, sum_down)
    sum_down = scatter_mid(sum_down, orders, 1, 9)
    grad_upw = outer_sum(normed_two, grad_pre)
    grad_middle = chip_cotangent.astype(FULL) + norm_back(
        grad_normed_two, unit_two, inverse_two, gain_two
    )
    grad_branch = grad_middle.astype(LOW)
    own_part = lax.dynamic_slice_in_dim(grad_branch, ix.core * out_wide, out_wide, 1)
    grad_outw = outer_sum(attended, own_part)
    own_out = lax.dynamic_slice_in_dim(out_w, ix.core * wide, wide, 0)
    grad_mixed = dot_turned(grad_branch, own_out).astype(LOW)
    grad_mixed, grad_outw, grad_upw, sum_down = tied(grad_mixed, grad_outw, grad_upw, sum_down)
    sum_second = take_apart(ix, [grad_outw, grad_upw], orders, second_spots)
    grad_mixed, sum_second = tied(grad_mixed, sum_second)
    sum_second = scatter_mid(sum_second, orders, 0, 1)
    early_back = attend_back(weights[1], grad_mixed, early_qkv, tok_rows, 0, SIDE - 1)
    sum_early = take_apart(ix, [outer_sum(near_normed, early_back)], orders[:1], first_spots[:1])
    sum_down = scatter_top(ix, sum_down)
    early_back, grad_mixed, sum_early, sum_second = tied(
        early_back, grad_mixed, sum_early, sum_second
    )
    sum_early = scatter_mid(sum_early, orders[:1], 0, 1)
    sum_second = scatter_mid(sum_second, orders, 1, 9)
    late_back = attend_back(weights[0], grad_mixed, late_qkv, tok_rows, SIDE - 1, 1)
    late_spots = [[(0, late, 0, 0)]]
    sum_late = take_apart(ix, [outer_sum(near_normed, late_back)], orders[1:], late_spots)
    sums_two = (
        grad_gain_two,
        grad_shift_two,
        jnp.sum(grad_branch.astype(FULL), axis=0),
        jnp.sum(cotangent.astype(FULL), axis=0),
        jnp.sum(grad_pre.astype(FULL), axis=0),
    )
    late_back, sum_late, sum_down, sum_second, sums_two = tied(
        late_back, sum_late, sum_down, sum_second, sums_two
    )
    sum_second = scatter_top(ix, sum_second)
    grad_gain_two, grad_shift_two, grad_bias_o, grad_bias_down, grad_bias_up = sums_two
    sum_late = scatter_mid(sum_late, orders[1:], 0, 1)

    grad_near = (dot_turned(early_back, early_w) + dot_turned(late_back, late_w)).astype(LOW)
    grad_gain_one = jnp.sum(grad_near.astype(FULL) * near_unit, axis=0)
    grad_shift_one = jnp.sum(grad_near.astype(FULL), axis=0)
    grad_gain_one, grad_shift_one, sum_early, sum_late = tied(
        grad_gain_one, grad_shift_one, sum_early, sum_late
    )
    sum_early = scatter_mid(sum_early, orders[:1], 1, 9)
    sum_late = scatter_mid(sum_late, orders[1:], 1, 9)
    grad_bias = jnp.concatenate(
        [jnp.sum(early_back.astype(FULL), axis=0), jnp.sum(late_back.astype(FULL), axis=0)]
    )
    blank = jnp.zeros((D,), FULL)
    grad_table = jnp.stack(
        [
            grad_gain_one,
            grad_shift_one,
            blank,
            blank,
            0.5 * grad_bias_o,
            grad_gain_two,
            grad_shift_two,
            grad_bias_down,
        ]
    )
    grad_vec = write_vec(ix, grad_table, grad_bias[None], grad_bias_up[None], share)
    blocks = grad_near.reshape(reach_count // 2 + 1, 2, tok_rows, D)
    own_blocks, other_blocks = by_core(ix, blocks[:, 0], blocks[:, 1])
    mate_blocks = flipped(other_blocks, 1)
    grad_vec, sum_second, mate_blocks = tied(grad_vec, sum_second, mate_blocks)
    vec_spots = [[(0, 128, 0, 0)]]
    sum_vec = scatter_mid(take_apart(ix, [grad_vec], orders[:1], vec_spots), orders[:1], 0, 9)

    own_blocks = own_blocks.astype(FULL) + mate_blocks.astype(FULL)
    four_back, two_back = own_blocks[0].astype(LOW), own_blocks[1].astype(LOW)
    sum_early, sum_late, sum_vec = tied(sum_early, sum_late, sum_vec)
    sum_first = scatter_top(ix, sum_early + sum_late + sum_vec)
    own = (
        own_blocks[2]
        + shifted(two_back, -2).astype(FULL)
        + shifted(four_back, -4).astype(FULL)
    )
    sum_first, sum_second, own = tied(sum_first, sum_second, own)
    unit_one, inverse_one = norm_parts(tokens.astype(FULL))
    own_grad_middle = lax.dynamic_slice_in_dim(grad_middle, ix.core * tok_rows, tok_rows, 0)
    input_grad = own_grad_middle + norm_back(own, unit_one, inverse_one, gain_one)

    keep_second, other_second = own_rows(ix, sum_second)
    keep_first, other_first = own_rows(ix, sum_first)
    g_vec = (keep_first[:, columns:] + other_first[:, columns:])[:, :VCOLS].reshape(-1)
    g_qkv = plain_columns(by_core(ix, keep_first[:, :columns], other_first[:, :columns]))
    g_out = jnp.concatenate(
        by_core(ix, keep_second[:, :out_wide], other_second[:, :out_wide]), axis=1
    )
    g_up = plain_hidden(by_core(ix, keep_second[:, out_wide:], other_second[:, out_wide:]), share)

    rate_qkv, rate_out, rate_up, rate_down = matrix_rates()
    entries = ix.me * vectors.shape[0] + jnp.arange(vectors.shape[0], dtype=jnp.int32)
    qkv_new = adamw(w_qkv, m_qkv, v_qkv, g_qkv.reshape(-1), rate_qkv, DECAY_RATE)
    out_new = adamw(w_out, m_out, v_out, g_out.reshape(-1), rate_out, DECAY_RATE)
    up_new = adamw(w_up, m_up, v_up, g_up.reshape(-1), rate_up, DECAY_RATE)
    down_new = adamw(w_down, m_down, v_down, sum_down.reshape(-1), rate_down, DECAY_RATE)
    vec_new = adamw(vectors, m_vec, v_vec, g_vec, vector_rates(entries), 0.0)
    return (out_tokens, input_grad) + qkv_new + out_new + up_new + down_new + vec_new


def solution(mesh):
    in_specs = (P("dev", None), P("dev", None)) + (P("dev"),) * 16
    out_specs = (P("dev", None), P("dev", None)) + (P("dev"),) * 15
    return jax.shard_map(body, mesh=mesh, in_specs=in_specs, out_specs=out_specs, check_vma=False)
```

```python
import jax
import jax.numpy as jnp
import numpy as np
from jax import lax
from jax.experimental import pallas as pl
from jax.experimental.pallas import tpu as pltpu
from jax.sharding import PartitionSpec as P

D = 768
HEAD_DIM = 64
HEADS = D // HEAD_DIM
FF = 3072
SEQ_MOST = 1024
STEP = 10
VCOLS = 12


NORM_EPS = 1e-05
BETA_ONE = 0.9
BETA_TWO = 0.999
ADAM_EPS = 1e-08
DECAY_RATE = 0.01
NEG_LARGE = -1e30

LOW = jnp.bfloat16
FULL = jnp.float32


def norm_parts(values):
    centre = jnp.mean(values, axis=-1, keepdims=True)
    centred = values - centre
    spread = jnp.mean(centred * centred, axis=-1, keepdims=True)
    inverse = lax.rsqrt(spread + NORM_EPS)
    return centred * inverse, inverse


def norm_back(grad, unit, inverse, gain_vec):
    scaled = grad * gain_vec
    along = jnp.mean(scaled * unit, axis=-1, keepdims=True)
    return inverse * (scaled - jnp.mean(scaled, axis=-1, keepdims=True) - unit * along)


def smooth_act(values):
    return jax.nn.gelu(values, approximate=True)


def adamw(weight, moment, second, gradient, step_rate, decay_rate):
    moment = BETA_ONE * moment + (1.0 - BETA_ONE) * gradient
    second = BETA_TWO * second + (1.0 - BETA_TWO) * gradient * gradient
    first_hat = moment / (1.0 - BETA_ONE**STEP)
    second_hat = second / (1.0 - BETA_TWO**STEP)
    weight = weight - step_rate * (
        first_hat / (jnp.sqrt(second_hat) + ADAM_EPS) + decay_rate * weight
    )
    return (moment, second, weight)


def matrix_rates():
    return (
        2.5 * D ** (-0.5),
        2.5 * max(1, D * 16 // SEQ_MOST) ** (-0.5),
        2.5 * D ** (-0.5),
        2.5 * FF ** (-0.5),
    )


def vector_rates(entries):
    column = entries % 8
    is_gain = (entries < 8 * D) & ((column == 0) | (column == 5))
    return jnp.where(is_gain, 0.3, 0.05).astype(jnp.float32)


def shifted(x, by):
    length = lax.axis_size("dev")
    return lax.ppermute(x, "dev", [(i, i + by) for i in range(length) if 0 <= i + by < length])


def flipped(x, mask):
    return lax.ppermute(x, "dev", [(i, i ^ mask) for i in range(lax.axis_size("dev"))])


def tied(*arrays):
    return lax.optimization_barrier(arrays)


class Index:
    def __init__(self):
        self.count = lax.axis_size("dev")
        self.me = lax.axis_index("dev")
        self.top = self.count.bit_length() - 3
        self.core = self.me & 1
        self.odd = self.core == 1
        middle = tuple(range(1, self.top))
        self.orders = (middle, tuple(reversed(middle)))

    def relative(self, order):
        seen = [r << self.top for r in range(4)]
        for b in reversed(order):
            seen = seen + [s | 1 << b for s in seen]
        return [s >> 1 for s in seen]


def by_core(ix, own, other):
    return jnp.where(ix.odd, other, own), jnp.where(ix.odd, own, other)


def cut_at(x, column):
    return (x[..., :column], x[..., column:])


def gather_top(ix, piece):
    return jnp.stack([piece] + [flipped(piece, r << ix.top) for r in (1, 2, 3)])


def gather_mid(sides, orders):
    done = []
    for x, order in zip(sides, orders):
        for b in reversed(order[1:]):
            x = jnp.concatenate([x, flipped(x, 1 << b)], axis=0)
        done.append(x)
    return done


def gather_last(sides, orders):
    return [(x, flipped(x, 1 << order[0])) for x, order in zip(sides, orders)]


def place_kernel(rows, count, moves, inward, chip_ref, *refs):
    ins, outs = refs[:count], refs[count:]
    chip = chip_ref[0]
    for part, at, column, whole, relative, whole_column, width in moves:
        start = pl.multiple_of((chip ^ relative) * rows, rows)
        spot = (pl.ds(start, rows), pl.ds(whole_column, width))
        if inward:
            outs[whole][spot] = ins[part][at, :, column : column + width]
        else:
            outs[part][at, :, column : column + width] = ins[whole][spot]


def place(ix, rows, ins, moves, inward, out_shape):
    return pl.pallas_call(
        lambda *refs: place_kernel(rows, len(ins), moves, inward, *refs),
        in_specs=[pl.BlockSpec(memory_space=pltpu.SMEM)]
        + [pl.BlockSpec(memory_space=pltpu.VMEM)] * len(ins),
        out_specs=[pl.BlockSpec(memory_space=pltpu.VMEM)] * len(out_shape),
        out_shape=[jax.ShapeDtypeStruct(shape, LOW) for shape in out_shape],
        compiler_params=pltpu.CompilerParams(
            vmem_limit_bytes=4 * sum(rows * move[-1] for move in moves) + 2**21
        ),
    )((ix.me >> 1).astype(jnp.int32).reshape(1), *ins)


def place_moves(ix, orders, spots):
    moves = []
    for s, order in enumerate(orders):
        for spot, relative in enumerate(ix.relative(order)):
            half, at = divmod(spot, ix.count // 4)
            for column, width, whole, whole_column in spots[s]:
                moves.append((2 * s + half, at, column, whole, relative, whole_column, width))
    return moves


def assemble(ix, sides, orders, spots, widths):
    chips = ix.count // 2
    rows = sides[0][0].shape[1]
    if rows % 16:
        parts = [{} for _ in widths]
        for side, order, spot in zip(sides, orders, spots):
            seen = ix.relative(order)
            place_of = jnp.array([seen.index(r) for r in range(chips)], jnp.int32)
            pick = place_of[(ix.me >> 1) ^ jnp.arange(chips)]
            full = jnp.take(jnp.concatenate(side, axis=0), pick, axis=0)
            full = full.reshape(chips * rows, -1)
            for column, width, whole, whole_column in spot:
                parts[whole][whole_column] = full[:, column : column + width]
        return [jnp.concatenate([p[c] for c in sorted(p)], axis=1) for p in parts]
    ins = [array for side in sides for array in side]
    shapes = [(chips * rows, width) for width in widths]
    return place(ix, rows, ins, place_moves(ix, orders, spots), True, shapes)


def take_apart(ix, wholes, orders, spots):
    chips = ix.count // 2
    rows = wholes[0].shape[0] // chips
    widths = [sum(spot[1] for spot in side) for side in spots]
    if rows % 16:
        sides = []
        for order, spot in zip(orders, spots):
            side = jnp.concatenate([wholes[w][:, c : c + n] for _, n, w, c in spot], axis=1)
            pick = (ix.me >> 1) ^ jnp.array(ix.relative(order), jnp.int32)
            full = jnp.take(side.reshape(chips, rows, -1), pick, axis=0)
            sides.append((full[: chips // 2], full[chips // 2 :]))
        return sides
    shapes = [(chips // 2, rows, width) for width in widths for _ in range(2)]
    outs = place(ix, rows, wholes, place_moves(ix, orders, spots), False, shapes)
    return [(outs[2 * s], outs[2 * s + 1]) for s in range(len(spots))]


def settle(keep, other, parts):
    size = keep.shape[0] // parts
    return [
        (
            keep[i * size : (i + 1) * size].astype(FULL)
            + other[i * size : (i + 1) * size].astype(FULL)
        ).astype(LOW)
        for i in range(parts)
    ]


def scatter_mid(sides, orders, first, last):
    done = []
    for (keep, send), order in zip(sides, orders):
        for i in range(first, min(last, len(order))):
            parts = 2 if i < len(order) - 1 else 4
            settled = settle(keep, flipped(send, 1 << order[i]), parts)
            keep, send = settled[0], settled[1] if parts == 2 else settled[1:]
        done.append((keep, send))
    return done


def scatter_top(ix, sides):
    total = jnp.concatenate([keep[0] for keep, _ in sides], axis=-1).astype(FULL)
    for r in (1, 2, 3):
        part = jnp.concatenate([send[r - 1][0] for _, send in sides], axis=-1)
        total = total + flipped(part, r << ix.top).astype(FULL)
    return total


def own_rows(ix, summed):
    rows = summed.shape[0] // 2
    keep = lax.dynamic_slice_in_dim(summed, ix.core * rows, rows, 0)
    other = lax.dynamic_slice_in_dim(summed, (1 - ix.core) * rows, rows, 0)
    return keep, flipped(other, 1)


PAIR = 2 * HEAD_DIM
PAIRS = HEADS // 2
SIDE = PAIRS // 2
SCALE = HEAD_DIM ** (-0.5)
VMEM_BYTES = 20 * 1024 * 1024


def by_head(pair):
    low_half = lax.broadcasted_iota(jnp.int32, pair.shape, 1) < HEAD_DIM
    zero = jnp.zeros_like(pair)
    return (
        low_half,
        jnp.where(low_half, pair, zero).astype(LOW),
        jnp.where(low_half, zero, pair).astype(LOW),
    )


def dot_over(operand_a, operand_b, dim_a, dim_b):
    return lax.dot_general(
        operand_a, operand_b, (((dim_a,), (dim_b,)), ((), ())), preferred_element_type=FULL
    )


def attend_kernel(first_ref, qkv_ref, out_ref, weights_ref):
    rows, near = weights_ref.shape[-2:]
    before = near - rows
    key = lax.broadcasted_iota(jnp.int32, (rows, near), 1)
    last = lax.broadcasted_iota(jnp.int32, (rows, near), 0) + (near - rows)
    for block in range(2):
        own, seen = pl.ds(block * rows, rows), pl.ds(block * rows, near)
        query = qkv_ref[pl.ds(before + block * rows, rows), :PAIR]
        low_half, *q_heads = by_head(query.astype(FULL) * SCALE)
        k, v = qkv_ref[seen, PAIR : 2 * PAIR], qkv_ref[seen, 2 * PAIR :]
        allowed = (key >= first_ref[own, :] - block * rows) & (key <= last)
        blended = []
        for head in range(2):
            scores = jnp.where(allowed, dot_over(q_heads[head], k, 1, 1), NEG_LARGE)
            weights = jnp.exp(scores - jnp.max(scores, axis=-1, keepdims=True))
            weights = weights * (1.0 / jnp.sum(weights, axis=-1, keepdims=True))
            weights = weights.astype(LOW)
            weights_ref[0, 2 * block + head] = weights
            blended.append(dot_over(weights, v, 1, 0))
        out_ref[own, :] = jnp.where(low_half, blended[0], blended[1]).astype(LOW)


def attend(first_key, qkv, rows, first, pairs):
    window = qkv.shape[0]
    near = window - rows
    return pl.pallas_call(
        attend_kernel,
        grid=(pairs,),
        in_specs=[
            pl.BlockSpec((2 * rows, 1), lambda i: (0, 0)),
            pl.BlockSpec((window, 3 * PAIR), lambda i: (0, i + first)),
        ],
        out_specs=[
            pl.BlockSpec((2 * rows, PAIR), lambda i: (0, i)),
            pl.BlockSpec((1, 4, rows, near), lambda i: (i, 0, 0, 0)),
        ],
        out_shape=[
            jax.ShapeDtypeStruct((2 * rows, pairs * PAIR), LOW),
            jax.ShapeDtypeStruct((pairs, 4, rows, near), LOW),
        ],
        compiler_params=pltpu.CompilerParams(vmem_limit_bytes=VMEM_BYTES),
    )(first_key, qkv)


def attend_back_kernel(weights_ref, grad_ref, qkv_ref, out_ref):
    rows, near = weights_ref.shape[-2:]
    before = near - rows
    out_ref[:before, :PAIR] = jnp.zeros((before, PAIR), LOW)
    turned = []
    for block in range(2):
        own, seen = pl.ds(block * rows, rows), pl.ds(block * rows, near)
        low_half, *grad_heads = by_head(grad_ref[own, :].astype(FULL))
        asking = pl.ds(before + block * rows, rows)
        _, *q_heads = by_head(qkv_ref[asking, :PAIR].astype(FULL))
        k, v = qkv_ref[seen, PAIR : 2 * PAIR], qkv_ref[seen, 2 * PAIR :]
        dq = []
        dk_turned = dv_turned = 0.0
        for head in range(2):
            weights_low = weights_ref[0, 2 * block + head]
            weights = weights_low.astype(FULL)
            grad_weights = dot_over(grad_heads[head], v, 1, 1)
            inner_sum = jnp.sum(weights * grad_weights, axis=-1, keepdims=True)
            grad_scores = (weights * (grad_weights - inner_sum)).astype(LOW)
            dq.append(dot_over(grad_scores, k, 1, 0))
            dk_turned += dot_over(q_heads[head], grad_scores, 0, 0)
            dv_turned += dot_over(grad_heads[head], weights_low, 0, 0)
        out_ref[asking, :PAIR] = (jnp.where(low_half, dq[0], dq[1]) * SCALE).astype(LOW)
        turned.append((dk_turned * SCALE, dv_turned))
    for which in range(2):
        early, late = turned[0][which], turned[1][which]
        whole = jnp.concatenate(
            [early[:, :rows], early[:, rows:] + late[:, : near - rows], late[:, near - rows :]],
            axis=1,
        )
        out_ref[:, (which + 1) * PAIR : (which + 2) * PAIR] = whole.T.astype(LOW)


def attend_back(weights, grad, qkv, rows, first, pairs):
    window = qkv.shape[0]
    near = window - rows
    return pl.pallas_call(
        attend_back_kernel,
        grid=(pairs,),
        in_specs=[
            pl.BlockSpec((1, 4, rows, near), lambda i: (i, 0, 0, 0)),
            pl.BlockSpec((2 * rows, PAIR), lambda i: (0, i + first)),
            pl.BlockSpec((window, 3 * PAIR), lambda i: (0, i)),
        ],
        out_specs=pl.BlockSpec((window, 3 * PAIR), lambda i: (0, i)),
        out_shape=jax.ShapeDtypeStruct((window, 3 * pairs * PAIR), LOW),
        compiler_params=pltpu.CompilerParams(vmem_limit_bytes=VMEM_BYTES),
    )(weights, grad, qkv)


def paired_columns(x):
    rows = x.shape[0]
    parts = x.reshape(rows, 3, 2, SIDE, PAIR).transpose(2, 0, 3, 1, 4)
    return parts.reshape(2, rows, 3 * SIDE * PAIR)


def plain_columns(sides):
    rows = sides[0].shape[0]
    parts = [side.reshape(rows, SIDE, 3, PAIR).transpose(0, 2, 1, 3) for side in sides]
    return jnp.stack(parts, axis=2).reshape(rows, 3 * D)


def hidden_columns(x, share):
    parts = x.reshape(x.shape[0], FF // (2 * share), 2, share)
    return [parts[:, :, s].reshape(x.shape[0], FF // 2) for s in range(2)]


def plain_hidden(sides, share):
    rows = sides[0].shape[0]
    parts = [side.reshape(rows, FF // (2 * share), 1, share) for side in sides]
    return jnp.concatenate(parts, axis=2).reshape(rows, FF)


TABLE_ROWS = 8 * D // VCOLS


def table_places():
    feature = np.arange(D)[None]
    entry = 8 * (feature % 3) + np.arange(8)[:, None]
    first_row = 2 * (feature // 3)
    return (
        jnp.asarray(first_row, jnp.int32),
        jnp.asarray(entry // VCOLS, jnp.int32),
        jnp.asarray(entry % VCOLS, jnp.int32),
    )


def up_places(ix, share):
    unit = np.arange(FF // 2)[None]
    row = 2 * (unit // share) * (share // VCOLS) + unit % share // VCOLS
    return (
        jnp.asarray(row, jnp.int32) + ix.core * (share // VCOLS),
        jnp.asarray(unit % VCOLS, jnp.int32),
    )


def one_at(row, rows):
    at = lax.broadcasted_iota(jnp.int32, (rows, row.shape[1]), 0)
    return jnp.where(at == row, 1.0, 0.0).astype(LOW)


def in_column(column):
    return lax.broadcasted_iota(jnp.int32, (16, column.shape[1]), 0) == column


def read_vec_kernel(vec_ref, first_ref, step_ref, column_ref, row_ref, spot_ref, table_ref, up_ref):
    vec = vec_ref[...]
    table = vec[:TABLE_ROWS]
    moved = [dot_over(table, one_at(first_ref[...] + d, TABLE_ROWS), 0, 0)[:16] for d in range(2)]
    for c in range(8):
        step = step_ref[c : c + 1, :]
        picked = jnp.where(step == 0, moved[0], moved[1])
        picked = jnp.where(in_column(column_ref[c : c + 1, :]), picked, 0.0)
        table_ref[c : c + 1, :] = jnp.sum(picked, axis=0, keepdims=True)
    rest = vec[TABLE_ROWS:]
    moved = dot_over(rest, one_at(row_ref[...], rest.shape[0]), 0, 0)[:16]
    picked = jnp.where(in_column(spot_ref[...]), moved, 0.0)
    up_ref[...] = jnp.sum(picked, axis=0, keepdims=True)


def read_vec(ix, vec, share):
    return pl.pallas_call(
        read_vec_kernel,
        out_shape=[
            jax.ShapeDtypeStruct((8, D), FULL),
            jax.ShapeDtypeStruct((1, FF // 2), FULL),
        ],
        compiler_params=pltpu.CompilerParams(vmem_limit_bytes=VMEM_BYTES),
    )(vec, *table_places(), *up_places(ix, share))


def write_vec_kernel(
    core_ref, table_ref, bias_ref, up_ref, first_ref, step_ref, column_ref, row_ref, spot_ref, out_ref
):
    core = core_ref[0]
    wide = SIDE * PAIR
    moved = [jnp.zeros((16, D), FULL) for _ in range(2)]
    for c in range(8):
        row = table_ref[c : c + 1, :]
        if c in (2, 3):
            part = 0 if c == 2 else 2
            half = jnp.concatenate(
                [
                    bias_ref[:, (3 * i + part) * PAIR : (3 * i + part + 1) * PAIR]
                    for i in range(SIDE)
                ],
                axis=1,
            )
            lane = lax.broadcasted_iota(jnp.int32, (1, D), 1)
            own = (lane >= core * wide) & (lane < (core + 1) * wide)
            row = jnp.where(own, jnp.concatenate([half, half], axis=1), 0.0)
        step = step_ref[c : c + 1, :]
        here = in_column(column_ref[c : c + 1, :])
        for d in range(2):
            moved[d] = moved[d] + jnp.where(here & (step == d), row, 0.0)
    blank = jnp.zeros((112, D), LOW)
    total = 0.0
    for d in range(2):
        wanted = jnp.concatenate([moved[d].astype(LOW), blank], axis=0)
        total = total + dot_over(one_at(first_ref[...] + d, TABLE_ROWS), wanted, 1, 1)
    out_ref[:TABLE_ROWS, :] = total.astype(LOW)
    rest = out_ref.shape[0] - TABLE_ROWS
    wanted = jnp.where(in_column(spot_ref[...]), up_ref[...], 0.0).astype(LOW)
    wanted = jnp.concatenate([wanted, jnp.zeros((112, wanted.shape[1]), LOW)], axis=0)
    out_ref[TABLE_ROWS:, :] = dot_over(one_at(row_ref[...], rest), wanted, 1, 1).astype(LOW)


def write_vec(ix, table, bias, up, share):
    whole = pl.BlockSpec(memory_space=pltpu.VMEM)
    return pl.pallas_call(
        write_vec_kernel,
        in_specs=[pl.BlockSpec(memory_space=pltpu.SMEM)] + [whole] * 8,
        out_specs=whole,
        out_shape=jax.ShapeDtypeStruct((D, 128), LOW),
        compiler_params=pltpu.CompilerParams(vmem_limit_bytes=VMEM_BYTES),
    )(
        ix.core.astype(jnp.int32).reshape(1),
        table,
        bias,
        up,
        *table_places(),
        *up_places(ix, share),
    )


def dot(operand_a, operand_b):
    return jnp.dot(operand_a, operand_b, preferred_element_type=FULL)


def outer_sum(operand_a, operand_b):
    return jnp.einsum("ti,tj->ij", operand_a, operand_b, preferred_element_type=FULL).astype(LOW)


def dot_turned(operand_a, operand_b):
    return jnp.einsum("ti,ji->tj", operand_a, operand_b, preferred_element_type=FULL)


def body(
    tokens,
    cotangent,
    starts,
    w_qkv,
    m_qkv,
    v_qkv,
    w_out,
    m_out,
    v_out,
    w_up,
    m_up,
    v_up,
    w_down,
    m_down,
    v_down,
    vectors,
    m_vec,
    v_vec,
):
    ix = Index()
    rows = D // ix.count
    share = FF // ix.count
    tok_rows = tokens.shape[0]
    reach_count = (SEQ_MOST + tok_rows - 2) // tok_rows
    assert reach_count == 4
    chip_rows = 2 * tok_rows
    near_rows = (reach_count + 2) * tok_rows
    wide = SIDE * PAIR
    columns = 3 * wide
    out_wide, up_wide = D // 2, FF // 2

    early = 3 * PAIR * (SIDE - 1)
    late = columns - early
    first_spots = [[(0, early, 0, 0)], [(0, late + 128, 0, 0)]]
    cut = (out_wide + up_wide) // 256 * 128
    second_spots = [
        [(0, out_wide, 0, 0), (out_wide, cut - out_wide, 1, 0)],
        [(0, out_wide + up_wide - cut, 1, cut - out_wide)],
    ]
    third_spots = [[(0, D // 2, 0, 0)], [(0, D // 2, 0, D // 2)]]
    orders = ix.orders
    vec_piece = jnp.pad(vectors.astype(LOW).reshape(rows, VCOLS), ((0, 0), (0, 128 - VCOLS)))
    qkv_mine, qkv_others = by_core(ix, *paired_columns(w_qkv.astype(LOW).reshape(rows, 3 * D)))
    mine = jnp.concatenate([qkv_mine, vec_piece], axis=1)
    others = jnp.concatenate([qkv_others, vec_piece], axis=1)
    first = jnp.concatenate(by_core(ix, mine, flipped(others, 1)), axis=0)
    first = gather_top(ix, first)
    first, w_out, w_up = tied(first, w_out, w_up)

    first = gather_mid((first[..., :early], first[..., early:]), orders)
    up_sides = hidden_columns(w_up.astype(LOW).reshape(rows, FF), share)
    out_low = w_out.astype(LOW).reshape(rows, D)
    pieces = [
        jnp.concatenate([out_low[:, s * out_wide : (s + 1) * out_wide], up_sides[s]], axis=1)
        for s in range(2)
    ]
    own_piece, others = by_core(ix, *pieces)
    second = jnp.concatenate(by_core(ix, own_piece, flipped(others, 1)), axis=0)
    *first, second, starts, tokens = tied(*first, second, starts, tokens)
    first = gather_last(first, orders)
    mine = jnp.stack([shifted(tokens, 4), shifted(tokens, 2), tokens])
    chip_starts = jnp.concatenate(by_core(ix, starts, flipped(starts, 1)))
    first, second, mine, chip_starts, cotangent, w_down = tied(
        first, second, mine, chip_starts, cotangent, w_down
    )
    near_tokens = jnp.stack(by_core(ix, mine, flipped(mine, 1)), axis=1).reshape(near_rows, D)
    second = gather_top(ix, second)
    early_w = assemble(ix, first[:1], orders[:1], first_spots[:1], [early])[0]
    late_w = assemble(ix, first[1:], orders[1:], first_spots[1:], [late + 128])[0]
    vec_table, up_bias = read_vec(ix, late_w[:, late:], share)
    late_w = late_w[:, :late]
    third = w_down.astype(LOW).reshape(4 * rows, D)
    gain_one, shift_one, bias_q, bias_v, bias_o, gain_two, shift_two, bias_down = (
        vec_table[i] for i in range(8)
    )
    bias_q = lax.dynamic_slice_in_dim(bias_q, ix.core * wide, wide)
    bias_v = lax.dynamic_slice_in_dim(bias_v, ix.core * wide, wide)

    near_unit, near_inverse = norm_parts(near_tokens.astype(FULL))
    near_normed = (near_unit * gain_one + shift_one).astype(LOW)
    near_normed, second, third, cotangent = tied(near_normed, second, third, cotangent)
    second = gather_mid(cut_at(second, cut), orders)
    third = gather_top(ix, third)
    chip_cotangent = jnp.concatenate(by_core(ix, cotangent, flipped(cotangent, 1)), axis=0)
    bias = jnp.stack(
        [bias_q.reshape(SIDE, PAIR), jnp.zeros((SIDE, PAIR), FULL), bias_v.reshape(SIDE, PAIR)],
        axis=1,
    ).reshape(columns)
    first_key = (chip_starts - ((ix.me >> 1) * chip_rows - reach_count * tok_rows))[:, None]
    early_qkv = (dot(near_normed, early_w) + bias[:early]).astype(LOW)
    late_qkv = (dot(near_normed, late_w) + bias[early:]).astype(LOW)
    early_qkv, late_qkv, second = tied(early_qkv, late_qkv, second)
    second = gather_last(second, orders)
    mixed, weights = [None, None], [None, None]
    mixed[0], weights[0] = attend(first_key, late_qkv, tok_rows, 0, 1)
    mixed[0], early_qkv = tied(mixed[0], early_qkv)
    mixed[1], weights[1] = attend(first_key, early_qkv, tok_rows, 0, SIDE - 1)
    mixed = jnp.concatenate([mixed[1], mixed[0]], axis=1)
    mixed, second, third = tied(mixed, second, third)
    third = gather_mid(cut_at(third, D // 2), orders)
    attended = jnp.concatenate(by_core(ix, mixed, flipped(mixed, 1)), axis=1)
    out_half, up_w = assemble(ix, second, orders, second_spots, [out_wide, up_wide])
    out_w = jnp.concatenate(by_core(ix, out_half, flipped(out_half, 1)), axis=1)
    attended, out_w, third = tied(attended, out_w, third)
    third = gather_last(third, orders)
    inputs = near_tokens[near_rows - chip_rows :].astype(FULL)
    middle = inputs + (dot(attended, out_w) + bias_o)
    unit_two, inverse_two = norm_parts(middle)
    normed_two = (unit_two * gain_two + shift_two).astype(LOW)
    hidden_pre = dot(normed_two, up_w) + up_bias
    hidden_low = smooth_act(hidden_pre).astype(LOW)
    grad_downw = outer_sum(hidden_low, chip_cotangent)
    hidden_low, hidden_pre, grad_downw = tied(hidden_low, hidden_pre, grad_downw)
    sum_down = scatter_mid(take_apart(ix, [grad_downw], orders, third_spots), orders, 0, 1)
    down_w = assemble(ix, third, orders, third_spots, [D])[0]
    result = dot(hidden_low, down_w).reshape(2, tok_rows, D)
    own_result, other_result = by_core(ix, result[0], result[1])
    own_result = own_result + flipped(other_result.astype(LOW), 1).astype(FULL)
    own_middle = lax.dynamic_slice_in_dim(middle, ix.core * tok_rows, tok_rows, 0)
    out_tokens = (own_middle + (own_result + bias_down)).astype(LOW)

    grad_hidden = dot_turned(chip_cotangent, down_w)
    act_value, act_back = jax.vjp(smooth_act, hidden_pre)
    grad_pre = act_back(grad_hidden)[0].astype(LOW)
    partial_two = dot_turned(grad_pre, up_w)
    grad_gain_two = jnp.sum(partial_two * unit_two, axis=0)
    grad_shift_two = jnp.sum(partial_two, axis=0)
    grad_normed_two = partial_two + flipped(partial_two.astype(LOW), 1).astype(FULL)
    grad_normed_two, grad_pre, sum_down = tied(grad_normed_two, grad_pre, sum_down)
    sum_down = scatter_mid(sum_down, orders, 1, 9)
    grad_upw = outer_sum(normed_two, grad_pre)
    grad_middle = chip_cotangent.astype(FULL) + norm_back(
        grad_normed_two, unit_two, inverse_two, gain_two
    )
    grad_branch = grad_middle.astype(LOW)
    own_part = lax.dynamic_slice_in_dim(grad_branch, ix.core * out_wide, out_wide, 1)
    grad_outw = outer_sum(attended, own_part)
    own_out = lax.dynamic_slice_in_dim(out_w, ix.core * wide, wide, 0)
    grad_mixed = dot_turned(grad_branch, own_out).astype(LOW)
    grad_mixed, grad_outw, grad_upw, sum_down = tied(grad_mixed, grad_outw, grad_upw, sum_down)
    sum_second = take_apart(ix, [grad_outw, grad_upw], orders, second_spots)
    grad_mixed, sum_second = tied(grad_mixed, sum_second)
    sum_second = scatter_mid(sum_second, orders, 0, 1)
    early_back = attend_back(weights[1], grad_mixed, early_qkv, tok_rows, 0, SIDE - 1)
    sum_early = take_apart(ix, [outer_sum(near_normed, early_back)], orders[:1], first_spots[:1])
    sum_down = scatter_top(ix, sum_down)
    early_back, grad_mixed, sum_early, sum_second = tied(
        early_back, grad_mixed, sum_early, sum_second
    )
    sum_early = scatter_mid(sum_early, orders[:1], 0, 1)
    sum_second = scatter_mid(sum_second, orders, 1, 9)
    late_back = attend_back(weights[0], grad_mixed, late_qkv, tok_rows, SIDE - 1, 1)
    late_spots = [[(0, late, 0, 0)]]
    sum_late = take_apart(ix, [outer_sum(near_normed, late_back)], orders[1:], late_spots)
    sums_two = (
        grad_gain_two,
        grad_shift_two,
        jnp.sum(grad_branch.astype(FULL), axis=0),
        jnp.sum(cotangent.astype(FULL), axis=0),
        jnp.sum(grad_pre.astype(FULL), axis=0),
    )
    late_back, sum_late, sum_down, sum_second, sums_two = tied(
        late_back, sum_late, sum_down, sum_second, sums_two
    )
    sum_second = scatter_top(ix, sum_second)
    grad_gain_two, grad_shift_two, grad_bias_o, grad_bias_down, grad_bias_up = sums_two
    sum_late = scatter_mid(sum_late, orders[1:], 0, 1)

    grad_near = (dot_turned(early_back, early_w) + dot_turned(late_back, late_w)).astype(LOW)
    grad_gain_one = jnp.sum(grad_near.astype(FULL) * near_unit, axis=0)
    grad_shift_one = jnp.sum(grad_near.astype(FULL), axis=0)
    grad_gain_one, grad_shift_one, sum_early, sum_late = tied(
        grad_gain_one, grad_shift_one, sum_early, sum_late
    )
    sum_early = scatter_mid(sum_early, orders[:1], 1, 9)
    sum_late = scatter_mid(sum_late, orders[1:], 1, 9)
    grad_bias = jnp.concatenate(
        [jnp.sum(early_back.astype(FULL), axis=0), jnp.sum(late_back.astype(FULL), axis=0)]
    )
    blank = jnp.zeros((D,), FULL)
    grad_table = jnp.stack(
        [
            grad_gain_one,
            grad_shift_one,
            blank,
            blank,
            0.5 * grad_bias_o,
            grad_gain_two,
            grad_shift_two,
            grad_bias_down,
        ]
    )
    grad_vec = write_vec(ix, grad_table, grad_bias[None], grad_bias_up[None], share)
    blocks = grad_near.reshape(reach_count // 2 + 1, 2, tok_rows, D)
    own_blocks, other_blocks = by_core(ix, blocks[:, 0], blocks[:, 1])
    mate_blocks = flipped(other_blocks, 1)
    grad_vec, sum_second, mate_blocks = tied(grad_vec, sum_second, mate_blocks)
    vec_spots = [[(0, 128, 0, 0)]]
    sum_vec = scatter_mid(take_apart(ix, [grad_vec], orders[:1], vec_spots), orders[:1], 0, 9)

    own_blocks = own_blocks.astype(FULL) + mate_blocks.astype(FULL)
    four_back, two_back = own_blocks[0].astype(LOW), own_blocks[1].astype(LOW)
    sum_early, sum_late, sum_vec = tied(sum_early, sum_late, sum_vec)
    sum_first = scatter_top(ix, sum_early + sum_late + sum_vec)
    own = (
        own_blocks[2]
        + shifted(two_back, -2).astype(FULL)
        + shifted(four_back, -4).astype(FULL)
    )
    sum_first, sum_second, own = tied(sum_first, sum_second, own)
    unit_one, inverse_one = norm_parts(tokens.astype(FULL))
    own_grad_middle = lax.dynamic_slice_in_dim(grad_middle, ix.core * tok_rows, tok_rows, 0)
    input_grad = own_grad_middle + norm_back(own, unit_one, inverse_one, gain_one)

    keep_second, other_second = own_rows(ix, sum_second)
    keep_first, other_first = own_rows(ix, sum_first)
    g_vec = (keep_first[:, columns:] + other_first[:, columns:])[:, :VCOLS].reshape(-1)
    g_qkv = plain_columns(by_core(ix, keep_first[:, :columns], other_first[:, :columns]))
    g_out = jnp.concatenate(
        by_core(ix, keep_second[:, :out_wide], other_second[:, :out_wide]), axis=1
    )
    g_up = plain_hidden(by_core(ix, keep_second[:, out_wide:], other_second[:, out_wide:]), share)

    rate_qkv, rate_out, rate_up, rate_down = matrix_rates()
    entries = ix.me * vectors.shape[0] + jnp.arange(vectors.shape[0], dtype=jnp.int32)
    qkv_new = adamw(w_qkv, m_qkv, v_qkv, g_qkv.reshape(-1), rate_qkv, DECAY_RATE)
    out_new = adamw(w_out, m_out, v_out, g_out.reshape(-1), rate_out, DECAY_RATE)
    up_new = adamw(w_up, m_up, v_up, g_up.reshape(-1), rate_up, DECAY_RATE)
    down_new = adamw(w_down, m_down, v_down, sum_down.reshape(-1), rate_down, DECAY_RATE)
    vec_new = adamw(vectors, m_vec, v_vec, g_vec, vector_rates(entries), 0.0)
    return (out_tokens, input_grad) + qkv_new + out_new + up_new + down_new + vec_new


def solution(mesh):
    in_specs = (P("dev", None), P("dev", None)) + (P("dev"),) * 16
    out_specs = (P("dev", None), P("dev", None)) + (P("dev"),) * 15
    return jax.shard_map(body, mesh=mesh, in_specs=in_specs, out_specs=out_specs, check_vma=False)
```

```python
import jax
import jax.numpy as jnp
import numpy as np
from jax import lax
from jax.experimental import pallas as pl
from jax.experimental.pallas import tpu as pltpu
from jax.sharding import PartitionSpec as P

D = 768
HEAD_DIM = 64
HEADS = D // HEAD_DIM
FF = 3072
SEQ_MOST = 1024
STEP = 10
VCOLS = 12


NORM_EPS = 1e-05
BETA_ONE = 0.9
BETA_TWO = 0.999
ADAM_EPS = 1e-08
DECAY_RATE = 0.01
NEG_LARGE = -1e30

LOW = jnp.bfloat16
FULL = jnp.float32


def norm_parts(values):
    centre = jnp.mean(values, axis=-1, keepdims=True)
    centred = values - centre
    spread = jnp.mean(centred * centred, axis=-1, keepdims=True)
    inverse = lax.rsqrt(spread + NORM_EPS)
    return centred * inverse, inverse


def norm_back(grad, unit, inverse, gain_vec):
    scaled = grad * gain_vec
    along = jnp.mean(scaled * unit, axis=-1, keepdims=True)
    return inverse * (scaled - jnp.mean(scaled, axis=-1, keepdims=True) - unit * along)


def smooth_act(values):
    return jax.nn.gelu(values, approximate=True)


def adamw(weight, moment, second, gradient, step_rate, decay_rate):
    moment = BETA_ONE * moment + (1.0 - BETA_ONE) * gradient
    second = BETA_TWO * second + (1.0 - BETA_TWO) * gradient * gradient
    first_hat = moment / (1.0 - BETA_ONE**STEP)
    second_hat = second / (1.0 - BETA_TWO**STEP)
    weight = weight - step_rate * (
        first_hat / (jnp.sqrt(second_hat) + ADAM_EPS) + decay_rate * weight
    )
    return (moment, second, weight)


def matrix_rates():
    return (
        2.5 * D ** (-0.5),
        2.5 * max(1, D * 16 // SEQ_MOST) ** (-0.5),
        2.5 * D ** (-0.5),
        2.5 * FF ** (-0.5),
    )


def vector_rates(entries):
    column = entries % 8
    is_gain = (entries < 8 * D) & ((column == 0) | (column == 5))
    return jnp.where(is_gain, 0.3, 0.05).astype(jnp.float32)


def shifted(x, by):
    length = lax.axis_size("dev")
    return lax.ppermute(x, "dev", [(i, i + by) for i in range(length) if 0 <= i + by < length])


def flipped(x, mask):
    return lax.ppermute(x, "dev", [(i, i ^ mask) for i in range(lax.axis_size("dev"))])


def tied(*arrays):
    return lax.optimization_barrier(arrays)


class Index:
    def __init__(self):
        self.count = lax.axis_size("dev")
        self.me = lax.axis_index("dev")
        self.top = self.count.bit_length() - 3
        self.core = self.me & 1
        self.odd = self.core == 1
        middle = tuple(range(1, self.top))
        self.orders = (middle, tuple(reversed(middle)))

    def relative(self, order):
        seen = [r << self.top for r in range(4)]
        for b in reversed(order):
            seen = seen + [s | 1 << b for s in seen]
        return [s >> 1 for s in seen]


def by_core(ix, own, other):
    return jnp.where(ix.odd, other, own), jnp.where(ix.odd, own, other)


def cut_at(x, column):
    return (x[..., :column], x[..., column:])


def gather_top(ix, piece):
    return jnp.stack([piece] + [flipped(piece, r << ix.top) for r in (1, 2, 3)])


def gather_mid(sides, orders):
    done = []
    for x, order in zip(sides, orders):
        for b in reversed(order[1:]):
            x = jnp.concatenate([x, flipped(x, 1 << b)], axis=0)
        done.append(x)
    return done


def gather_last(sides, orders):
    return [(x, flipped(x, 1 << order[0])) for x, order in zip(sides, orders)]


def place_kernel(rows, count, moves, inward, chip_ref, *refs):
    ins, outs = refs[:count], refs[count:]
    chip = chip_ref[0]
    for part, at, column, whole, relative, whole_column, width in moves:
        start = pl.multiple_of((chip ^ relative) * rows, rows)
        spot = (pl.ds(start, rows), pl.ds(whole_column, width))
        if inward:
            outs[whole][spot] = ins[part][at, :, column : column + width]
        else:
            outs[part][at, :, column : column + width] = ins[whole][spot]


def place(ix, rows, ins, moves, inward, out_shape):
    return pl.pallas_call(
        lambda *refs: place_kernel(rows, len(ins), moves, inward, *refs),
        in_specs=[pl.BlockSpec(memory_space=pltpu.SMEM)]
        + [pl.BlockSpec(memory_space=pltpu.VMEM)] * len(ins),
        out_specs=[pl.BlockSpec(memory_space=pltpu.VMEM)] * len(out_shape),
        out_shape=[jax.ShapeDtypeStruct(shape, LOW) for shape in out_shape],
        compiler_params=pltpu.CompilerParams(
            vmem_limit_bytes=4 * sum(rows * move[-1] for move in moves) + 2**21
        ),
    )((ix.me >> 1).astype(jnp.int32).reshape(1), *ins)


def place_moves(ix, orders, spots):
    moves = []
    for s, order in enumerate(orders):
        for spot, relative in enumerate(ix.relative(order)):
            half, at = divmod(spot, ix.count // 4)
            for column, width, whole, whole_column in spots[s]:
                moves.append((2 * s + half, at, column, whole, relative, whole_column, width))
    return moves


def assemble(ix, sides, orders, spots, widths):
    chips = ix.count // 2
    rows = sides[0][0].shape[1]
    if rows % 16:
        parts = [{} for _ in widths]
        for side, order, spot in zip(sides, orders, spots):
            seen = ix.relative(order)
            place_of = jnp.array([seen.index(r) for r in range(chips)], jnp.int32)
            pick = place_of[(ix.me >> 1) ^ jnp.arange(chips)]
            full = jnp.take(jnp.concatenate(side, axis=0), pick, axis=0)
            full = full.reshape(chips * rows, -1)
            for column, width, whole, whole_column in spot:
                parts[whole][whole_column] = full[:, column : column + width]
        return [jnp.concatenate([p[c] for c in sorted(p)], axis=1) for p in parts]
    ins = [array for side in sides for array in side]
    shapes = [(chips * rows, width) for width in widths]
    return place(ix, rows, ins, place_moves(ix, orders, spots), True, shapes)


def take_apart(ix, wholes, orders, spots):
    chips = ix.count // 2
    rows = wholes[0].shape[0] // chips
    widths = [sum(spot[1] for spot in side) for side in spots]
    if rows % 16:
        sides = []
        for order, spot in zip(orders, spots):
            side = jnp.concatenate([wholes[w][:, c : c + n] for _, n, w, c in spot], axis=1)
            pick = (ix.me >> 1) ^ jnp.array(ix.relative(order), jnp.int32)
            full = jnp.take(side.reshape(chips, rows, -1), pick, axis=0)
            sides.append((full[: chips // 2], full[chips // 2 :]))
        return sides
    shapes = [(chips // 2, rows, width) for width in widths for _ in range(2)]
    outs = place(ix, rows, wholes, place_moves(ix, orders, spots), False, shapes)
    return [(outs[2 * s], outs[2 * s + 1]) for s in range(len(spots))]


def settle(keep, other, parts):
    size = keep.shape[0] // parts
    return [
        (
            keep[i * size : (i + 1) * size].astype(FULL)
            + other[i * size : (i + 1) * size].astype(FULL)
        ).astype(LOW)
        for i in range(parts)
    ]


def scatter_mid(sides, orders, first, last):
    done = []
    for (keep, send), order in zip(sides, orders):
        for i in range(first, min(last, len(order))):
            parts = 2 if i < len(order) - 1 else 4
            settled = settle(keep, flipped(send, 1 << order[i]), parts)
            keep, send = settled[0], settled[1] if parts == 2 else settled[1:]
        done.append((keep, send))
    return done


def scatter_top(ix, sides):
    total = jnp.concatenate([keep[0] for keep, _ in sides], axis=-1).astype(FULL)
    for r in (1, 2, 3):
        part = jnp.concatenate([send[r - 1][0] for _, send in sides], axis=-1)
        total = total + flipped(part, r << ix.top).astype(FULL)
    return total


def own_rows(ix, summed):
    rows = summed.shape[0] // 2
    keep = lax.dynamic_slice_in_dim(summed, ix.core * rows, rows, 0)
    other = lax.dynamic_slice_in_dim(summed, (1 - ix.core) * rows, rows, 0)
    return keep, flipped(other, 1)


PAIR = 2 * HEAD_DIM
PAIRS = HEADS // 2
SIDE = PAIRS // 2
SCALE = HEAD_DIM ** (-0.5)
VMEM_BYTES = 20 * 1024 * 1024


def by_head(pair):
    low_half = lax.broadcasted_iota(jnp.int32, pair.shape, 1) < HEAD_DIM
    zero = jnp.zeros_like(pair)
    return (
        low_half,
        jnp.where(low_half, pair, zero).astype(LOW),
        jnp.where(low_half, zero, pair).astype(LOW),
    )


def dot_over(operand_a, operand_b, dim_a, dim_b):
    return lax.dot_general(
        operand_a, operand_b, (((dim_a,), (dim_b,)), ((), ())), preferred_element_type=FULL
    )


def attend_kernel(first_ref, qkv_ref, out_ref, weights_ref):
    rows, near = weights_ref.shape[-2:]
    before = near - rows
    key = lax.broadcasted_iota(jnp.int32, (rows, near), 1)
    last = lax.broadcasted_iota(jnp.int32, (rows, near), 0) + (near - rows)
    for block in range(2):
        own, seen = pl.ds(block * rows, rows), pl.ds(block * rows, near)
        query = qkv_ref[pl.ds(before + block * rows, rows), :PAIR]
        low_half, *q_heads = by_head(query.astype(FULL) * SCALE)
        k, v = qkv_ref[seen, PAIR : 2 * PAIR], qkv_ref[seen, 2 * PAIR :]
        allowed = (key >= first_ref[own, :] - block * rows) & (key <= last)
        blended = []
        for head in range(2):
            scores = jnp.where(allowed, dot_over(q_heads[head], k, 1, 1), NEG_LARGE)
            weights = jnp.exp(scores - jnp.max(scores, axis=-1, keepdims=True))
            weights = weights * (1.0 / jnp.sum(weights, axis=-1, keepdims=True))
            weights = weights.astype(LOW)
            weights_ref[0, 2 * block + head] = weights
            blended.append(dot_over(weights, v, 1, 0))
        out_ref[own, :] = jnp.where(low_half, blended[0], blended[1]).astype(LOW)


def attend(first_key, qkv, rows, first, pairs):
    window = qkv.shape[0]
    near = window - rows
    return pl.pallas_call(
        attend_kernel,
        grid=(pairs,),
        in_specs=[
            pl.BlockSpec((2 * rows, 1), lambda i: (0, 0)),
            pl.BlockSpec((window, 3 * PAIR), lambda i: (0, i + first)),
        ],
        out_specs=[
            pl.BlockSpec((2 * rows, PAIR), lambda i: (0, i)),
            pl.BlockSpec((1, 4, rows, near), lambda i: (i, 0, 0, 0)),
        ],
        out_shape=[
            jax.ShapeDtypeStruct((2 * rows, pairs * PAIR), LOW),
            jax.ShapeDtypeStruct((pairs, 4, rows, near), LOW),
        ],
        compiler_params=pltpu.CompilerParams(vmem_limit_bytes=VMEM_BYTES),
    )(first_key, qkv)


def attend_back_kernel(weights_ref, grad_ref, qkv_ref, out_ref):
    rows, near = weights_ref.shape[-2:]
    before = near - rows
    out_ref[:before, :PAIR] = jnp.zeros((before, PAIR), LOW)
    turned = []
    for block in range(2):
        own, seen = pl.ds(block * rows, rows), pl.ds(block * rows, near)
        low_half, *grad_heads = by_head(grad_ref[own, :].astype(FULL))
        asking = pl.ds(before + block * rows, rows)
        _, *q_heads = by_head(qkv_ref[asking, :PAIR].astype(FULL))
        k, v = qkv_ref[seen, PAIR : 2 * PAIR], qkv_ref[seen, 2 * PAIR :]
        dq = []
        dk_turned = dv_turned = 0.0
        for head in range(2):
            weights_low = weights_ref[0, 2 * block + head]
            weights = weights_low.astype(FULL)
            grad_weights = dot_over(grad_heads[head], v, 1, 1)
            inner_sum = jnp.sum(weights * grad_weights, axis=-1, keepdims=True)
            grad_scores = (weights * (grad_weights - inner_sum)).astype(LOW)
            dq.append(dot_over(grad_scores, k, 1, 0))
            dk_turned += dot_over(q_heads[head], grad_scores, 0, 0)
            dv_turned += dot_over(grad_heads[head], weights_low, 0, 0)
        out_ref[asking, :PAIR] = (jnp.where(low_half, dq[0], dq[1]) * SCALE).astype(LOW)
        turned.append((dk_turned * SCALE, dv_turned))
    for which in range(2):
        early, late = turned[0][which], turned[1][which]
        whole = jnp.concatenate(
            [early[:, :rows], early[:, rows:] + late[:, : near - rows], late[:, near - rows :]],
            axis=1,
        )
        out_ref[:, (which + 1) * PAIR : (which + 2) * PAIR] = whole.T.astype(LOW)


def attend_back(weights, grad, qkv, rows, first, pairs):
    window = qkv.shape[0]
    near = window - rows
    return pl.pallas_call(
        attend_back_kernel,
        grid=(pairs,),
        in_specs=[
            pl.BlockSpec((1, 4, rows, near), lambda i: (i, 0, 0, 0)),
            pl.BlockSpec((2 * rows, PAIR), lambda i: (0, i + first)),
            pl.BlockSpec((window, 3 * PAIR), lambda i: (0, i)),
        ],
        out_specs=pl.BlockSpec((window, 3 * PAIR), lambda i: (0, i)),
        out_shape=jax.ShapeDtypeStruct((window, 3 * pairs * PAIR), LOW),
        compiler_params=pltpu.CompilerParams(vmem_limit_bytes=VMEM_BYTES),
    )(weights, grad, qkv)


def paired_columns(x):
    rows = x.shape[0]
    parts = x.reshape(rows, 3, 2, SIDE, PAIR).transpose(2, 0, 3, 1, 4)
    return parts.reshape(2, rows, 3 * SIDE * PAIR)


def plain_columns(sides):
    rows = sides[0].shape[0]
    parts = [side.reshape(rows, SIDE, 3, PAIR).transpose(0, 2, 1, 3) for side in sides]
    return jnp.stack(parts, axis=2).reshape(rows, 3 * D)


def hidden_columns(x, share):
    parts = x.reshape(x.shape[0], FF // (2 * share), 2, share)
    return [parts[:, :, s].reshape(x.shape[0], FF // 2) for s in range(2)]


def plain_hidden(sides, share):
    rows = sides[0].shape[0]
    parts = [side.reshape(rows, FF // (2 * share), 1, share) for side in sides]
    return jnp.concatenate(parts, axis=2).reshape(rows, FF)


TABLE_ROWS = 8 * D // VCOLS


def table_places():
    feature = np.arange(D)[None]
    entry = 8 * (feature % 3) + np.arange(8)[:, None]
    first_row = 2 * (feature // 3)
    return (
        jnp.asarray(first_row, jnp.int32),
        jnp.asarray(entry // VCOLS, jnp.int32),
        jnp.asarray(entry % VCOLS, jnp.int32),
    )


def up_places(ix, share):
    unit = np.arange(FF // 2)[None]
    row = 2 * (unit // share) * (share // VCOLS) + unit % share // VCOLS
    return (
        jnp.asarray(row, jnp.int32) + ix.core * (share // VCOLS),
        jnp.asarray(unit % VCOLS, jnp.int32),
    )


def one_at(row, rows):
    at = lax.broadcasted_iota(jnp.int32, (rows, row.shape[1]), 0)
    return jnp.where(at == row, 1.0, 0.0).astype(LOW)


def in_column(column):
    return lax.broadcasted_iota(jnp.int32, (16, column.shape[1]), 0) == column


def read_vec_kernel(vec_ref, first_ref, step_ref, column_ref, row_ref, spot_ref, table_ref, up_ref):
    vec = vec_ref[...]
    table = vec[:TABLE_ROWS]
    moved = [dot_over(table, one_at(first_ref[...] + d, TABLE_ROWS), 0, 0)[:16] for d in range(2)]
    for c in range(8):
        step = step_ref[c : c + 1, :]
        picked = jnp.where(step == 0, moved[0], moved[1])
        picked = jnp.where(in_column(column_ref[c : c + 1, :]), picked, 0.0)
        table_ref[c : c + 1, :] = jnp.sum(picked, axis=0, keepdims=True)
    rest = vec[TABLE_ROWS:]
    moved = dot_over(rest, one_at(row_ref[...], rest.shape[0]), 0, 0)[:16]
    picked = jnp.where(in_column(spot_ref[...]), moved, 0.0)
    up_ref[...] = jnp.sum(picked, axis=0, keepdims=True)


def read_vec(ix, vec, share):
    return pl.pallas_call(
        read_vec_kernel,
        out_shape=[
            jax.ShapeDtypeStruct((8, D), FULL),
            jax.ShapeDtypeStruct((1, FF // 2), FULL),
        ],
        compiler_params=pltpu.CompilerParams(vmem_limit_bytes=VMEM_BYTES),
    )(vec, *table_places(), *up_places(ix, share))


def write_vec_kernel(
    core_ref, table_ref, bias_ref, up_ref, first_ref, step_ref, column_ref, row_ref, spot_ref, out_ref
):
    core = core_ref[0]
    wide = SIDE * PAIR
    moved = [jnp.zeros((16, D), FULL) for _ in range(2)]
    for c in range(8):
        row = table_ref[c : c + 1, :]
        if c in (2, 3):
            part = 0 if c == 2 else 2
            half = jnp.concatenate(
                [
                    bias_ref[:, (3 * i + part) * PAIR : (3 * i + part + 1) * PAIR]
                    for i in range(SIDE)
                ],
                axis=1,
            )
            lane = lax.broadcasted_iota(jnp.int32, (1, D), 1)
            own = (lane >= core * wide) & (lane < (core + 1) * wide)
            row = jnp.where(own, jnp.concatenate([half, half], axis=1), 0.0)
        step = step_ref[c : c + 1, :]
        here = in_column(column_ref[c : c + 1, :])
        for d in range(2):
            moved[d] = moved[d] + jnp.where(here & (step == d), row, 0.0)
    blank = jnp.zeros((112, D), LOW)
    total = 0.0
    for d in range(2):
        wanted = jnp.concatenate([moved[d].astype(LOW), blank], axis=0)
        total = total + dot_over(one_at(first_ref[...] + d, TABLE_ROWS), wanted, 1, 1)
    out_ref[:TABLE_ROWS, :] = total.astype(LOW)
    rest = out_ref.shape[0] - TABLE_ROWS
    wanted = jnp.where(in_column(spot_ref[...]), up_ref[...], 0.0).astype(LOW)
    wanted = jnp.concatenate([wanted, jnp.zeros((112, wanted.shape[1]), LOW)], axis=0)
    out_ref[TABLE_ROWS:, :] = dot_over(one_at(row_ref[...], rest), wanted, 1, 1).astype(LOW)


def write_vec(ix, table, bias, up, share):
    whole = pl.BlockSpec(memory_space=pltpu.VMEM)
    return pl.pallas_call(
        write_vec_kernel,
        in_specs=[pl.BlockSpec(memory_space=pltpu.SMEM)] + [whole] * 8,
        out_specs=whole,
        out_shape=jax.ShapeDtypeStruct((D, 128), LOW),
        compiler_params=pltpu.CompilerParams(vmem_limit_bytes=VMEM_BYTES),
    )(
        ix.core.astype(jnp.int32).reshape(1),
        table,
        bias,
        up,
        *table_places(),
        *up_places(ix, share),
    )


def dot(operand_a, operand_b):
    return jnp.dot(operand_a, operand_b, preferred_element_type=FULL)


def outer_sum(operand_a, operand_b):
    return jnp.einsum("ti,tj->ij", operand_a, operand_b, preferred_element_type=FULL).astype(LOW)


def dot_turned(operand_a, operand_b):
    return jnp.einsum("ti,ji->tj", operand_a, operand_b, preferred_element_type=FULL)


def body(
    tokens,
    cotangent,
    starts,
    w_qkv,
    m_qkv,
    v_qkv,
    w_out,
    m_out,
    v_out,
    w_up,
    m_up,
    v_up,
    w_down,
    m_down,
    v_down,
    vectors,
    m_vec,
    v_vec,
):
    ix = Index()
    rows = D // ix.count
    share = FF // ix.count
    tok_rows = tokens.shape[0]
    reach_count = (SEQ_MOST + tok_rows - 2) // tok_rows
    assert reach_count == 4
    chip_rows = 2 * tok_rows
    near_rows = (reach_count + 2) * tok_rows
    wide = SIDE * PAIR
    columns = 3 * wide
    out_wide, up_wide = D // 2, FF // 2

    early = 3 * PAIR * (SIDE - 1)
    late = columns - early
    first_spots = [[(0, early, 0, 0)], [(0, late + 128, 0, 0)]]
    cut = (out_wide + up_wide) // 256 * 128
    second_spots = [
        [(0, out_wide, 0, 0), (out_wide, cut - out_wide, 1, 0)],
        [(0, out_wide + up_wide - cut, 1, cut - out_wide)],
    ]
    third_spots = [[(0, D // 2, 0, 0)], [(0, D // 2, 0, D // 2)]]
    orders = ix.orders
    vec_piece = jnp.pad(vectors.astype(LOW).reshape(rows, VCOLS), ((0, 0), (0, 128 - VCOLS)))
    qkv_mine, qkv_others = by_core(ix, *paired_columns(w_qkv.astype(LOW).reshape(rows, 3 * D)))
    mine = jnp.concatenate([qkv_mine, vec_piece], axis=1)
    others = jnp.concatenate([qkv_others, vec_piece], axis=1)
    first = jnp.concatenate(by_core(ix, mine, flipped(others, 1)), axis=0)
    first = gather_top(ix, first)
    first, w_out, w_up = tied(first, w_out, w_up)

    first = gather_mid((first[..., :early], first[..., early:]), orders)
    up_sides = hidden_columns(w_up.astype(LOW).reshape(rows, FF), share)
    out_low = w_out.astype(LOW).reshape(rows, D)
    pieces = [
        jnp.concatenate([out_low[:, s * out_wide : (s + 1) * out_wide], up_sides[s]], axis=1)
        for s in range(2)
    ]
    own_piece, others = by_core(ix, *pieces)
    second = jnp.concatenate(by_core(ix, own_piece, flipped(others, 1)), axis=0)
    *first, second, starts, tokens = tied(*first, second, starts, tokens)
    first = gather_last(first, orders)
    mine = jnp.stack([shifted(tokens, 4), shifted(tokens, 2), tokens])
    chip_starts = jnp.concatenate(by_core(ix, starts, flipped(starts, 1)))
    first, second, mine, chip_starts, cotangent, w_down = tied(
        first, second, mine, chip_starts, cotangent, w_down
    )
    near_tokens = jnp.stack(by_core(ix, mine, flipped(mine, 1)), axis=1).reshape(near_rows, D)
    second = gather_top(ix, second)
    early_w = assemble(ix, first[:1], orders[:1], first_spots[:1], [early])[0]
    late_w = assemble(ix, first[1:], orders[1:], first_spots[1:], [late + 128])[0]
    vec_table, up_bias = read_vec(ix, late_w[:, late:], share)
    late_w = late_w[:, :late]
    third = w_down.astype(LOW).reshape(4 * rows, D)
    gain_one, shift_one, bias_q, bias_v, bias_o, gain_two, shift_two, bias_down = (
        vec_table[i] for i in range(8)
    )
    bias_q = lax.dynamic_slice_in_dim(bias_q, ix.core * wide, wide)
    bias_v = lax.dynamic_slice_in_dim(bias_v, ix.core * wide, wide)

    near_unit, near_inverse = norm_parts(near_tokens.astype(FULL))
    near_normed = (near_unit * gain_one + shift_one).astype(LOW)
    near_normed, cotangent = tied(near_normed, cotangent)
    chip_cotangent = jnp.concatenate(by_core(ix, cotangent, flipped(cotangent, 1)), axis=0)
    bias = jnp.stack(
        [bias_q.reshape(SIDE, PAIR), jnp.zeros((SIDE, PAIR), FULL), bias_v.reshape(SIDE, PAIR)],
        axis=1,
    ).reshape(columns)
    first_key = (chip_starts - ((ix.me >> 1) * chip_rows - reach_count * tok_rows))[:, None]
    early_qkv = (dot(near_normed, early_w) + bias[:early]).astype(LOW)
    late_qkv = (dot(near_normed, late_w) + bias[early:]).astype(LOW)
    early_qkv, late_qkv, second = tied(early_qkv, late_qkv, second)
    second = gather_mid(cut_at(second, cut), orders)
    mixed, weights = [None, None], [None, None]
    mixed[0], weights[0] = attend(first_key, late_qkv, tok_rows, 0, 1)
    mixed[0], early_qkv, second, third = tied(mixed[0], early_qkv, second, third)
    second = gather_last(second, orders)
    third = gather_top(ix, third)
    mixed[1], weights[1] = attend(first_key, early_qkv, tok_rows, 0, SIDE - 1)
    mixed = jnp.concatenate([mixed[1], mixed[0]], axis=1)
    mixed, second, third = tied(mixed, second, third)
    third = gather_mid(cut_at(third, D // 2), orders)
    attended = jnp.concatenate(by_core(ix, mixed, flipped(mixed, 1)), axis=1)
    out_half, up_w = assemble(ix, second, orders, second_spots, [out_wide, up_wide])
    out_w = jnp.concatenate(by_core(ix, out_half, flipped(out_half, 1)), axis=1)
    attended, out_w, third = tied(attended, out_w, third)
    third = gather_last(third, orders)
    inputs = near_tokens[near_rows - chip_rows :].astype(FULL)
    middle = inputs + (dot(attended, out_w) + bias_o)
    unit_two, inverse_two = norm_parts(middle)
    normed_two = (unit_two * gain_two + shift_two).astype(LOW)
    hidden_pre = dot(normed_two, up_w) + up_bias
    hidden_low = smooth_act(hidden_pre).astype(LOW)
    grad_downw = outer_sum(hidden_low, chip_cotangent)
    hidden_low, hidden_pre, grad_downw = tied(hidden_low, hidden_pre, grad_downw)
    sum_down = scatter_mid(take_apart(ix, [grad_downw], orders, third_spots), orders, 0, 1)
    down_w = assemble(ix, third, orders, third_spots, [D])[0]
    result = dot(hidden_low, down_w).reshape(2, tok_rows, D)
    own_result, other_result = by_core(ix, result[0], result[1])
    own_result = own_result + flipped(other_result.astype(LOW), 1).astype(FULL)
    own_middle = lax.dynamic_slice_in_dim(middle, ix.core * tok_rows, tok_rows, 0)
    out_tokens = (own_middle + (own_result + bias_down)).astype(LOW)

    grad_hidden = dot_turned(chip_cotangent, down_w)
    act_value, act_back = jax.vjp(smooth_act, hidden_pre)
    grad_pre = act_back(grad_hidden)[0].astype(LOW)
    partial_two = dot_turned(grad_pre, up_w)
    grad_gain_two = jnp.sum(partial_two * unit_two, axis=0)
    grad_shift_two = jnp.sum(partial_two, axis=0)
    grad_normed_two = partial_two + flipped(partial_two.astype(LOW), 1).astype(FULL)
    grad_normed_two, grad_pre, sum_down = tied(grad_normed_two, grad_pre, sum_down)
    sum_down = scatter_mid(sum_down, orders, 1, 9)
    grad_upw = outer_sum(normed_two, grad_pre)
    grad_middle = chip_cotangent.astype(FULL) + norm_back(
        grad_normed_two, unit_two, inverse_two, gain_two
    )
    grad_branch = grad_middle.astype(LOW)
    own_part = lax.dynamic_slice_in_dim(grad_branch, ix.core * out_wide, out_wide, 1)
    grad_outw = outer_sum(attended, own_part)
    own_out = lax.dynamic_slice_in_dim(out_w, ix.core * wide, wide, 0)
    grad_mixed = dot_turned(grad_branch, own_out).astype(LOW)
    grad_mixed, grad_outw, grad_upw, sum_down = tied(grad_mixed, grad_outw, grad_upw, sum_down)
    sum_second = take_apart(ix, [grad_outw, grad_upw], orders, second_spots)
    grad_mixed, sum_second = tied(grad_mixed, sum_second)
    sum_second = scatter_mid(sum_second, orders, 0, 1)
    early_back = attend_back(weights[1], grad_mixed, early_qkv, tok_rows, 0, SIDE - 1)
    sum_early = take_apart(ix, [outer_sum(near_normed, early_back)], orders[:1], first_spots[:1])
    sum_down = scatter_top(ix, sum_down)
    early_back, grad_mixed, sum_early, sum_second = tied(
        early_back, grad_mixed, sum_early, sum_second
    )
    sum_early = scatter_mid(sum_early, orders[:1], 0, 1)
    sum_second = scatter_mid(sum_second, orders, 1, 9)
    late_back = attend_back(weights[0], grad_mixed, late_qkv, tok_rows, SIDE - 1, 1)
    late_spots = [[(0, late, 0, 0)]]
    sum_late = take_apart(ix, [outer_sum(near_normed, late_back)], orders[1:], late_spots)
    sums_two = (
        grad_gain_two,
        grad_shift_two,
        jnp.sum(grad_branch.astype(FULL), axis=0),
        jnp.sum(cotangent.astype(FULL), axis=0),
        jnp.sum(grad_pre.astype(FULL), axis=0),
    )
    late_back, sum_late, sum_down, sum_second, sums_two = tied(
        late_back, sum_late, sum_down, sum_second, sums_two
    )
    sum_second = scatter_top(ix, sum_second)
    grad_gain_two, grad_shift_two, grad_bias_o, grad_bias_down, grad_bias_up = sums_two
    sum_late = scatter_mid(sum_late, orders[1:], 0, 1)

    grad_near = (dot_turned(early_back, early_w) + dot_turned(late_back, late_w)).astype(LOW)
    grad_gain_one = jnp.sum(grad_near.astype(FULL) * near_unit, axis=0)
    grad_shift_one = jnp.sum(grad_near.astype(FULL), axis=0)
    grad_gain_one, grad_shift_one, sum_early, sum_late = tied(
        grad_gain_one, grad_shift_one, sum_early, sum_late
    )
    sum_early = scatter_mid(sum_early, orders[:1], 1, 9)
    sum_late = scatter_mid(sum_late, orders[1:], 1, 9)
    grad_bias = jnp.concatenate(
        [jnp.sum(early_back.astype(FULL), axis=0), jnp.sum(late_back.astype(FULL), axis=0)]
    )
    blank = jnp.zeros((D,), FULL)
    grad_table = jnp.stack(
        [
            grad_gain_one,
            grad_shift_one,
            blank,
            blank,
            0.5 * grad_bias_o,
            grad_gain_two,
            grad_shift_two,
            grad_bias_down,
        ]
    )
    grad_vec = write_vec(ix, grad_table, grad_bias[None], grad_bias_up[None], share)
    blocks = grad_near.reshape(reach_count // 2 + 1, 2, tok_rows, D)
    own_blocks, other_blocks = by_core(ix, blocks[:, 0], blocks[:, 1])
    mate_blocks = flipped(other_blocks, 1)
    grad_vec, sum_second, mate_blocks = tied(grad_vec, sum_second, mate_blocks)
    vec_spots = [[(0, 128, 0, 0)]]
    sum_vec = scatter_mid(take_apart(ix, [grad_vec], orders[:1], vec_spots), orders[:1], 0, 9)

    own_blocks = own_blocks.astype(FULL) + mate_blocks.astype(FULL)
    four_back, two_back = own_blocks[0].astype(LOW), own_blocks[1].astype(LOW)
    sum_early, sum_late, sum_vec = tied(sum_early, sum_late, sum_vec)
    sum_first = scatter_top(ix, sum_early + sum_late + sum_vec)
    own = (
        own_blocks[2]
        + shifted(two_back, -2).astype(FULL)
        + shifted(four_back, -4).astype(FULL)
    )
    sum_first, sum_second, own = tied(sum_first, sum_second, own)
    unit_one, inverse_one = norm_parts(tokens.astype(FULL))
    own_grad_middle = lax.dynamic_slice_in_dim(grad_middle, ix.core * tok_rows, tok_rows, 0)
    input_grad = own_grad_middle + norm_back(own, unit_one, inverse_one, gain_one)

    keep_second, other_second = own_rows(ix, sum_second)
    keep_first, other_first = own_rows(ix, sum_first)
    g_vec = (keep_first[:, columns:] + other_first[:, columns:])[:, :VCOLS].reshape(-1)
    g_qkv = plain_columns(by_core(ix, keep_first[:, :columns], other_first[:, :columns]))
    g_out = jnp.concatenate(
        by_core(ix, keep_second[:, :out_wide], other_second[:, :out_wide]), axis=1
    )
    g_up = plain_hidden(by_core(ix, keep_second[:, out_wide:], other_second[:, out_wide:]), share)

    rate_qkv, rate_out, rate_up, rate_down = matrix_rates()
    entries = ix.me * vectors.shape[0] + jnp.arange(vectors.shape[0], dtype=jnp.int32)
    qkv_new = adamw(w_qkv, m_qkv, v_qkv, g_qkv.reshape(-1), rate_qkv, DECAY_RATE)
    out_new = adamw(w_out, m_out, v_out, g_out.reshape(-1), rate_out, DECAY_RATE)
    up_new = adamw(w_up, m_up, v_up, g_up.reshape(-1), rate_up, DECAY_RATE)
    down_new = adamw(w_down, m_down, v_down, sum_down.reshape(-1), rate_down, DECAY_RATE)
    vec_new = adamw(vectors, m_vec, v_vec, g_vec, vector_rates(entries), 0.0)
    return (out_tokens, input_grad) + qkv_new + out_new + up_new + down_new + vec_new


def solution(mesh):
    in_specs = (P("dev", None), P("dev", None)) + (P("dev"),) * 16
    out_specs = (P("dev", None), P("dev", None)) + (P("dev"),) * 15
    return jax.shard_map(body, mesh=mesh, in_specs=in_specs, out_specs=out_specs, check_vma=False)
```
